32 devices in a mesh: dom: 8 (over z, y), rep: 4 (over x, core).
Axes of the slice: x: 2, y: 2, z: 4, core: 2. Of those that a mesh axis runs over, the one named last changes fastest.
Arguments:
- node_feats: bfloat16 [4, 1024, 256], P('rep', 'dom'), may hold values from -6 to 6
- out_grad: bfloat16 [4, 1024, 256], P('rep', 'dom'), may hold values from -6 to 6
- norm1_gain: float32 [256], replicated, may hold values from 0.1 to 1.9
- w_query: bfloat16 [256, 256], replicated, may hold values from -0.375 to 0.375
- w_key: bfloat16 [256, 256], replicated, may hold values from -0.375 to 0.375
- w_value: bfloat16 [256, 256], replicated, may hold values from -0.375 to 0.375
- w_out: bfloat16 [256, 256], replicated, may hold values from -0.375 to 0.375
- norm2_gain: float32 [256], replicated, may hold values from 0.1 to 1.9
- w_up: bfloat16 [256, 512], replicated, may hold values from -0.375 to 0.375
- w_down: bfloat16 [512, 256], replicated, may hold values from -0.25 to 0.25
- local_gain: float32 [4], replicated, may hold values from 0.5 to 2
- expander_gain: float32 [4], replicated, may hold values from 2 to 8
- partner_perm: int32 [4, 4, 8, 128], P('rep', None, 'dom'), may hold values from 0 to 127, each once within a row
- block_pairs: int32 [4, 8, 1], P('rep', 'dom'), may hold values from 0 to 0, as said below
- pair_count: int32 [4, 8], P('rep', 'dom'), may hold values from 1 to 1, as said below
Outputs:
- node_out: bfloat16 [4, 1024, 256], P('rep', 'dom')
- grad_feats: bfloat16 [4, 1024, 256], P('rep', 'dom')
- grad_norm1_gain: float32 [256], replicated
- grad_w_query: float32 [256, 256], replicated
- grad_w_key: float32 [256, 256], replicated
- grad_w_value: float32 [256, 256], replicated
- grad_w_out: float32 [256, 256], replicated
- grad_norm2_gain: float32 [256], replicated
- grad_w_up: float32 [256, 512], replicated
- grad_w_down: float32 [512, 256], replicated
- grad_local_gain: float32 [4], replicated
- grad_expander_gain: float32 [4], replicated
The draws below stay inside these ranges and needn't reach their ends.
Inputs may be any that keep to these rules, and one draw needn't show every extreme that they name: `partner_perm`: each row is a permutation of the 128 local node indices. `block_pairs`: an entry e names query block e // 1 and key block e % 1 of the same partition; the first pair_count entries of a partition are distinct, the rest are not edges. `pair_count`: in every cluster some partition has exactly 1 pairs and another exactly 1.
All inputs are finite; a program needn't handle non-finite values.
Results may differ from the reference program's by a relative error of at most 0.029.
Values may be sent and summed in bfloat16 or wider, within the bound.
No kernel may reach another device: no remote copies, remote signals or barrier semaphores. Data moves between devices by JAX's collectives and lax.ppermute only.
A program may use at most 64 MiB of HBM per device.

```python
import math
import jax
import jax.numpy as jnp
from jax import lax

D = 256
H = 4
FF = 512
BLK = 128
MATCH = 4
NODE_DEV = 128
HD = 64
NB = 1
MAXP = 1
NODES = 1024
CLUSTERS = 4
N_DOM = 8


def pair_tables(key):
    folded = jax.random.fold_in(key, 11)
    rolled_key, busy_key, drawn_key, order_key = jax.random.split(folded, 4)
    spread = 64
    rolled = jax.random.randint(rolled_key, (CLUSTERS, N_DOM), 0, spread + 1)
    headroom = MAXP - NB
    surplus = headroom * rolled * rolled * rolled // (spread * spread * spread)
    busiest = jax.random.randint(busy_key, (CLUSTERS, 1), 0, N_DOM)
    calmest = (busiest + jax.random.randint(drawn_key, (CLUSTERS, 1), 1, N_DOM)) % N_DOM
    columns = jnp.arange(N_DOM)[None, :]
    surplus = jnp.where(columns == busiest, headroom, surplus)
    surplus = jnp.where(columns == calmest, 0, surplus)
    counted = (NB + surplus).astype(jnp.int32)
    candidates = NB * NB
    jitter = jax.random.randint(order_key, (CLUSTERS, N_DOM, candidates), 0, 1 << 20)
    ranked = jitter * candidates + jnp.arange(candidates)[None, None, :]
    ordering = jnp.argsort(ranked, axis=-1)
    return (ordering[:, :, :MAXP].astype(jnp.int32), counted)


def draw_block_pairs(key, part):
    return pair_tables(key)[0]


def draw_pair_count(key, part):
    return pair_tables(key)[1]


def strengthened(values, rng, source, target, parts, factor):
    def block_of(axis_at):
        return (jnp.arange(values.shape[axis_at]) // (values.shape[axis_at] // parts)).reshape((-1,) + (1,) * (values.ndim - 1 - axis_at))

    one_side = jax.random.permutation(rng, parts)[block_of(target)]
    other_side = (block_of(target) + parts // 2) % parts
    return jnp.where((block_of(source) == one_side) | (block_of(source) == other_side), factor * values, values)


def level_of(stream_key, dims, pieces, least, largest):
    level = 1.0
    for position, parts in pieces:
        steps = jax.random.uniform(jax.random.fold_in(jax.random.fold_in(stream_key, 6), position), (parts,), jnp.float32, least / len(pieces), largest / len(pieces))
        level = level * jnp.repeat(jnp.exp(steps), dims[position] // parts).reshape((-1,) + (1,) * (len(dims) - 1 - position))
    return level


def centred(key, extent, deviation, reach, cuts=(), kind=jnp.bfloat16):
    array = jax.random.normal(key, extent, jnp.float32) * deviation
    if len(cuts) > 0:
        array = level_of(key, extent, cuts, -0.22, 0.18) * array
    return jnp.clip(array, min=-reach, max=reach).astype(kind)


def heavy_noise(rng, extent, scale, most, pieces, heavy, held_as=jnp.bfloat16):
    values = scale * jax.random.normal(rng, extent, jnp.float32)
    if pieces:
        values = values * level_of(rng, extent, pieces, -0.22, 0.18)
    return jnp.clip(strengthened(values, jax.random.fold_in(rng, 3), *heavy), -most, most).astype(held_as)


def setup_inputs(seed: int = 0) -> dict:
    arg_keys = jax.random.split(jax.random.key(seed), 16)
    return {
        "node_feats": centred(arg_keys[0], (CLUSTERS, NODES, D), 1.0, 6.0, ((0, 4), (1, 8))),
        "out_grad": heavy_noise(arg_keys[1], (CLUSTERS, NODES, D), 1.0, 6.0, ((0, 4), (1, 8)), (1, 2, 8, 2.0)),
        "norm1_gain": jnp.clip(1.0 + 0.18 * jax.random.normal(arg_keys[2], (D,), jnp.float32), 0.1, 1.9),
        "w_query": centred(arg_keys[3], (D, D), D ** -0.5, 0.375),
        "w_key": centred(arg_keys[4], (D, D), D ** -0.5, 0.375),
        "w_value": centred(arg_keys[5], (D, D), D ** -0.5, 0.375),
        "w_out": centred(arg_keys[6], (D, D), D ** -0.5, 0.375),
        "norm2_gain": jnp.clip(1.0 + 0.18 * jax.random.normal(arg_keys[7], (D,), jnp.float32), 0.1, 1.9),
        "w_up": centred(arg_keys[8], (D, FF), D ** -0.5, 0.375),
        "w_down": centred(arg_keys[9], (FF, D), FF ** -0.5, 0.25),
        "local_gain": jnp.clip(jnp.exp(jax.random.uniform(arg_keys[10], (H,), jnp.float32, math.log(0.5), math.log(2.0))), 0.5, 2.0),
        "expander_gain": jnp.clip(jnp.exp(jax.random.uniform(arg_keys[11], (H,), jnp.float32, math.log(2.0), math.log(8.0))), 2.0, 8.0),
        "partner_perm": jax.vmap(lambda own: jax.random.permutation(own, NODE_DEV))(jax.random.split(arg_keys[12], CLUSTERS * MATCH * N_DOM)).reshape((CLUSTERS, MATCH, N_DOM, NODE_DEV)).astype(jnp.int32),
        "block_pairs": draw_block_pairs(jax.random.fold_in(arg_keys[15], 71), 0),
        "pair_count": draw_pair_count(jax.random.fold_in(arg_keys[15], 71), 0),
    }


EPSILON = 1e-05
SCORE_CAP = 5.0
GELU_ROOT = 0.7978845608028654
GELU_CUBIC = 0.044715

def rounded(matrix):
    return lax.optimization_barrier(matrix.astype(jnp.bfloat16)).astype(jnp.float32)

def gelu_parts(preact):
    tangent = jnp.tanh(GELU_ROOT * (preact + GELU_CUBIC * preact * preact * preact))
    result = 0.5 * preact * (1.0 + tangent)
    derivative = 0.5 * (1.0 + tangent) + 0.5 * preact * (1.0 - tangent * tangent) * GELU_ROOT * (1.0 + 3.0 * GELU_CUBIC * preact * preact)
    return (result, derivative)

def norm_forward(matrix):
    center = lax.optimization_barrier(jnp.mean(matrix, axis=-1, keepdims=True))
    shifted = matrix - center
    inverse = lax.rsqrt(lax.optimization_barrier(jnp.mean(shifted * shifted, axis=-1, keepdims=True)) + EPSILON)
    return (shifted * inverse, inverse)

def norm_backward(upstream, normed, inverse, gain):
    scaled_up = upstream * gain
    return inverse * (scaled_up - lax.optimization_barrier(jnp.mean(scaled_up, axis=-1, keepdims=True)) - normed * lax.optimization_barrier(jnp.mean(scaled_up * normed, axis=-1, keepdims=True)))

def project(first_op, second_op):
    return jnp.dot(first_op, second_op, preferred_element_type=jnp.float32)

def project_back(first_op, second_op):
    return lax.dot_general(first_op, second_op, (((1,), (1,)), ((), ())), preferred_element_type=jnp.float32)

def project_outer(first_op, second_op):
    return lax.dot_general(first_op, second_op, (((0,), (0,)), ((), ())), preferred_element_type=jnp.float32)

def block_mask(pair_list, listed):
    active = (jnp.arange(MAXP) < listed).astype(jnp.float32)
    hits = (pair_list[:, None] == jnp.arange(NB * NB, dtype=jnp.int32)[None, :]).astype(jnp.float32)
    blocks = lax.optimization_barrier(jnp.sum(hits * active[:, None], axis=0)).reshape(NB, NB)
    return jnp.repeat(jnp.repeat(blocks, BLK, axis=0), BLK, axis=1)

def reference(node_feats, out_grad, norm1_gain, w_query, w_key, w_value, w_out, norm2_gain, w_up, w_down, local_gain, expander_gain, partner_perm, block_pairs, pair_count):
    levels = N_DOM.bit_length() - 1
    flip_bits = [(levels - 1 - matching) % levels for matching in range(MATCH)]
    score_scale = float(HD) ** 0.5
    devices = jnp.arange(N_DOM, dtype=jnp.int32)
    local_col = local_gain[:, None, None]
    far_col = expander_gain[None, :, None]
    node_outs = []
    feat_grads = []
    grad_totals = None
    for cluster in range(CLUSTERS):
        features = node_feats[cluster].astype(jnp.float32)
        normed1, inverse1 = norm_forward(features)
        hidden = (normed1 * norm1_gain).astype(jnp.bfloat16)
        queries = project(hidden, w_query).astype(jnp.bfloat16).reshape(N_DOM, NODE_DEV, D)
        key_rows = project(hidden, w_key).astype(jnp.bfloat16).reshape(N_DOM, NODE_DEV, D)
        value_rows = project(hidden, w_value).astype(jnp.bfloat16).reshape(N_DOM, NODE_DEV, D)
        partners = partner_perm[cluster]
        pair_lists = block_pairs[cluster]
        pair_totals = pair_count[cluster]

        def attend(device):
            own_query = queries[device].astype(jnp.float32).reshape(NODE_DEV, H, HD)
            own_key = key_rows[device].astype(jnp.float32).reshape(NODE_DEV, H, HD)
            own_value = value_rows[device].astype(jnp.float32).reshape(NODE_DEV, H, HD)
            nodemask = block_mask(pair_lists[device], pair_totals[device])
            raw_local = jnp.einsum('ihd,jhd->hij', own_query, own_key) / score_scale
            tanh_local = jnp.tanh(local_col * raw_local / SCORE_CAP)
            exp_local = jnp.exp(SCORE_CAP * tanh_local) * nodemask[None]
            far_keys = []
            far_values = []
            for matching in range(MATCH):
                source = jnp.bitwise_xor(device, 1 << flip_bits[matching])
                picked = partners[matching][device]
                far_keys.append(key_rows[source][picked])
                far_values.append(value_rows[source][picked])
            far_key = jnp.stack(far_keys).astype(jnp.float32).reshape(MATCH, NODE_DEV, H, HD)
            far_value = jnp.stack(far_values).astype(jnp.float32).reshape(MATCH, NODE_DEV, H, HD)
            raw_far = jnp.einsum('ihd,mihd->mhi', own_query, far_key) / score_scale
            tanh_far = jnp.tanh(far_col * raw_far / SCORE_CAP)
            exp_far = jnp.exp(SCORE_CAP * tanh_far)
            denominator = lax.optimization_barrier(jnp.sum(exp_local, axis=-1)) + lax.optimization_barrier(jnp.sum(exp_far, axis=0))
            weight_local = rounded(exp_local / denominator[:, :, None])
            weight_far = rounded(exp_far / denominator[None])
            attended = jnp.einsum('hij,jhd->ihd', weight_local, own_value) + jnp.einsum('mhi,mihd->ihd', weight_far, far_value)
            saved = (own_query, own_key, own_value, far_key, far_value, raw_local, tanh_local, weight_local, raw_far, tanh_far, weight_far)
            return (attended.reshape(NODE_DEV, D), saved)
        attended32 = lax.map(lambda device: attend(device)[0], devices)
        attended = attended32.reshape(NODES, D).astype(jnp.bfloat16)
        mixed = (features + project(attended, w_out)).astype(jnp.bfloat16)
        normed2, inverse2 = norm_forward(mixed.astype(jnp.float32))
        hidden2 = (normed2 * norm2_gain).astype(jnp.bfloat16)
        preact = project(hidden2, w_up)
        activ, derivative = gelu_parts(preact)
        activ = activ.astype(jnp.bfloat16)
        node_outs.append((mixed.astype(jnp.float32) + project(activ, w_down)).astype(jnp.bfloat16))
        upstream = out_grad[cluster]
        grad_down = project_outer(activ, upstream)
        grad_pre = (project_back(upstream, w_down) * derivative).astype(jnp.bfloat16)
        grad_up = project_outer(hidden2, grad_pre)
        grad_hidden2 = project_back(grad_pre, w_up)
        grad_gain2 = lax.optimization_barrier(jnp.sum(grad_hidden2 * normed2, axis=0))
        grad_mixed = upstream.astype(jnp.float32) + norm_backward(grad_hidden2, normed2, inverse2, norm2_gain)
        grad_mixed16 = grad_mixed.astype(jnp.bfloat16)
        grad_wout = project_outer(attended, grad_mixed16)
        grad_att = project_back(grad_mixed16, w_out).astype(jnp.bfloat16).reshape(N_DOM, NODE_DEV, D)

        def backward_rows(device):
            _, saved = attend(device)
            own_query, own_key, own_value, far_key, far_value, raw_local, tanh_local, weight_local, raw_far, tanh_far, weight_far = saved
            grad_out = grad_att[device].astype(jnp.float32).reshape(NODE_DEV, H, HD)
            delta = jnp.einsum('ihd,ihd->hi', grad_out, attended32[device].reshape(NODE_DEV, H, HD))
            dots_local = jnp.einsum('ihd,jhd->hij', grad_out, own_value)
            dlogit_local = weight_local * (dots_local - delta[:, :, None])
            slope_local = 1.0 - tanh_local * tanh_local
            gain_local_term = lax.optimization_barrier(jnp.sum(dlogit_local * raw_local * slope_local, axis=(1, 2)))
            dscore_local = rounded(dlogit_local * local_col * slope_local / score_scale)
            dots_far = jnp.einsum('ihd,mihd->mhi', grad_out, far_value)
            dlogit_far = weight_far * (dots_far - delta[None])
            slope_far = 1.0 - tanh_far * tanh_far
            gain_far_term = lax.optimization_barrier(jnp.sum(dlogit_far * raw_far * slope_far, axis=(0, 2)))
            dscore_far = rounded(dlogit_far * far_col * slope_far / score_scale)
            grad_query = jnp.einsum('hij,jhd->ihd', dscore_local, own_key) + jnp.einsum('mhi,mihd->ihd', dscore_far, far_key)
            grad_key = jnp.einsum('hij,ihd->jhd', dscore_local, own_query)
            grad_value = jnp.einsum('hij,ihd->jhd', weight_local, grad_out)
            return (grad_query.reshape(NODE_DEV, D), grad_key.reshape(NODE_DEV, D), grad_value.reshape(NODE_DEV, D), dscore_far, weight_far, gain_local_term, gain_far_term)
        grad_query, key_local, value_local, dscore_far, weight_far, gain_local_terms, gain_far_terms = lax.map(backward_rows, devices)

        def receive_rows(device):
            key_total = key_local[device]
            value_total = value_local[device]
            for matching in range(MATCH):
                source = jnp.bitwise_xor(device, 1 << flip_bits[matching])
                source_query = queries[source].astype(jnp.float32).reshape(NODE_DEV, H, HD)
                source_grad = grad_att[source].astype(jnp.float32).reshape(NODE_DEV, H, HD)
                key_term = rounded(jnp.einsum('hi,ihd->ihd', dscore_far[source, matching], source_query).reshape(NODE_DEV, D))
                value_term = rounded(jnp.einsum('hi,ihd->ihd', weight_far[source, matching], source_grad).reshape(NODE_DEV, D))
                placed = partners[matching][source]
                key_total = key_total + jnp.zeros((NODE_DEV, D), jnp.float32).at[placed].set(key_term)
                value_total = value_total + jnp.zeros((NODE_DEV, D), jnp.float32).at[placed].set(value_term)
            return (key_total, value_total)
        key_total, value_total = lax.map(receive_rows, devices)
        grad_query16 = grad_query.reshape(NODES, D).astype(jnp.bfloat16)
        grad_key16 = key_total.reshape(NODES, D).astype(jnp.bfloat16)
        grad_value16 = value_total.reshape(NODES, D).astype(jnp.bfloat16)
        grad_wq = project_outer(hidden, grad_query16)
        grad_wk = project_outer(hidden, grad_key16)
        grad_wv = project_outer(hidden, grad_value16)
        grad_hidden = project_back(grad_query16, w_query) + project_back(grad_key16, w_key) + project_back(grad_value16, w_value)
        grad_gain1 = lax.optimization_barrier(jnp.sum(grad_hidden * normed1, axis=0))
        feat_grads.append((grad_mixed + norm_backward(grad_hidden, normed1, inverse1, norm1_gain)).astype(jnp.bfloat16))
        cluster_grads = (grad_gain1, grad_wq, grad_wk, grad_wv, grad_wout, grad_gain2, grad_up, grad_down, lax.optimization_barrier(jnp.sum(gain_local_terms, axis=0)), lax.optimization_barrier(jnp.sum(gain_far_terms, axis=0)))
        if grad_totals is None:
            grad_totals = cluster_grads
        else:
            grad_totals = tuple((former + latter for former, latter in zip(grad_totals, cluster_grads)))
    return (jnp.stack(node_outs), jnp.stack(feat_grads), grad_totals[0], grad_totals[1], grad_totals[2], grad_totals[3], grad_totals[4], grad_totals[5], grad_totals[6], grad_totals[7], grad_totals[8], grad_totals[9])
```

```python
import functools

import jax
import jax.numpy as jnp
from jax import lax
from jax.experimental import pallas as pl
from jax.experimental.pallas import tpu as pltpu
from jax.sharding import PartitionSpec as P

EPSILON = 1e-05
SCORE_CAP = 5.0
GELU_ROOT = 0.7978845608028654
GELU_CUBIC = 0.044715
SMALL = 16
AXES = ("dom", "rep")
VMEM_LIMIT = 48 * 1024 * 1024
F32 = jnp.float32
BF16 = jnp.bfloat16


def dot(a, b):
    return lax.dot_general(a, b, (((1,), (0,)), ((), ())), preferred_element_type=F32)


def dot_rhs_t(a, b):
    return lax.dot_general(a, b, (((1,), (1,)), ((), ())), preferred_element_type=F32)


def dot_lhs_t(a, b):
    return lax.dot_general(a, b, (((0,), (0,)), ((), ())), preferred_element_type=F32)


def norm_forward(matrix):
    center = jnp.mean(matrix, axis=-1, keepdims=True)
    shifted = matrix - center
    inverse = lax.rsqrt(jnp.mean(shifted * shifted, axis=-1, keepdims=True) + EPSILON)
    return (shifted * inverse, inverse)


def norm_backward(upstream, normed, inverse, gain):
    scaled_up = upstream * gain
    return inverse * (
        scaled_up
        - jnp.mean(scaled_up, axis=-1, keepdims=True)
        - normed * jnp.mean(scaled_up * normed, axis=-1, keepdims=True)
    )


def gelu_parts(preact):
    tangent = jnp.tanh(GELU_ROOT * (preact + GELU_CUBIC * preact * preact * preact))
    result = 0.5 * preact * (1.0 + tangent)
    derivative = 0.5 * (1.0 + tangent) + 0.5 * preact * (1.0 - tangent * tangent) * GELU_ROOT * (
        1.0 + 3.0 * GELU_CUBIC * preact * preact
    )
    return (result, derivative)


def split_parts(rows):
    high = rows.astype(BF16).astype(F32)
    return jnp.concatenate([high, rows - high], axis=0).astype(BF16)


def join_parts(packed):
    wide = packed.astype(F32)
    return wide[: SMALL // 2] + wide[SMALL // 2 :]


def device_bits():
    flat = lax.axis_index("dom") * lax.axis_size("rep") + lax.axis_index("rep")
    core = flat & 1
    first = (flat >> 1) & 1
    second = (flat >> 2) & 1
    swap = core == 1
    return (core, jnp.where(swap, second, first), jnp.where(swap, first, second))


def layer_kernel(groups, *refs):
    count = len(groups)
    feats_refs = refs[: count + 1]
    (
        up_ref,
        gain1_ref,
        wq_ref,
        wk_ref,
        wv_ref,
        wo_ref,
        gain2_ref,
        wup_ref,
        wdown_ref,
        local_ref,
        far_ref,
        perm_ref,
    ) = refs[count + 1 : count + 13]
    out_ref, keep_ref, send_ref, small_ref, own_ref, mixed_ref = refs[count + 13 : count + 19]
    back_refs = refs[count + 19 : 2 * count + 19]
    raw_s, tanh_s, weight_s, dscore_s = refs[2 * count + 19 :]

    rows, width = out_ref.shape
    heads = local_ref.shape[0]
    head_dim = width // heads
    scale = 1.0 / float(head_dim) ** 0.5
    core, level1, level2 = device_bits()
    half = 4 * width

    def put(chunk, value):
        value = value.astype(BF16)
        upper = (chunk >> 1) & 1
        lower = chunk & 1
        same = core == (chunk >> 2)

        @pl.when(same)
        def _():
            rel = (upper ^ level1) * 2 + (lower ^ level2)
            keep_ref[pl.ds(pl.multiple_of(rel * width, width), width), :] = value

        @pl.when(jnp.logical_not(same))
        def _():
            rel = (upper ^ level2) * 2 + (lower ^ level1)
            send_ref[pl.ds(pl.multiple_of(rel * width, width), width), :] = value

    gain1 = gain1_ref[...]
    gain2 = gain2_ref[...]
    upstream = up_ref[...]
    feats = jnp.concatenate([ref[...] for ref in feats_refs], axis=0).astype(F32)
    normed1, _ = norm_forward(feats)
    hidden = (normed1 * gain1).astype(BF16)
    queries = dot(hidden[:rows], wq_ref[...])
    key_all = dot(hidden, wk_ref[...]).astype(BF16)
    value_all = dot(hidden, wv_ref[...]).astype(BF16)

    lane = lax.broadcasted_iota(jnp.int32, (rows, width), 1) // head_dim
    head_masks = [lane == h for h in range(heads)]

    def stacked(matrix):
        return jnp.concatenate([jnp.where(m, matrix, 0.0) for m in head_masks], axis=0).astype(BF16)

    query_stack = stacked(queries)
    raw_s[...] = dot_rhs_t(query_stack, key_all) * scale

    target = lax.broadcasted_iota(jnp.int32, (rows, rows), 0)
    counts = []
    for members in groups:
        total = 0.0
        for m in members:
            total = total + jnp.where(target == perm_ref[m : m + 1, :], 1.0, 0.0)
        counts.append(total.T)
    far_counts = jnp.concatenate(counts, axis=1)

    for h in range(heads):
        block = pl.ds(h * rows, rows)
        tl = jnp.tanh(raw_s[block, :rows] * (local_ref[h] / SCORE_CAP))
        tf = jnp.tanh(raw_s[block, rows:] * (far_ref[h] / SCORE_CAP))
        el = jnp.exp(SCORE_CAP * tl)
        ef = jnp.exp(SCORE_CAP * tf) * far_counts
        inv = 1.0 / (jnp.sum(el, axis=1, keepdims=True) + jnp.sum(ef, axis=1, keepdims=True))
        tanh_s[block, :rows] = tl
        tanh_s[block, rows:] = tf
        weight_s[block, :rows] = (el * inv).astype(BF16)
        weight_s[block, rows:] = (ef * inv).astype(BF16)

    def collapse(matrix):
        total = jnp.where(head_masks[0], matrix[:rows], 0.0)
        for h in range(1, heads):
            total = total + jnp.where(head_masks[h], matrix[h * rows : (h + 1) * rows], 0.0)
        return total

    attended32 = collapse(dot(weight_s[...], value_all))
    attended = attended32.astype(BF16)
    mixed = (feats[:rows] + dot(attended, wo_ref[...])).astype(BF16)
    normed2, inverse2 = norm_forward(mixed.astype(F32))
    hidden2 = (normed2 * gain2).astype(BF16)
    preact = dot(hidden2, wup_ref[...])
    act32, derivative = gelu_parts(preact)
    act = act32.astype(BF16)
    out_ref[...] = (mixed.astype(F32) + dot(act, wdown_ref[...])).astype(BF16)
    grad_down = dot_lhs_t(act, upstream)
    put(6, grad_down[:width])
    put(7, grad_down[width:])
    grad_pre = (dot_rhs_t(upstream, wdown_ref[...]) * derivative).astype(BF16)
    grad_up = dot_lhs_t(hidden2, grad_pre)
    put(4, grad_up[:, :width])
    put(5, grad_up[:, width:])
    grad_hidden2 = dot_rhs_t(grad_pre, wup_ref[...])
    grad_gain2 = jnp.sum(grad_hidden2 * normed2, axis=0, keepdims=True)
    grad_mixed = upstream.astype(F32) + norm_backward(grad_hidden2, normed2, inverse2, gain2)
    mixed_ref[...] = grad_mixed
    grad_mixed16 = grad_mixed.astype(BF16)
    put(3, dot_lhs_t(attended, grad_mixed16))
    grad_att = dot_rhs_t(grad_mixed16, wo_ref[...]).astype(BF16).astype(F32)
    grad_stack = stacked(grad_att)
    product = grad_att * attended32
    dots = dot_rhs_t(grad_stack, value_all)

    local_terms = []
    far_terms = []
    for h in range(heads):
        block = pl.ds(h * rows, rows)
        delta = jnp.sum(jnp.where(head_masks[h], product, 0.0), axis=1, keepdims=True)
        tangent = tanh_s[block, :]
        slope = 1.0 - tangent * tangent
        dlogit = weight_s[block, :].astype(F32) * (dots[h * rows : (h + 1) * rows] - delta)
        sloped = dlogit * slope
        terms = jnp.sum(sloped * raw_s[block, :], axis=0, keepdims=True)
        local_terms.append(jnp.sum(terms[:, :rows], axis=1, keepdims=True))
        far_terms.append(jnp.sum(terms[:, rows:], axis=1, keepdims=True))
        dscore_s[block, :rows] = (sloped[:, :rows] * (local_ref[h] * scale)).astype(BF16)
        dscore_s[block, rows:] = (sloped[:, rows:] * (far_ref[h] * scale)).astype(BF16)

    grad_query = collapse(dot(dscore_s[...], key_all)).astype(BF16)
    grad_key = dot_lhs_t(dscore_s[...], query_stack).astype(BF16)
    grad_value = dot_lhs_t(weight_s[...], grad_stack).astype(BF16)
    put(0, dot_lhs_t(hidden[:rows], grad_query))
    put(1, dot_lhs_t(hidden, grad_key))
    put(2, dot_lhs_t(hidden, grad_value))
    grad_hidden = dot_rhs_t(grad_key, wk_ref[...]) + dot_rhs_t(grad_value, wv_ref[...])
    own = grad_hidden[:rows] + dot_rhs_t(grad_query, wq_ref[...])
    own_ref[...] = own
    grad_gain1 = jnp.sum(own * normed1[:rows], axis=0, keepdims=True)
    grad_gain1 = grad_gain1 + jnp.sum(grad_hidden[rows:] * normed1[rows:], axis=0, keepdims=True)
    for k, ref in enumerate(back_refs):
        ref[...] = grad_hidden[(k + 1) * rows : (k + 2) * rows].astype(BF16)

    column = lax.broadcasted_iota(jnp.int32, (1, width), 1)
    gains = jnp.zeros((1, width), F32)
    for h in range(heads):
        gains = jnp.where(column == h, local_terms[h], gains)
        gains = jnp.where(column == heads + h, far_terms[h], gains)
    line = lax.broadcasted_iota(jnp.int32, (SMALL // 2, width), 0)
    small = jnp.where(line == 0, grad_gain1, jnp.where(line == 1, grad_gain2, jnp.where(line == 2, gains, 0.0)))
    packed = split_parts(small)
    small_ref[...] = packed
    send_ref[half:, :] = packed


def merge_kernel(keep_ref, small_ref, recv_ref, *out_refs):
    rows = keep_ref.shape[0]
    total = keep_ref[...].astype(F32) + recv_ref[:rows, :].astype(F32)
    total = total.astype(BF16)
    packed = split_parts(join_parts(small_ref[...]) + join_parts(recv_ref[rows:, :]))
    if len(out_refs) == 3:
        kept, sent, small = out_refs
        kept[...] = total[: rows // 2]
        sent[: rows // 2, :] = total[rows // 2 :]
        sent[rows // 2 :, :] = packed
        small[...] = packed
    else:
        out_refs[0][:rows, :] = total
        out_refs[0][rows:, :] = packed


def double_kernel(own_ref, recv_ref, out_ref):
    rows = own_ref.shape[0] - SMALL
    out_ref[:rows, :] = (own_ref[:rows, :].astype(F32) + recv_ref[:rows, :].astype(F32)).astype(BF16)
    out_ref[rows:, :] = split_parts(join_parts(own_ref[rows:, :]) + join_parts(recv_ref[rows:, :]))


def tail_kernel(*refs):
    count = len(refs) - 5
    feats_ref, own_ref, mixed_ref, gain_ref = refs[:4]
    normed, inverse = norm_forward(feats_ref[...].astype(F32))
    grad_hidden = own_ref[...]
    for ref in refs[4 : 4 + count]:
        grad_hidden = grad_hidden + ref[...].astype(F32)
    refs[-1][...] = (mixed_ref[...] + norm_backward(grad_hidden, normed, inverse, gain_ref[...])).astype(BF16)


def spread_kernel(*refs):
    pieces = refs[:7]
    gain1_ref, wq_ref, wk_ref, wv_ref, wo_ref, gain2_ref, up_ref, down_ref, tiny_ref, chunks, sems = refs[7:]
    width = wq_ref.shape[0]
    core, level1, level2 = device_bits()

    def place(rel, value):
        upper, lower = (level2, level1) if rel >= 4 else (level1, level2)
        index = (core ^ (rel >> 2)) * 4 + (upper ^ ((rel >> 1) & 1)) * 2 + (lower ^ (rel & 1))
        chunks[index] = value.astype(F32)

    base, one, two, far_base, far_one, far_two, _ = pieces
    place(0, base[:width, :])
    place(1, one[...])
    place(2, two[:width, :])
    place(3, two[width:, :])
    place(4, far_base[:width, :])
    place(5, far_one[...])
    place(6, far_two[:width, :])
    place(7, far_two[width:, :])
    targets = [
        wq_ref,
        wk_ref,
        wv_ref,
        wo_ref,
        up_ref.at[:, :width],
        up_ref.at[:, width:],
        down_ref.at[:width, :],
        down_ref.at[width:, :],
    ]
    copies = [pltpu.make_async_copy(chunks.at[k], t, sems.at[k]) for k, t in enumerate(targets)]
    for copy in copies:
        copy.start()
    small = join_parts(base[width:, :])
    gain1_ref[...] = small[0:1]
    gain2_ref[...] = small[1:2]
    tiny_ref[...] = small[2:3, :128]
    for copy in copies:
        copy.wait()


def struct(shape, dtype):
    return jax.ShapeDtypeStruct(shape, dtype)


VM = pl.BlockSpec(memory_space=pltpu.VMEM)
SM = pl.BlockSpec(memory_space=pltpu.SMEM)
ANY = pl.BlockSpec(memory_space=pl.ANY)
PARAMS = pltpu.CompilerParams(vmem_limit_bytes=VMEM_LIMIT)


def call(kernel, outs, *args, in_specs=None, **kwargs):
    return pl.pallas_call(
        kernel,
        out_shape=outs,
        in_specs=in_specs or [VM] * len(args),
        out_specs=jax.tree.map(lambda _: VM, outs),
        compiler_params=PARAMS,
        **kwargs,
    )(*args)


def flipped(x, bits_even, bits_odd):
    size = lax.axis_size("dom") * lax.axis_size("rep")
    pairs = [(i, i ^ (bits_odd if i & 1 else bits_even)) for i in range(size)]
    return lax.ppermute(x, AXES, pairs)


def local(
    node_feats,
    out_grad,
    norm1_gain,
    w_query,
    w_key,
    w_value,
    w_out,
    norm2_gain,
    w_up,
    w_down,
    local_gain,
    expander_gain,
    partner_perm,
    block_pairs,
    pair_count,
):
    feats = node_feats[0]
    partners = partner_perm[0, :, 0, :]
    rows, width = feats.shape
    heads = local_gain.shape[0]
    size = lax.axis_size("dom") * lax.axis_size("rep")
    levels = lax.axis_size("dom").bit_length() - 1
    by_bit = {}
    for matching in range(partners.shape[0]):
        by_bit.setdefault((levels - 1 - matching) % levels, []).append(matching)
    bits = list(by_bit)
    groups = [by_bit[b] for b in bits]

    def swapped(x, bit):
        return lax.ppermute(x, "dom", [(i, i ^ 1 << bit) for i in range(lax.axis_size("dom"))])

    others = [swapped(feats, b) for b in bits]
    count = len(bits)
    tall = (count + 1) * rows
    gain1 = norm1_gain.reshape(1, width)
    outs = (
        struct((rows, width), BF16),
        struct((4 * width, width), BF16),
        struct((4 * width + SMALL, width), BF16),
        struct((SMALL, width), BF16),
        struct((rows, width), F32),
        struct((rows, width), F32),
    ) + tuple(struct((rows, width), BF16) for _ in bits)
    node_out, keep, send, small, own, grad_mixed, *back = call(
        functools.partial(layer_kernel, groups),
        outs,
        feats,
        *others,
        out_grad[0],
        gain1,
        w_query,
        w_key,
        w_value,
        w_out,
        norm2_gain.reshape(1, width),
        w_up,
        w_down,
        local_gain,
        expander_gain,
        partners,
        in_specs=[VM] * (count + 10) + [SM, SM, VM],
        scratch_shapes=[
            pltpu.VMEM((heads * rows, tall), F32),
            pltpu.VMEM((heads * rows, tall), F32),
            pltpu.VMEM((heads * rows, tall), BF16),
            pltpu.VMEM((heads * rows, tall), BF16),
        ],
    )

    recv = flipped(send, 1, 1)
    keep, send, small = call(
        merge_kernel,
        (struct((2 * width, width), BF16), struct((2 * width + SMALL, width), BF16), struct((SMALL, width), BF16)),
        keep,
        small,
        recv,
    )
    recv = flipped(send, 2, 4)
    keep, send, small = call(
        merge_kernel,
        (struct((width, width), BF16), struct((width + SMALL, width), BF16), struct((SMALL, width), BF16)),
        keep,
        small,
        recv,
    )
    recv = flipped(send, 4, 2)
    (base,) = call(merge_kernel, (struct((width + SMALL, width), BF16),), keep, small, recv)

    returned = [swapped(x, b) for x, b in zip(back, bits)]
    grad_feats = call(tail_kernel, struct((rows, width), BF16), feats, own, grad_mixed, gain1, *returned)

    high_bits = [1 << k for k in range(3, size.bit_length() - 1)]
    for even, odd in zip(high_bits, high_bits[::-1]):
        base = call(double_kernel, struct(base.shape, BF16), base, flipped(base, even, odd))

    one = flipped(base[:width], 4, 2)
    two = flipped(jnp.concatenate([base[:width], one], axis=0), 2, 4)
    far_base = flipped(base[:width], 1, 1)
    far_one = flipped(one, 1, 1)
    far_two = flipped(two, 1, 1)
    square = struct((width, width), F32)
    results = pl.pallas_call(
        spread_kernel,
        out_shape=(
            struct((1, width), F32),
            square,
            square,
            square,
            square,
            struct((1, width), F32),
            struct((width, 2 * width), F32),
            struct((2 * width, width), F32),
            struct((1, 128), F32),
        ),
        in_specs=[VM] * 7,
        out_specs=(VM, ANY, ANY, ANY, ANY, VM, ANY, ANY, VM),
        scratch_shapes=[pltpu.VMEM((8, width, width), F32), pltpu.SemaphoreType.DMA((8,))],
        compiler_params=PARAMS,
    )(base, one, two, far_base, far_one, far_two, gain1)
    grad_gain1, grad_wq, grad_wk, grad_wv, grad_wout, grad_gain2, grad_up, grad_down, tiny = results
    return (
        node_out[None],
        grad_feats[None],
        grad_gain1.reshape(width),
        grad_wq,
        grad_wk,
        grad_wv,
        grad_wout,
        grad_gain2.reshape(width),
        grad_up,
        grad_down,
        tiny[0, :heads],
        tiny[0, heads : 2 * heads],
    )


def solution(mesh):
    whole = P()
    rows = P("rep", "dom", None)
    return jax.shard_map(
        local,
        mesh=mesh,
        in_specs=(rows, rows)
        + (whole,) * 10
        + (P("rep", None, "dom", None), rows, P("rep", "dom")),
        out_specs=(rows, rows) + (whole,) * 10,
        check_vma=False,
    )
```

```python
import functools

import jax
import jax.numpy as jnp
from jax import lax
from jax.experimental import pallas as pl
from jax.experimental.pallas import tpu as pltpu
from jax.sharding import PartitionSpec as P

EPSILON = 1e-05
SCORE_CAP = 5.0
GELU_ROOT = 0.7978845608028654
GELU_CUBIC = 0.044715
SMALL = 16
AXES = ("dom", "rep")
VMEM_LIMIT = 48 * 1024 * 1024
F32 = jnp.float32
BF16 = jnp.bfloat16


def dot(a, b):
    return lax.dot_general(a, b, (((1,), (0,)), ((), ())), preferred_element_type=F32)


def dot_rhs_t(a, b):
    return lax.dot_general(a, b, (((1,), (1,)), ((), ())), preferred_element_type=F32)


def dot_lhs_t(a, b):
    return lax.dot_general(a, b, (((0,), (0,)), ((), ())), preferred_element_type=F32)


def norm_forward(matrix):
    center = jnp.mean(matrix, axis=-1, keepdims=True)
    shifted = matrix - center
    inverse = lax.rsqrt(jnp.mean(shifted * shifted, axis=-1, keepdims=True) + EPSILON)
    return (shifted * inverse, inverse)


def norm_backward(upstream, normed, inverse, gain):
    scaled_up = upstream * gain
    return inverse * (
        scaled_up
        - jnp.mean(scaled_up, axis=-1, keepdims=True)
        - normed * jnp.mean(scaled_up * normed, axis=-1, keepdims=True)
    )


def gelu_parts(preact):
    tangent = jnp.tanh(GELU_ROOT * (preact + GELU_CUBIC * preact * preact * preact))
    result = 0.5 * preact * (1.0 + tangent)
    derivative = 0.5 * (1.0 + tangent) + 0.5 * preact * (1.0 - tangent * tangent) * GELU_ROOT * (
        1.0 + 3.0 * GELU_CUBIC * preact * preact
    )
    return (result, derivative)


def split_parts(rows):
    high = rows.astype(BF16).astype(F32)
    return jnp.concatenate([high, rows - high], axis=0).astype(BF16)


def join_parts(packed):
    wide = packed.astype(F32)
    return wide[: SMALL // 2] + wide[SMALL // 2 :]


def device_bits():
    flat = lax.axis_index("dom") * lax.axis_size("rep") + lax.axis_index("rep")
    core = flat & 1
    first = (flat >> 1) & 1
    second = (flat >> 2) & 1
    swap = core == 1
    return (core, jnp.where(swap, second, first), jnp.where(swap, first, second))


def fetch(pairs, sems):
    copies = [pltpu.make_async_copy(src, dst, sems.at[k]) for k, (src, dst) in enumerate(pairs)]
    for copy in copies:
        copy.start()
    return copies


def head_masks_of(shape, heads):
    lane = lax.broadcasted_iota(jnp.int32, shape, 1) // (shape[1] // heads)
    return [lane == h for h in range(heads)]


def stack_heads(matrix, masks):
    return jnp.concatenate([jnp.where(m, matrix, 0.0) for m in masks], axis=0).astype(BF16)


def own_kernel(
    groups,
    feats_ref,
    up_ref,
    gain1_ref,
    wq_hbm,
    wk_hbm,
    wv_hbm,
    wo_hbm,
    wup_hbm,
    wdown_hbm,
    local_ref,
    perm_ref,
    wq_ref,
    wk_ref,
    wv_ref,
    wo_ref,
    wup_ref,
    wdown_ref,
    normed_ref,
    query_ref,
    key_ref,
    value_ref,
    raw_ref,
    tanh_ref,
    exp_ref,
    count_ref,
    back_ref,
    sems,
):
    rows, width = feats_ref.shape
    heads = local_ref.shape[0]
    scale = 1.0 / float(width // heads) ** 0.5
    copies = fetch(
        [
            (wq_hbm, wq_ref),
            (wk_hbm, wk_ref),
            (wv_hbm, wv_ref),
            (wdown_hbm, wdown_ref),
            (wo_hbm, wo_ref),
            (wup_hbm, wup_ref),
        ],
        sems,
    )
    target = lax.broadcasted_iota(jnp.int32, (rows, rows), 0)
    for g, members in enumerate(groups):
        total = 0.0
        for m in members:
            total = total + jnp.where(target == perm_ref[m : m + 1, :], 1.0, 0.0)
        count_ref[:, g * rows : (g + 1) * rows] = total.T
    normed, _ = norm_forward(feats_ref[...].astype(F32))
    normed_ref[...] = normed
    hidden = (normed * gain1_ref[...]).astype(BF16)
    copies[0].wait()
    query = stack_heads(dot(hidden, wq_ref[...]), head_masks_of((rows, width), heads))
    query_ref[...] = query
    copies[1].wait()
    key = dot(hidden, wk_ref[...]).astype(BF16)
    key_ref[...] = key
    copies[2].wait()
    value_ref[...] = dot(hidden, wv_ref[...]).astype(BF16)
    raw_ref[...] = dot_rhs_t(query, key) * scale
    for h in range(heads):
        block = pl.ds(h * rows, rows)
        tangent = jnp.tanh(raw_ref[block, :] * (local_ref[h] / SCORE_CAP))
        tanh_ref[block, :] = tangent
        exp_ref[block, :] = jnp.exp(SCORE_CAP * tangent)
    copies[3].wait()
    back_ref[...] = dot_rhs_t(up_ref[...], wdown_ref[...])
    copies[4].wait()
    copies[5].wait()


def layer_kernel(slots, count, *refs):
    others = refs[:count]
    (
        feats_ref,
        up_ref,
        gain1_ref,
        gain2_ref,
        wq_ref,
        wk_ref,
        wv_ref,
        wo_ref,
        wup_ref,
        wdown_ref,
        normed_ref,
        query_ref,
        key_ref,
        value_ref,
        raw_ref,
        tanh_ref,
        exp_ref,
        count_ref,
        back_ref,
        local_ref,
        far_ref,
        out_ref,
        keep_ref,
        send_ref,
        own_ref,
        mixed_ref,
    ) = refs[count : count + 26]
    slot_refs = refs[count + 26 : count + 26 + len(slots)]
    raw_s, tanh_s, wl_s, wf_s, dl_s, df_s = refs[count + 26 + len(slots) :]

    rows, width = out_ref.shape
    heads = local_ref.shape[0]
    scale = 1.0 / float(width // heads) ** 0.5
    core, level1, level2 = device_bits()
    half = 4 * width

    def put(chunk, value):
        value = value.astype(BF16)
        upper = (chunk >> 1) & 1
        lower = chunk & 1
        same = core == (chunk >> 2)

        @pl.when(same)
        def _():
            rel = (upper ^ level1) * 2 + (lower ^ level2)
            keep_ref[pl.ds(pl.multiple_of(rel * width, width), width), :] = value

        @pl.when(jnp.logical_not(same))
        def _():
            rel = (upper ^ level2) * 2 + (lower ^ level1)
            send_ref[pl.ds(pl.multiple_of(rel * width, width), width), :] = value

    gain1 = gain1_ref[...]
    gain2 = gain2_ref[...]
    upstream = up_ref[...]
    masks = head_masks_of((rows, width), heads)
    normed_far, _ = norm_forward(jnp.concatenate([ref[...] for ref in others], axis=0).astype(F32))
    hidden_far = (normed_far * gain1).astype(BF16)
    key_far = dot(hidden_far, wk_ref[...]).astype(BF16)
    value_far = dot(hidden_far, wv_ref[...]).astype(BF16)
    query_stack = query_ref[...]
    raw_s[...] = dot_rhs_t(query_stack, key_far) * scale
    far_counts = count_ref[...]

    for h in range(heads):
        block = pl.ds(h * rows, rows)
        tangent = jnp.tanh(raw_s[block, :] * (far_ref[h] / SCORE_CAP))
        near = exp_ref[block, :]
        far = jnp.exp(SCORE_CAP * tangent) * far_counts
        inv = 1.0 / (jnp.sum(near, axis=1, keepdims=True) + jnp.sum(far, axis=1, keepdims=True))
        tanh_s[block, :] = tangent
        wl_s[block, :] = (near * inv).astype(BF16)
        wf_s[block, :] = (far * inv).astype(BF16)

    def collapse(matrix):
        total = jnp.where(masks[0], matrix[:rows], 0.0)
        for h in range(1, heads):
            total = total + jnp.where(masks[h], matrix[h * rows : (h + 1) * rows], 0.0)
        return total

    attended32 = collapse(dot(wl_s[...], value_ref[...]) + dot(wf_s[...], value_far))
    attended = attended32.astype(BF16)
    mixed = (feats_ref[...].astype(F32) + dot(attended, wo_ref[...])).astype(BF16)
    normed2, inverse2 = norm_forward(mixed.astype(F32))
    hidden2 = (normed2 * gain2).astype(BF16)
    preact = dot(hidden2, wup_ref[...])
    act32, derivative = gelu_parts(preact)
    act = act32.astype(BF16)
    out_ref[...] = (mixed.astype(F32) + dot(act, wdown_ref[...])).astype(BF16)
    grad_down = dot_lhs_t(act, upstream)
    put(6, grad_down[:width])
    put(7, grad_down[width:])
    grad_pre = (back_ref[...] * derivative).astype(BF16)
    grad_up = dot_lhs_t(hidden2, grad_pre)
    put(4, grad_up[:, :width])
    put(5, grad_up[:, width:])
    grad_hidden2 = dot_rhs_t(grad_pre, wup_ref[...])
    grad_gain2 = jnp.sum(grad_hidden2 * normed2, axis=0, keepdims=True)
    grad_mixed = upstream.astype(F32) + norm_backward(grad_hidden2, normed2, inverse2, gain2)
    mixed_ref[...] = grad_mixed
    grad_mixed16 = grad_mixed.astype(BF16)
    put(3, dot_lhs_t(attended, grad_mixed16))
    grad_att = dot_rhs_t(grad_mixed16, wo_ref[...]).astype(BF16).astype(F32)
    grad_stack = stack_heads(grad_att, masks)
    product = grad_att * attended32
    near_dots = dot_rhs_t(grad_stack, value_ref[...])
    far_dots = dot_rhs_t(grad_stack, value_far)

    near_terms = []
    far_terms = []
    for h in range(heads):
        block = pl.ds(h * rows, rows)
        span = slice(h * rows, (h + 1) * rows)
        delta = jnp.sum(jnp.where(masks[h], product, 0.0), axis=1, keepdims=True)
        for weights, dots, tangents, raw, dscore, gain, terms in (
            (wl_s, near_dots, tanh_ref, raw_ref, dl_s, local_ref[h], near_terms),
            (wf_s, far_dots, tanh_s, raw_s, df_s, far_ref[h], far_terms),
        ):
            tangent = tangents[block, :]
            slope = 1.0 - tangent * tangent
            sloped = weights[block, :].astype(F32) * (dots[span] - delta) * slope
            total = jnp.sum(sloped * raw[block, :], axis=0, keepdims=True)
            terms.append(jnp.sum(total, axis=1, keepdims=True))
            dscore[block, :] = (sloped * (gain * scale)).astype(BF16)

    grad_query = collapse(dot(dl_s[...], key_ref[...]) + dot(df_s[...], key_far)).astype(BF16)
    key_near16 = dot_lhs_t(dl_s[...], query_stack).astype(BF16)
    value_near16 = dot_lhs_t(wl_s[...], grad_stack).astype(BF16)
    key_far16 = dot_lhs_t(df_s[...], query_stack).astype(BF16)
    value_far16 = dot_lhs_t(wf_s[...], grad_stack).astype(BF16)
    normed1 = normed_ref[...]
    hidden = (normed1 * gain1).astype(BF16)
    put(0, dot_lhs_t(hidden, grad_query))
    put(1, dot_lhs_t(hidden, key_near16) + dot_lhs_t(hidden_far, key_far16))
    put(2, dot_lhs_t(hidden, value_near16) + dot_lhs_t(hidden_far, value_far16))
    own = (
        dot_rhs_t(key_near16, wk_ref[...])
        + dot_rhs_t(value_near16, wv_ref[...])
        + dot_rhs_t(grad_query, wq_ref[...])
    )
    own_ref[...] = own
    theirs = dot_rhs_t(key_far16, wk_ref[...]) + dot_rhs_t(value_far16, wv_ref[...])
    grad_gain1 = jnp.sum(own * normed1, axis=0, keepdims=True)
    grad_gain1 = grad_gain1 + jnp.sum(theirs * normed_far, axis=0, keepdims=True)
    back = [theirs[k * rows : (k + 1) * rows] for k in range(count)]
    for (even, odd), ref in zip(slots, slot_refs):
        ref[...] = jnp.where(
            core == 1, 0.0 if odd is None else back[odd], 0.0 if even is None else back[even]
        ).astype(BF16)

    column = lax.broadcasted_iota(jnp.int32, (1, width), 1)
    gains = jnp.zeros((1, width), F32)
    for h in range(heads):
        gains = jnp.where(column == h, near_terms[h], gains)
        gains = jnp.where(column == heads + h, far_terms[h], gains)
    line = lax.broadcasted_iota(jnp.int32, (SMALL // 2, width), 0)
    small = jnp.where(line == 0, grad_gain1, jnp.where(line == 1, grad_gain2, jnp.where(line == 2, gains, 0.0)))
    send_ref[half:, :] = split_parts(small)


def merge_kernel(rows, halve, *refs):
    keep_ref, sent_ref, recv_ref = refs[:3]
    slot = refs[3:4] if len(refs) == (6 if halve else 5) else ()
    total = keep_ref[:rows, :].astype(F32) + recv_ref[:rows, :].astype(F32)
    total = total.astype(BF16)
    span = slice(rows, rows + SMALL)
    packed = split_parts(join_parts(sent_ref[span, :]) + join_parts(recv_ref[span, :]))
    next_ref = refs[-1]
    size = rows // 2 if halve else rows
    if halve:
        refs[-2][...] = total[:size]
    next_ref[:size, :] = total[size:] if halve else total
    next_ref[size : size + SMALL, :] = packed
    if slot:
        next_ref[size + SMALL :, :] = slot[0][...]


def tail_kernel(start, *refs):
    feats_ref, own_ref, mixed_ref, gain_ref = refs[:4]
    normed, inverse = norm_forward(feats_ref[...].astype(F32))
    grad_hidden = own_ref[...]
    for ref, first in zip(refs[4:-1], start):
        grad_hidden = grad_hidden + ref[first:, :].astype(F32)
    refs[-1][...] = (mixed_ref[...] + norm_backward(grad_hidden, normed, inverse, gain_ref[...])).astype(BF16)


def spread_kernel(
    pieces_ref,
    base_ref,
    gain1_ref,
    wq_ref,
    wk_ref,
    wv_ref,
    wo_ref,
    gain2_ref,
    up_ref,
    down_ref,
    local_ref,
    far_ref,
    chunks,
    sems,
):
    width = wq_ref.shape[0]
    heads = local_ref.shape[0]
    core, level1, level2 = device_bits()
    targets = [
        wq_ref,
        wk_ref,
        wv_ref,
        wo_ref,
        up_ref.at[:, :width],
        up_ref.at[:, width:],
        down_ref.at[:width, :],
        down_ref.at[width:, :],
    ]
    copies = []
    for chunk, target in enumerate(targets):
        other = core ^ (chunk >> 2)
        upper = (chunk >> 1) & 1
        lower = chunk & 1
        rel = jnp.where(
            other == 1,
            4 + (upper ^ level2) * 2 + (lower ^ level1),
            (upper ^ level1) * 2 + (lower ^ level2),
        )
        start = pl.multiple_of(rel * width, width)
        chunks[chunk] = pieces_ref[pl.ds(start, width), :].astype(F32)
        copy = pltpu.make_async_copy(chunks.at[chunk], target, sems.at[chunk])
        copy.start()
        copies.append(copy)
    small = join_parts(base_ref[width:, :])
    gain1_ref[...] = small[0:1]
    gain2_ref[...] = small[1:2]
    local_ref[...] = small[2, :heads]
    far_ref[...] = small[2, heads : 2 * heads]
    for copy in copies:
        copy.wait()


def struct(shape, dtype):
    return jax.ShapeDtypeStruct(shape, dtype)


VM = pl.BlockSpec(memory_space=pltpu.VMEM)
SM = pl.BlockSpec(memory_space=pltpu.SMEM)
ANY = pl.BlockSpec(memory_space=pl.ANY)
PARAMS = pltpu.CompilerParams(vmem_limit_bytes=VMEM_LIMIT)


def call(kernel, outs, *args, in_specs=None, **kwargs):
    return pl.pallas_call(
        kernel,
        out_shape=outs,
        in_specs=in_specs or [VM] * len(args),
        out_specs=jax.tree.map(lambda _: VM, outs),
        compiler_params=PARAMS,
        **kwargs,
    )(*args)


def flipped(x, bits_even, bits_odd):
    size = lax.axis_size("dom") * lax.axis_size("rep")
    pairs = [(i, i ^ (bits_odd if i & 1 else bits_even)) for i in range(size)]
    return lax.ppermute(x, AXES, pairs)


def local(
    node_feats,
    out_grad,
    norm1_gain,
    w_query,
    w_key,
    w_value,
    w_out,
    norm2_gain,
    w_up,
    w_down,
    local_gain,
    expander_gain,
    partner_perm,
    block_pairs,
    pair_count,
):
    feats = node_feats[0]
    partners = partner_perm[0, :, 0, :]
    rows, width = feats.shape
    heads = local_gain.shape[0]
    size = lax.axis_size("dom") * lax.axis_size("rep")
    levels = lax.axis_size("dom").bit_length() - 1
    by_bit = {}
    for matching in range(partners.shape[0]):
        by_bit.setdefault((levels - 1 - matching) % levels, []).append(matching)
    bits = list(by_bit)
    groups = [by_bit[b] for b in bits]

    def swapped(x, bit):
        return lax.ppermute(x, "dom", [(i, i ^ 1 << bit) for i in range(lax.axis_size("dom"))])

    rep_bits = lax.axis_size("rep").bit_length() - 1
    high_bits = [1 << k for k in range(3, size.bit_length() - 1)]
    steps = [(1, 1), (2, 4), (4, 2)] + list(zip(high_bits, high_bits[::-1]))
    flat = {1 << (b + rep_bits): k for k, b in enumerate(bits)}
    slots = [(flat.get(even), flat.get(odd)) for even, odd in steps]
    filled = [k for k, pair in enumerate(slots) if pair != (None, None)]
    assert filled[0] > 0 and len(set(flat)) == len(bits)

    others = [swapped(feats, b) for b in bits]
    count = len(bits)
    tall = count * rows
    stacked = heads * rows
    gain1 = norm1_gain.reshape(1, width)
    gain2 = norm2_gain.reshape(1, width)
    upstream = out_grad[0]
    weights = (w_query, w_key, w_value, w_out, w_up, w_down)
    prepared = call(
        functools.partial(own_kernel, groups),
        tuple(struct(w.shape, BF16) for w in weights)
        + (
            struct((rows, width), F32),
            struct((stacked, width), BF16),
            struct((rows, width), BF16),
            struct((rows, width), BF16),
            struct((stacked, rows), F32),
            struct((stacked, rows), F32),
            struct((stacked, rows), F32),
            struct((rows, tall), F32),
            struct((rows, w_up.shape[1]), F32),
        ),
        feats,
        upstream,
        gain1,
        *weights,
        local_gain,
        partners,
        in_specs=[VM] * 3 + [ANY] * 6 + [SM, VM],
        scratch_shapes=[pltpu.SemaphoreType.DMA((6,))],
    )
    node_out, keep, send, own, grad_mixed, *slot_rows = call(
        functools.partial(layer_kernel, [slots[k] for k in filled], count),
        (
            struct((rows, width), BF16),
            struct((4 * width, width), BF16),
            struct((4 * width + SMALL, width), BF16),
            struct((rows, width), F32),
            struct((rows, width), F32),
        )
        + tuple(struct((rows, width), BF16) for _ in filled),
        *others,
        feats,
        upstream,
        gain1,
        gain2,
        *prepared,
        local_gain,
        expander_gain,
        in_specs=[VM] * (count + 19) + [SM, SM],
        scratch_shapes=[
            pltpu.VMEM((stacked, tall), F32),
            pltpu.VMEM((stacked, tall), F32),
            pltpu.VMEM((stacked, rows), BF16),
            pltpu.VMEM((stacked, tall), BF16),
            pltpu.VMEM((stacked, rows), BF16),
            pltpu.VMEM((stacked, tall), BF16),
        ],
    )
    slot_at = dict(zip(filled, slot_rows))

    returned = []
    starts = []
    data = 4 * width
    for k, (even, odd) in enumerate(steps):
        recv = flipped(send, even, odd)
        if k in slot_at:
            returned.append(recv)
            starts.append(data + SMALL)
        halve = k < 2
        size_next = data // 2 if halve else data
        extra = [slot_at[k + 1]] if k + 1 in slot_at else []
        outs = (struct((size_next + SMALL + rows * len(extra), width), BF16),)
        if halve:
            outs = (struct((size_next, width), BF16),) + outs
        res = call(
            functools.partial(merge_kernel, data, halve),
            outs,
            keep if k <= 2 else send,
            send,
            recv,
            *extra,
        )
        keep, send = res[0], res[-1]
        data = size_next
    base = send
    grad_feats = call(
        functools.partial(tail_kernel, starts),
        struct((rows, width), BF16),
        feats,
        own,
        grad_mixed,
        gain1,
        *returned,
    )

    one = flipped(base[:width], 4, 2)
    near = jnp.concatenate([base[:width], one], axis=0)
    near = jnp.concatenate([near, flipped(near, 2, 4)], axis=0)
    pieces = jnp.concatenate([near, flipped(near, 1, 1)], axis=0)
    square = struct((width, width), F32)
    results = pl.pallas_call(
        spread_kernel,
        out_shape=(
            struct((1, width), F32),
            square,
            square,
            square,
            square,
            struct((1, width), F32),
            struct((width, 2 * width), F32),
            struct((2 * width, width), F32),
            struct((heads,), F32),
            struct((heads,), F32),
        ),
        in_specs=[VM] * 2,
        out_specs=(VM, ANY, ANY, ANY, ANY, VM, ANY, ANY, VM, VM),
        scratch_shapes=[pltpu.VMEM((8, width, width), F32), pltpu.SemaphoreType.DMA((8,))],
        compiler_params=PARAMS,
    )(pieces, base)
    grad_gain1, grad_wq, grad_wk, grad_wv, grad_wout, grad_gain2, grad_up, grad_down, grad_local, grad_far = results
    return (
        node_out[None],
        grad_feats[None],
        grad_gain1.reshape(width),
        grad_wq,
        grad_wk,
        grad_wv,
        grad_wout,
        grad_gain2.reshape(width),
        grad_up,
        grad_down,
        grad_local,
        grad_far,
    )


def solution(mesh):
    whole = P()
    rows = P("rep", "dom", None)
    return jax.shard_map(
        local,
        mesh=mesh,
        in_specs=(rows, rows)
        + (whole,) * 10
        + (P("rep", None, "dom", None), rows, P("rep", "dom")),
        out_specs=(rows, rows) + (whole,) * 10,
        check_vma=False,
    )
```

```python
import functools

import jax
import jax.numpy as jnp
from jax import lax
from jax.experimental import pallas as pl
from jax.experimental.pallas import tpu as pltpu
from jax.sharding import PartitionSpec as P

EPSILON = 1e-05
SCORE_CAP = 5.0
GELU_ROOT = 0.7978845608028654
GELU_CUBIC = 0.044715
SMALL = 16
AXES = ("dom", "rep")
VMEM_LIMIT = 48 * 1024 * 1024
F32 = jnp.float32
BF16 = jnp.bfloat16


def dot(a, b):
    return lax.dot_general(a, b, (((1,), (0,)), ((), ())), preferred_element_type=F32)


def dot_rhs_t(a, b):
    return lax.dot_general(a, b, (((1,), (1,)), ((), ())), preferred_element_type=F32)


def dot_lhs_t(a, b):
    return lax.dot_general(a, b, (((0,), (0,)), ((), ())), preferred_element_type=F32)


def norm_forward(matrix):
    center = jnp.mean(matrix, axis=-1, keepdims=True)
    shifted = matrix - center
    inverse = lax.rsqrt(jnp.mean(shifted * shifted, axis=-1, keepdims=True) + EPSILON)
    return (shifted * inverse, inverse)


def norm_backward(upstream, normed, inverse, gain):
    scaled_up = upstream * gain
    return inverse * (
        scaled_up
        - jnp.mean(scaled_up, axis=-1, keepdims=True)
        - normed * jnp.mean(scaled_up * normed, axis=-1, keepdims=True)
    )


def gelu_parts(preact):
    tangent = jnp.tanh(GELU_ROOT * (preact + GELU_CUBIC * preact * preact * preact))
    result = 0.5 * preact * (1.0 + tangent)
    derivative = 0.5 * (1.0 + tangent) + 0.5 * preact * (1.0 - tangent * tangent) * GELU_ROOT * (
        1.0 + 3.0 * GELU_CUBIC * preact * preact
    )
    return (result, derivative)


def split_parts(rows):
    high = rows.astype(BF16).astype(F32)
    return jnp.concatenate([high, rows - high], axis=0).astype(BF16)


def join_parts(packed):
    wide = packed.astype(F32)
    return wide[: SMALL // 2] + wide[SMALL // 2 :]


def device_bits():
    flat = lax.axis_index("dom") * lax.axis_size("rep") + lax.axis_index("rep")
    return (flat & 1, (flat >> 1) & 3)


def head_masks_of(shape, heads):
    lane = lax.broadcasted_iota(jnp.int32, shape, 1) // (shape[1] // heads)
    return [lane == h for h in range(heads)]


def stack_heads(matrix, masks):
    return jnp.concatenate([jnp.where(m, matrix, 0.0) for m in masks], axis=0).astype(BF16)


def first_kernel(groups, feats_ref, gain1_ref, perm_ref, normed_ref, hidden_ref, count_ref):
    rows = feats_ref.shape[0]
    target = lax.broadcasted_iota(jnp.int32, (rows, rows), 0)
    for g, members in enumerate(groups):
        total = 0.0
        for m in members:
            total = total + jnp.where(target == perm_ref[m : m + 1, :], 1.0, 0.0)
        count_ref[:, g * rows : (g + 1) * rows] = total.T
    normed, _ = norm_forward(feats_ref[...].astype(F32))
    normed_ref[...] = normed
    hidden_ref[...] = (normed * gain1_ref[...]).astype(BF16)


def own_kernel(
    hidden_ref,
    up_ref,
    wq_ref,
    wk_ref,
    wv_ref,
    wdown_ref,
    local_ref,
    query_ref,
    key_ref,
    value_ref,
    raw_ref,
    tanh_ref,
    exp_ref,
    back_ref,
):
    rows, width = hidden_ref.shape
    heads = local_ref.shape[0]
    scale = 1.0 / float(width // heads) ** 0.5
    hidden = hidden_ref[...]
    query = stack_heads(dot(hidden, wq_ref[...]), head_masks_of((rows, width), heads))
    query_ref[...] = query
    key = dot(hidden, wk_ref[...]).astype(BF16)
    key_ref[...] = key
    value_ref[...] = dot(hidden, wv_ref[...]).astype(BF16)
    raw_ref[...] = dot_rhs_t(query, key) * scale
    for h in range(heads):
        block = pl.ds(h * rows, rows)
        tangent = jnp.tanh(raw_ref[block, :] * (local_ref[h] / SCORE_CAP))
        tanh_ref[block, :] = tangent
        exp_ref[block, :] = jnp.exp(SCORE_CAP * tangent)
    back_ref[...] = dot_rhs_t(up_ref[...], wdown_ref[...])


def put_unit(keep_ref, send_ref, bits, unit, value):
    core, quad = bits
    rows = value.shape[0]
    span = pl.ds(pl.multiple_of(((unit & 3) ^ quad) * rows, rows), rows)
    same = core == (unit >> 2)

    @pl.when(same)
    def _():
        keep_ref[span, :] = value

    @pl.when(jnp.logical_not(same))
    def _():
        send_ref[span, :] = value


def put_square(keep_ref, send_ref, bits, chunk, value):
    value = value.astype(BF16)
    half = value.shape[0] // 2
    put_unit(keep_ref, send_ref, bits, 2 * chunk, value[:half])
    put_unit(keep_ref, send_ref, bits, 2 * chunk + 1, value[half:])


def collapse(matrix, masks):
    rows = matrix.shape[0] // len(masks)
    total = jnp.where(masks[0], matrix[:rows], 0.0)
    for h in range(1, len(masks)):
        total = total + jnp.where(masks[h], matrix[h * rows : (h + 1) * rows], 0.0)
    return total


def forward_kernel(count, *refs):
    others = refs[:count]
    (
        feats_ref,
        up_ref,
        gain1_ref,
        gain2_ref,
        wk_ref,
        wv_ref,
        wo_ref,
        wup_ref,
        wdown_ref,
        query_ref,
        value_ref,
        exp_ref,
        count_ref,
        back_ref,
        far_ref,
        out_ref,
        keep_ref,
        send_ref,
        mixed_ref,
        gain_ref,
        normed_ref,
        hidden_ref,
        keyf_ref,
        valuef_ref,
        raw_ref,
        tanh_ref,
        wl_ref,
        wf_ref,
        att_ref,
    ) = refs[count:]
    rows, width = out_ref.shape
    heads = far_ref.shape[0]
    scale = 1.0 / float(width // heads) ** 0.5
    bits = device_bits()
    upstream = up_ref[...]
    masks = head_masks_of((rows, width), heads)
    normed_far, _ = norm_forward(jnp.concatenate([ref[...] for ref in others], axis=0).astype(F32))
    normed_ref[...] = normed_far
    hidden_far = (normed_far * gain1_ref[...]).astype(BF16)
    hidden_ref[...] = hidden_far
    key_far = dot(hidden_far, wk_ref[...]).astype(BF16)
    value_far = dot(hidden_far, wv_ref[...]).astype(BF16)
    keyf_ref[...] = key_far
    valuef_ref[...] = value_far
    raw_ref[...] = dot_rhs_t(query_ref[...], key_far) * scale
    far_counts = count_ref[...]
    for h in range(heads):
        block = pl.ds(h * rows, rows)
        tangent = jnp.tanh(raw_ref[block, :] * (far_ref[h] / SCORE_CAP))
        near = exp_ref[block, :]
        far = jnp.exp(SCORE_CAP * tangent) * far_counts
        inv = 1.0 / (jnp.sum(near, axis=1, keepdims=True) + jnp.sum(far, axis=1, keepdims=True))
        tanh_ref[block, :] = tangent
        wl_ref[block, :] = (near * inv).astype(BF16)
        wf_ref[block, :] = (far * inv).astype(BF16)

    attended32 = collapse(dot(wl_ref[...], value_ref[...]) + dot(wf_ref[...], value_far), masks)
    att_ref[...] = attended32
    mixed = (feats_ref[...].astype(F32) + dot(attended32.astype(BF16), wo_ref[...])).astype(BF16)
    normed2, inverse2 = norm_forward(mixed.astype(F32))
    gain2 = gain2_ref[...]
    hidden2 = (normed2 * gain2).astype(BF16)
    preact = dot(hidden2, wup_ref[...])
    act32, derivative = gelu_parts(preact)
    act = act32.astype(BF16)
    grad_down = dot_lhs_t(act, upstream)
    put_square(keep_ref, send_ref, bits, 2, grad_down[:width])
    put_square(keep_ref, send_ref, bits, 3, grad_down[width:])
    grad_pre = (back_ref[...] * derivative).astype(BF16)
    grad_up = dot_lhs_t(hidden2, grad_pre)
    put_square(keep_ref, send_ref, bits, 0, grad_up[:, :width])
    put_square(keep_ref, send_ref, bits, 1, grad_up[:, width:])
    out_ref[...] = (mixed.astype(F32) + dot(act, wdown_ref[...])).astype(BF16)
    grad_hidden2 = dot_rhs_t(grad_pre, wup_ref[...])
    gain_ref[...] = jnp.sum(grad_hidden2 * normed2, axis=0, keepdims=True)
    mixed_ref[...] = upstream.astype(F32) + norm_backward(grad_hidden2, normed2, inverse2, gain2)


def backward_kernel(slots, count, *refs):
    (
        gain1_ref,
        gain2g_ref,
        wq_ref,
        wk_ref,
        wv_ref,
        wo_ref,
        near_hidden_ref,
        near_normed_ref,
        query_ref,
        key_ref,
        value_ref,
        rawl_ref,
        tanhl_ref,
        mixed_ref,
        normed_ref,
        hidden_ref,
        keyf_ref,
        valuef_ref,
        rawf_ref,
        tanhf_ref,
        wl_ref,
        wf_ref,
        att_ref,
        local_ref,
        far_ref,
        keep_ref,
        send_ref,
        own_ref,
    ) = refs[:28]
    slot_refs = refs[28 : 28 + len(slots)]
    dl_s, df_s = refs[28 + len(slots) :]
    rows, width = own_ref.shape
    heads = far_ref.shape[0]
    scale = 1.0 / float(width // heads) ** 0.5
    bits = device_bits()
    core = bits[0]
    masks = head_masks_of((rows, width), heads)
    attended32 = att_ref[...]
    grad_mixed16 = mixed_ref[...].astype(BF16)
    put_square(keep_ref, send_ref, bits, 3, dot_lhs_t(attended32.astype(BF16), grad_mixed16))
    grad_att = dot_rhs_t(grad_mixed16, wo_ref[...]).astype(BF16).astype(F32)
    grad_stack = stack_heads(grad_att, masks)
    product = grad_att * attended32
    near_dots = dot_rhs_t(grad_stack, value_ref[...])
    far_dots = dot_rhs_t(grad_stack, valuef_ref[...])

    near_terms = []
    far_terms = []
    for h in range(heads):
        block = pl.ds(h * rows, rows)
        span = slice(h * rows, (h + 1) * rows)
        delta = jnp.sum(jnp.where(masks[h], product, 0.0), axis=1, keepdims=True)
        for weights, dots, tangents, raw, dscore, gain, terms in (
            (wl_ref, near_dots, tanhl_ref, rawl_ref, dl_s, local_ref[h], near_terms),
            (wf_ref, far_dots, tanhf_ref, rawf_ref, df_s, far_ref[h], far_terms),
        ):
            tangent = tangents[block, :]
            slope = 1.0 - tangent * tangent
            sloped = weights[block, :].astype(F32) * (dots[span] - delta) * slope
            total = jnp.sum(sloped * raw[block, :], axis=0, keepdims=True)
            terms.append(jnp.sum(total, axis=1, keepdims=True))
            dscore[block, :] = (sloped * (gain * scale)).astype(BF16)

    query_stack = query_ref[...]
    grad_query = collapse(dot(dl_s[...], key_ref[...]) + dot(df_s[...], keyf_ref[...]), masks).astype(BF16)
    key_near = dot_lhs_t(dl_s[...], query_stack).astype(BF16)
    value_near = dot_lhs_t(wl_ref[...], grad_stack).astype(BF16)
    key_far = dot_lhs_t(df_s[...], query_stack).astype(BF16)
    value_far = dot_lhs_t(wf_ref[...], grad_stack).astype(BF16)
    hidden = near_hidden_ref[...]
    hidden_far = hidden_ref[...]
    put_square(keep_ref, send_ref, bits, 0, dot_lhs_t(hidden, grad_query))
    put_square(keep_ref, send_ref, bits, 1, dot_lhs_t(hidden, key_near) + dot_lhs_t(hidden_far, key_far))
    put_square(keep_ref, send_ref, bits, 2, dot_lhs_t(hidden, value_near) + dot_lhs_t(hidden_far, value_far))
    own = (
        dot_rhs_t(key_near, wk_ref[...])
        + dot_rhs_t(value_near, wv_ref[...])
        + dot_rhs_t(grad_query, wq_ref[...])
    )
    own_ref[...] = own
    theirs = dot_rhs_t(key_far, wk_ref[...]) + dot_rhs_t(value_far, wv_ref[...])
    grad_gain1 = jnp.sum(own * near_normed_ref[...], axis=0, keepdims=True)
    grad_gain1 = grad_gain1 + jnp.sum(theirs * normed_ref[...], axis=0, keepdims=True)
    back = [theirs[k * rows : (k + 1) * rows] for k in range(count)]
    for (even, odd), ref in zip(slots, slot_refs):
        ref[...] = jnp.where(
            core == 1, 0.0 if odd is None else back[odd], 0.0 if even is None else back[even]
        ).astype(BF16)

    column = lax.broadcasted_iota(jnp.int32, (1, width), 1)
    gains = jnp.zeros((1, width), F32)
    for h in range(heads):
        gains = jnp.where(column == h, near_terms[h], gains)
        gains = jnp.where(column == heads + h, far_terms[h], gains)
    line = lax.broadcasted_iota(jnp.int32, (SMALL // 2, width), 0)
    small = jnp.where(line == 0, grad_gain1, jnp.where(line == 1, gain2g_ref[...], jnp.where(line == 2, gains, 0.0)))
    send_ref[keep_ref.shape[0] :, :] = split_parts(small)


def pair_kernel(slots, keepw_ref, recvw_ref, keeps_ref, sents_ref, recvs_ref, *refs):
    slot_refs = refs[: sum(slots)]
    out_refs = refs[sum(slots) :]
    rows = keepw_ref.shape[0] // 4
    wide = (keepw_ref[...].astype(F32) + recvw_ref[...].astype(F32)).astype(BF16)
    square = (keeps_ref[...].astype(F32) + recvs_ref[: 4 * rows, :].astype(F32)).astype(BF16)
    packed = split_parts(join_parts(sents_ref[4 * rows :, :]) + join_parts(recvs_ref[4 * rows :, :]))
    used = 0
    for r in range(4):
        span = slice(r * rows, (r + 1) * rows)
        out_refs[r][:rows, :] = wide[span]
        out_refs[r][rows : 2 * rows, :] = square[span]
        out_refs[r][2 * rows : 2 * rows + SMALL, :] = packed
        if r and slots[r - 1]:
            out_refs[r][2 * rows + SMALL :, :] = slot_refs[used][...]
            used += 1


def quad_kernel(has_slot, own_ref, one_ref, two_ref, three_ref, *refs):
    wide_ref, square_ref = refs[-2:]
    total_rows = own_ref.shape[0]
    rows = (total_rows - SMALL) // 2
    data = [ref[: 2 * rows, :].astype(F32) for ref in (own_ref, one_ref, two_ref, three_ref)]
    small = [join_parts(ref[2 * rows : total_rows, :]) for ref in (own_ref, one_ref, two_ref, three_ref)]
    total = ((data[0] + data[1]) + (data[2] + data[3])).astype(BF16)
    wide_ref[:rows, :] = total[:rows]
    square_ref[:rows, :] = total[rows:]
    square_ref[rows:, :] = split_parts((small[0] + small[1]) + (small[2] + small[3]))
    if has_slot:
        wide_ref[rows:, :] = refs[0][...]


def double_kernel(rows, small, has_slot, own_ref, recv_ref, *refs):
    out_ref = refs[-1]
    total = own_ref[:rows, :].astype(F32) + recv_ref[:rows, :].astype(F32)
    out_ref[:rows, :] = total.astype(BF16)
    if small:
        span = slice(rows, rows + SMALL)
        out_ref[span, :] = split_parts(join_parts(own_ref[span, :]) + join_parts(recv_ref[span, :]))
    if has_slot:
        out_ref[rows:, :] = refs[0][...]


def join_kernel(wide_ref, square_ref, out_ref):
    rows = out_ref.shape[0] // 2
    out_ref[:rows, :] = wide_ref[:rows, :]
    out_ref[rows:, :] = square_ref[:rows, :]


def tail_kernel(start, *refs):
    feats_ref, own_ref, mixed_ref, gain_ref = refs[:4]
    normed, inverse = norm_forward(feats_ref[...].astype(F32))
    grad_hidden = own_ref[...]
    for ref, first in zip(refs[4:-1], start):
        grad_hidden = grad_hidden + ref[first:, :].astype(F32)
    refs[-1][...] = (mixed_ref[...] + norm_backward(grad_hidden, normed, inverse, gain_ref[...])).astype(BF16)


def spread_kernel(*refs):
    piece_refs = refs[:8]
    small_ref = refs[8]
    (
        gain1_ref,
        wq_ref,
        wk_ref,
        wv_ref,
        wo_ref,
        gain2_ref,
        up_ref,
        down_ref,
        local_ref,
        far_ref,
        pieces,
        chunks,
        sems,
    ) = refs[9:]
    width = wq_ref.shape[0]
    half = width // 2
    heads = local_ref.shape[0]
    core, quad = device_bits()
    for k, ref in enumerate(piece_refs):
        pieces[k] = ref[...]
    targets = [
        up_ref.at[:, :width],
        up_ref.at[:, width:],
        down_ref.at[:width, :],
        down_ref.at[width:, :],
        wq_ref,
        wk_ref,
        wv_ref,
        wo_ref,
    ]
    copies = []
    for chunk, target in enumerate(targets):
        first = 0 if chunk < 4 else half
        for part in range(2):
            unit = 2 * (chunk % 4) + part
            rel = (core ^ (unit >> 2)) * 4 + (quad ^ (unit & 3))
            value = pieces[rel, first : first + half, :]
            chunks[chunk, part * half : (part + 1) * half, :] = value.astype(F32)
        copy = pltpu.make_async_copy(chunks.at[chunk], target, sems.at[chunk])
        copy.start()
        copies.append(copy)
    small = join_parts(small_ref[small_ref.shape[0] - SMALL :, :])
    gain1_ref[...] = small[0:1]
    gain2_ref[...] = small[1:2]
    local_ref[...] = small[2, :heads]
    far_ref[...] = small[2, heads : 2 * heads]
    for copy in copies:
        copy.wait()


def struct(shape, dtype):
    return jax.ShapeDtypeStruct(shape, dtype)


VM = pl.BlockSpec(memory_space=pltpu.VMEM)
SM = pl.BlockSpec(memory_space=pltpu.SMEM)
ANY = pl.BlockSpec(memory_space=pl.ANY)
PARAMS = pltpu.CompilerParams(vmem_limit_bytes=VMEM_LIMIT)


def call(kernel, outs, *args, in_specs=None, **kwargs):
    return pl.pallas_call(
        kernel,
        out_shape=outs,
        in_specs=in_specs or [VM] * len(args),
        out_specs=jax.tree.map(lambda _: VM, outs),
        compiler_params=PARAMS,
        **kwargs,
    )(*args)


def flipped(x, bits_even, bits_odd):
    size = lax.axis_size("dom") * lax.axis_size("rep")
    pairs = [(i, i ^ (bits_odd if i & 1 else bits_even)) for i in range(size)]
    return lax.ppermute(x, AXES, pairs)


def local(
    node_feats,
    out_grad,
    norm1_gain,
    w_query,
    w_key,
    w_value,
    w_out,
    norm2_gain,
    w_up,
    w_down,
    local_gain,
    expander_gain,
    partner_perm,
    block_pairs,
    pair_count,
):
    feats = node_feats[0]
    partners = partner_perm[0, :, 0, :]
    rows, width = feats.shape
    heads = local_gain.shape[0]
    size = lax.axis_size("dom") * lax.axis_size("rep")
    levels = lax.axis_size("dom").bit_length() - 1
    by_bit = {}
    for matching in range(partners.shape[0]):
        by_bit.setdefault((levels - 1 - matching) % levels, []).append(matching)
    bits = list(by_bit)
    groups = [by_bit[b] for b in bits]

    def swapped(x, bit):
        return lax.ppermute(x, "dom", [(i, i ^ 1 << bit) for i in range(lax.axis_size("dom"))])

    rep_bits = lax.axis_size("rep").bit_length() - 1
    high_bits = [1 << k for k in range(3, size.bit_length() - 1)]
    flat = {1 << (b + rep_bits): k for k, b in enumerate(bits)}
    quad_slots = [flat.get(bit) for bit in (2, 4, 6)]
    orders = (list(zip(high_bits, high_bits[::-1])), list(zip(high_bits[::-1], high_bits)))
    high_slots = [(flat.get(even), flat.get(odd)) for even, odd in orders[0]]
    slots = [(k, k) for k in quad_slots if k is not None]
    slots += [pair for pair in high_slots if pair != (None, None)]

    others = [swapped(feats, b) for b in bits]
    count = len(bits)
    tall = count * rows
    stacked = heads * rows
    gain1 = norm1_gain.reshape(1, width)
    gain2 = norm2_gain.reshape(1, width)
    upstream = out_grad[0]
    normed, hidden, counts = call(
        functools.partial(first_kernel, groups),
        (struct((rows, width), F32), struct((rows, width), BF16), struct((rows, tall), F32)),
        feats,
        gain1,
        partners,
        cost_estimate=pl.CostEstimate(flops=10**10, bytes_accessed=1, transcendentals=0),
    )
    query, key, value, raw, tangent, powers, back = call(
        own_kernel,
        (
            struct((stacked, width), BF16),
            struct((rows, width), BF16),
            struct((rows, width), BF16),
            struct((stacked, rows), F32),
            struct((stacked, rows), F32),
            struct((stacked, rows), F32),
            struct((rows, w_up.shape[1]), F32),
        ),
        hidden,
        upstream,
        w_query,
        w_key,
        w_value,
        w_down,
        local_gain,
        in_specs=[VM] * 6 + [SM],
    )
    half = width // 2
    (
        node_out,
        keep_wide,
        send_wide,
        grad_mixed,
        grad_gain2,
        normed_far,
        hidden_far,
        key_far,
        value_far,
        raw_far,
        tanh_far,
        weight_near,
        weight_far,
        attended,
    ) = call(
        functools.partial(forward_kernel, count),
        (
            struct((rows, width), BF16),
            struct((4 * half, width), BF16),
            struct((4 * half, width), BF16),
            struct((rows, width), F32),
            struct((1, width), F32),
            struct((tall, width), F32),
            struct((tall, width), BF16),
            struct((tall, width), BF16),
            struct((tall, width), BF16),
            struct((stacked, tall), F32),
            struct((stacked, tall), F32),
            struct((stacked, rows), BF16),
            struct((stacked, tall), BF16),
            struct((rows, width), F32),
        ),
        *others,
        feats,
        upstream,
        gain1,
        gain2,
        w_key,
        w_value,
        w_out,
        w_up,
        w_down,
        query,
        value,
        powers,
        counts,
        back,
        expander_gain,
        in_specs=[VM] * (count + 14) + [SM],
    )
    keep_square, send_square, own, *slot_rows = call(
        functools.partial(backward_kernel, slots, count),
        (
            struct((4 * half, width), BF16),
            struct((4 * half + SMALL, width), BF16),
            struct((rows, width), F32),
        )
        + tuple(struct((rows, width), BF16) for _ in slots),
        gain1,
        grad_gain2,
        w_query,
        w_key,
        w_value,
        w_out,
        hidden,
        normed,
        query,
        key,
        value,
        raw,
        tangent,
        grad_mixed,
        normed_far,
        hidden_far,
        key_far,
        value_far,
        raw_far,
        tanh_far,
        weight_near,
        weight_far,
        attended,
        local_gain,
        expander_gain,
        in_specs=[VM] * 23 + [SM, SM],
        scratch_shapes=[pltpu.VMEM((stacked, rows), BF16), pltpu.VMEM((stacked, tall), BF16)],
    )
    slot_rows = iter(slot_rows)
    slot_quad = [None if k is None else next(slot_rows) for k in quad_slots]
    slot_high = [None if pair == (None, None) else next(slot_rows) for pair in high_slots]

    def present(*items):
        return [x for x in items if x is not None]

    def sized(base, slot):
        return struct((base + (0 if slot is None else rows), width), BF16)

    half = width // 2
    recv_wide = flipped(send_wide, 1, 1)
    recv_square = flipped(send_square, 1, 1)
    data = 2 * half + SMALL
    own_quad, *send_quad = call(
        functools.partial(pair_kernel, [x is not None for x in slot_quad]),
        (struct((data, width), BF16),) + tuple(sized(data, x) for x in slot_quad),
        keep_wide,
        recv_wide,
        keep_square,
        send_square,
        recv_square,
        *present(*slot_quad),
    )
    recv_quad = [flipped(x, bit, bit) for x, bit in zip(send_quad, (2, 4, 6))]
    returned = [x for x, slot in zip(recv_quad, slot_quad) if slot is not None]
    starts = [data] * len(returned)
    wide, square = call(
        functools.partial(quad_kernel, slot_high[0] is not None),
        (sized(half, slot_high[0]), struct((half + SMALL, width), BF16)),
        own_quad,
        *recv_quad,
        *present(slot_high[0]),
    )
    for k in range(len(high_bits)):
        recv_wide = flipped(wide, *orders[0][k])
        recv_square = flipped(square, *orders[1][k])
        if slot_high[k] is not None:
            returned.append(recv_wide)
            starts.append(half)
        slot = slot_high[k + 1] if k + 1 < len(high_bits) else None
        wide = call(
            functools.partial(double_kernel, half, False, slot is not None),
            sized(half, slot),
            wide,
            recv_wide,
            *present(slot, square),
        )
        square = call(
            functools.partial(double_kernel, half, True, False),
            struct((half + SMALL, width), BF16),
            square,
            recv_square,
            wide,
        )
    base = call(join_kernel, struct((2 * half, width), BF16), wide, square)
    near = [base] + [flipped(base, bit, bit) for bit in (2, 4, 6)]
    over = [flipped(x, 1, 1) for x in near]
    grad_feats = call(
        functools.partial(tail_kernel, starts),
        struct((rows, width), BF16),
        feats,
        own,
        grad_mixed,
        gain1,
        *returned,
    )
    one = struct((1, width), F32)
    full = struct((width, width), F32)
    few = struct((heads,), F32)
    results = pl.pallas_call(
        spread_kernel,
        out_shape=(
            one,
            full,
            full,
            full,
            full,
            one,
            struct((width, 2 * width), F32),
            struct((2 * width, width), F32),
            few,
            few,
        ),
        in_specs=[VM] * 9,
        out_specs=(VM, ANY, ANY, ANY, ANY, VM, ANY, ANY, VM, VM),
        scratch_shapes=[
            pltpu.VMEM((8, width, width), BF16),
            pltpu.VMEM((8, width, width), F32),
            pltpu.SemaphoreType.DMA((8,)),
        ],
        compiler_params=PARAMS,
    )(*near, *over, square)
    grad_gain1, grad_wq, grad_wk, grad_wv, grad_wout, grad_gain2, grad_up, grad_down, grad_local, grad_far = results
    return (
        node_out[None],
        grad_feats[None],
        grad_gain1.reshape(width),
        grad_wq,
        grad_wk,
        grad_wv,
        grad_wout,
        grad_gain2.reshape(width),
        grad_up,
        grad_down,
        grad_local,
        grad_far,
    )


def solution(mesh):
    whole = P()
    rows = P("rep", "dom", None)
    return jax.shard_map(
        local,
        mesh=mesh,
        in_specs=(rows, rows)
        + (whole,) * 10
        + (P("rep", None, "dom", None), rows, P("rep", "dom")),
        out_specs=(rows, rows) + (whole,) * 10,
        check_vma=False,
    )
```

```python
import functools

import jax
import jax.numpy as jnp
from jax import lax
from jax.experimental import pallas as pl
from jax.experimental.pallas import tpu as pltpu
from jax.sharding import PartitionSpec as P

EPSILON = 1e-05
SCORE_CAP = 5.0
GELU_ROOT = 0.7978845608028654
GELU_CUBIC = 0.044715
SMALL = 16
AXES = ("dom", "rep")
VMEM_LIMIT = 48 * 1024 * 1024
F32 = jnp.float32
BF16 = jnp.bfloat16


def dot(a, b):
    return lax.dot_general(a, b, (((1,), (0,)), ((), ())), preferred_element_type=F32)


def dot_rhs_t(a, b):
    return lax.dot_general(a, b, (((1,), (1,)), ((), ())), preferred_element_type=F32)


def dot_lhs_t(a, b):
    return lax.dot_general(a, b, (((0,), (0,)), ((), ())), preferred_element_type=F32)


def norm_forward(matrix):
    center = jnp.mean(matrix, axis=-1, keepdims=True)
    shifted = matrix - center
    inverse = lax.rsqrt(jnp.mean(shifted * shifted, axis=-1, keepdims=True) + EPSILON)
    return (shifted * inverse, inverse)


def norm_backward(upstream, normed, inverse, gain):
    scaled_up = upstream * gain
    return inverse * (
        scaled_up
        - jnp.mean(scaled_up, axis=-1, keepdims=True)
        - normed * jnp.mean(scaled_up * normed, axis=-1, keepdims=True)
    )


def gelu_parts(preact):
    tangent = jnp.tanh(GELU_ROOT * (preact + GELU_CUBIC * preact * preact * preact))
    result = 0.5 * preact * (1.0 + tangent)
    derivative = 0.5 * (1.0 + tangent) + 0.5 * preact * (1.0 - tangent * tangent) * GELU_ROOT * (
        1.0 + 3.0 * GELU_CUBIC * preact * preact
    )
    return (result, derivative)


def split_parts(rows):
    high = rows.astype(BF16).astype(F32)
    return jnp.concatenate([high, rows - high], axis=0).astype(BF16)


def join_parts(packed):
    wide = packed.astype(F32)
    return wide[: SMALL // 2] + wide[SMALL // 2 :]


def device_bits():
    flat = lax.axis_index("dom") * lax.axis_size("rep") + lax.axis_index("rep")
    return (flat & 1, (flat >> 1) & 3)


def head_masks_of(shape, heads):
    lane = lax.broadcasted_iota(jnp.int32, shape, 1) // (shape[1] // heads)
    return [lane == h for h in range(heads)]


def stack_heads(matrix, masks):
    return jnp.concatenate([jnp.where(m, matrix, 0.0) for m in masks], axis=0).astype(BF16)


def relay(source_refs, out_refs):
    for source, out in zip(source_refs, out_refs):
        out[...] = source[...]


def flag_kernel(flag_ref):
    flag_ref[...] = jnp.zeros(flag_ref.shape, F32)


def count_kernel(groups, flag_ref, perm_ref, *refs):
    sources = refs[: len(refs) // 2]
    count_ref = refs[len(sources)]
    relay(sources, refs[len(sources) + 1 :])
    rows = perm_ref.shape[1]
    target = lax.broadcasted_iota(jnp.int32, (rows, rows), 0)
    for g, members in enumerate(groups):
        total = 0.0
        for m in members:
            total = total + jnp.where(target == perm_ref[m : m + 1, :], 1.0, 0.0)
        count_ref[:, g * rows : (g + 1) * rows] = total.T


def sort_units(units_ref, keep_ref, send_ref, bits):
    core, quad = bits
    rows = units_ref.shape[0] // 8
    for r in range(4):
        span = slice(r * rows, (r + 1) * rows)
        for owner, out_ref in ((core, keep_ref), (1 - core, send_ref)):
            start = pl.multiple_of((owner * 4 + (quad ^ r)) * rows, rows)
            out_ref[span, :] = units_ref[pl.ds(start, rows), :]


def collapse(matrix, masks):
    rows = matrix.shape[0] // len(masks)
    total = jnp.where(masks[0], matrix[:rows], 0.0)
    for h in range(1, len(masks)):
        total = total + jnp.where(masks[h], matrix[h * rows : (h + 1) * rows], 0.0)
    return total


def layer_kernel(slots, count, *refs):
    feats_refs = refs[: count + 1]
    (
        up_ref,
        gain1_ref,
        wq_ref,
        wk_ref,
        wv_ref,
        wo_ref,
        gain2_ref,
        wup_ref,
        wdown_ref,
        local_ref,
        far_ref,
        count_ref,
    ) = refs[count + 1 : count + 13]
    out_ref, keepw_ref, sendw_ref, keeps_ref, sends_ref, own_ref, mixed_ref = refs[count + 13 : count + 20]
    slot_refs = refs[count + 20 : count + 20 + len(slots)]
    raw_s, tanh_s, weight_s, dscore_s, wide_s, square_s = refs[count + 20 + len(slots) :]

    rows, width = out_ref.shape
    heads = local_ref.shape[0]
    head_dim = width // heads
    scale = 1.0 / float(head_dim) ** 0.5
    bits = device_bits()
    core = bits[0]

    gain1 = gain1_ref[...]
    gain2 = gain2_ref[...]
    upstream = up_ref[...]
    feats = jnp.concatenate([ref[...] for ref in feats_refs], axis=0).astype(F32)
    normed1, _ = norm_forward(feats)
    hidden = (normed1 * gain1).astype(BF16)
    queries = dot(hidden[:rows], wq_ref[...])
    key_all = dot(hidden, wk_ref[...]).astype(BF16)
    value_all = dot(hidden, wv_ref[...]).astype(BF16)

    head_masks = head_masks_of((rows, width), heads)
    query_stack = stack_heads(queries, head_masks)
    raw_s[...] = dot_rhs_t(query_stack, key_all) * scale

    far_counts = count_ref[...]

    for h in range(heads):
        block = pl.ds(h * rows, rows)
        tl = jnp.tanh(raw_s[block, :rows] * (local_ref[h] / SCORE_CAP))
        tf = jnp.tanh(raw_s[block, rows:] * (far_ref[h] / SCORE_CAP))
        el = jnp.exp(SCORE_CAP * tl)
        ef = jnp.exp(SCORE_CAP * tf) * far_counts
        inv = 1.0 / (jnp.sum(el, axis=1, keepdims=True) + jnp.sum(ef, axis=1, keepdims=True))
        tanh_s[block, :rows] = tl
        tanh_s[block, rows:] = tf
        weight_s[block, :rows] = (el * inv).astype(BF16)
        weight_s[block, rows:] = (ef * inv).astype(BF16)

    attended32 = collapse(dot(weight_s[...], value_all), head_masks)
    attended = attended32.astype(BF16)
    mixed = (feats[:rows] + dot(attended, wo_ref[...])).astype(BF16)
    normed2, inverse2 = norm_forward(mixed.astype(F32))
    hidden2 = (normed2 * gain2).astype(BF16)
    preact = dot(hidden2, wup_ref[...])
    act32, derivative = gelu_parts(preact)
    act = act32.astype(BF16)
    out_ref[...] = (mixed.astype(F32) + dot(act, wdown_ref[...])).astype(BF16)
    grad_down = dot_lhs_t(act, upstream)
    wide_s[2 * width : 3 * width, :] = grad_down[:width].astype(BF16)
    wide_s[3 * width : 4 * width, :] = grad_down[width:].astype(BF16)
    grad_pre = (dot_rhs_t(upstream, wdown_ref[...]) * derivative).astype(BF16)
    grad_up = dot_lhs_t(hidden2, grad_pre)
    wide_s[0 * width : 1 * width, :] = grad_up[:, :width].astype(BF16)
    wide_s[1 * width : 2 * width, :] = grad_up[:, width:].astype(BF16)
    grad_hidden2 = dot_rhs_t(grad_pre, wup_ref[...])
    grad_gain2 = jnp.sum(grad_hidden2 * normed2, axis=0, keepdims=True)
    grad_mixed = upstream.astype(F32) + norm_backward(grad_hidden2, normed2, inverse2, gain2)
    mixed_ref[...] = grad_mixed
    grad_mixed16 = grad_mixed.astype(BF16)
    square_s[3 * width : 4 * width, :] = dot_lhs_t(attended, grad_mixed16).astype(BF16)
    grad_att = dot_rhs_t(grad_mixed16, wo_ref[...]).astype(BF16).astype(F32)
    grad_stack = stack_heads(grad_att, head_masks)
    product = grad_att * attended32
    dots = dot_rhs_t(grad_stack, value_all)

    local_terms = []
    far_terms = []
    for h in range(heads):
        block = pl.ds(h * rows, rows)
        delta = jnp.sum(jnp.where(head_masks[h], product, 0.0), axis=1, keepdims=True)
        tangent = tanh_s[block, :]
        slope = 1.0 - tangent * tangent
        dlogit = weight_s[block, :].astype(F32) * (dots[h * rows : (h + 1) * rows] - delta)
        sloped = dlogit * slope
        terms = jnp.sum(sloped * raw_s[block, :], axis=0, keepdims=True)
        local_terms.append(jnp.sum(terms[:, :rows], axis=1, keepdims=True))
        far_terms.append(jnp.sum(terms[:, rows:], axis=1, keepdims=True))
        dscore_s[block, :rows] = (sloped[:, :rows] * (local_ref[h] * scale)).astype(BF16)
        dscore_s[block, rows:] = (sloped[:, rows:] * (far_ref[h] * scale)).astype(BF16)

    grad_query = collapse(dot(dscore_s[...], key_all), head_masks).astype(BF16)
    grad_key = dot_lhs_t(dscore_s[...], query_stack).astype(BF16)
    grad_value = dot_lhs_t(weight_s[...], grad_stack).astype(BF16)
    square_s[0 * width : 1 * width, :] = dot_lhs_t(hidden[:rows], grad_query).astype(BF16)
    square_s[1 * width : 2 * width, :] = dot_lhs_t(hidden, grad_key).astype(BF16)
    square_s[2 * width : 3 * width, :] = dot_lhs_t(hidden, grad_value).astype(BF16)
    grad_hidden = dot_rhs_t(grad_key, wk_ref[...]) + dot_rhs_t(grad_value, wv_ref[...])
    own = grad_hidden[:rows] + dot_rhs_t(grad_query, wq_ref[...])
    own_ref[...] = own
    grad_gain1 = jnp.sum(own * normed1[:rows], axis=0, keepdims=True)
    grad_gain1 = grad_gain1 + jnp.sum(grad_hidden[rows:] * normed1[rows:], axis=0, keepdims=True)
    back = [grad_hidden[(k + 1) * rows : (k + 2) * rows] for k in range(count)]
    for (even, odd), ref in zip(slots, slot_refs):
        ref[...] = jnp.where(
            core == 1, 0.0 if odd is None else back[odd], 0.0 if even is None else back[even]
        ).astype(BF16)

    column = lax.broadcasted_iota(jnp.int32, (1, width), 1)
    gains = jnp.zeros((1, width), F32)
    for h in range(heads):
        gains = jnp.where(column == h, local_terms[h], gains)
        gains = jnp.where(column == heads + h, far_terms[h], gains)
    line = lax.broadcasted_iota(jnp.int32, (SMALL // 2, width), 0)
    small = jnp.where(line == 0, grad_gain1, jnp.where(line == 1, grad_gain2, jnp.where(line == 2, gains, 0.0)))
    sends_ref[keeps_ref.shape[0] :, :] = split_parts(small)
    sort_units(wide_s, keepw_ref, sendw_ref, bits)
    sort_units(square_s, keeps_ref, sends_ref, bits)


def pair_kernel(slots, keepw_ref, recvw_ref, keeps_ref, sents_ref, recvs_ref, *refs):
    slot_refs = refs[: sum(slots)]
    out_refs = refs[sum(slots) :]
    rows = keepw_ref.shape[0] // 4
    wide = (keepw_ref[...].astype(F32) + recvw_ref[...].astype(F32)).astype(BF16)
    square = (keeps_ref[...].astype(F32) + recvs_ref[: 4 * rows, :].astype(F32)).astype(BF16)
    packed = split_parts(join_parts(sents_ref[4 * rows :, :]) + join_parts(recvs_ref[4 * rows :, :]))
    used = 0
    for r in range(4):
        span = slice(r * rows, (r + 1) * rows)
        out_refs[r][:rows, :] = wide[span]
        out_refs[r][rows : 2 * rows, :] = square[span]
        out_refs[r][2 * rows : 2 * rows + SMALL, :] = packed
        if r and slots[r - 1]:
            out_refs[r][2 * rows + SMALL :, :] = slot_refs[used][...]
            used += 1


def quad_kernel(has_slot, own_ref, one_ref, two_ref, three_ref, *refs):
    wide_ref, square_ref = refs[-2:]
    total_rows = own_ref.shape[0]
    rows = (total_rows - SMALL) // 2
    data = [ref[: 2 * rows, :].astype(F32) for ref in (own_ref, one_ref, two_ref, three_ref)]
    small = [join_parts(ref[2 * rows : total_rows, :]) for ref in (own_ref, one_ref, two_ref, three_ref)]
    total = ((data[0] + data[1]) + (data[2] + data[3])).astype(BF16)
    wide_ref[:rows, :] = total[:rows]
    square_ref[:rows, :] = total[rows:]
    square_ref[rows:, :] = split_parts((small[0] + small[1]) + (small[2] + small[3]))
    if has_slot:
        wide_ref[rows:, :] = refs[0][...]


def double_kernel(rows, small, has_slot, own_ref, recv_ref, *refs):
    out_ref = refs[-1]
    total = own_ref[:rows, :].astype(F32) + recv_ref[:rows, :].astype(F32)
    out_ref[:rows, :] = total.astype(BF16)
    if small:
        span = slice(rows, rows + SMALL)
        out_ref[span, :] = split_parts(join_parts(own_ref[span, :]) + join_parts(recv_ref[span, :]))
    if has_slot:
        out_ref[rows:, :] = refs[0][...]


def join_kernel(wide_ref, square_ref, out_ref):
    rows = out_ref.shape[0] // 2
    out_ref[:rows, :] = wide_ref[:rows, :]
    out_ref[rows:, :] = square_ref[:rows, :]


def tail_kernel(start, *refs):
    count = len(start)
    feats_ref, rows_ref, own_ref, mixed_ref, gain_ref, small_ref = refs[:6]
    out_ref, grad_ref, gain1_ref, gain2_ref, local_ref, far_ref, flag_ref = refs[6 + count :]
    out_ref[...] = rows_ref[...]
    normed, inverse = norm_forward(feats_ref[...].astype(F32))
    grad_hidden = own_ref[...]
    for ref, first in zip(refs[6 : 6 + count], start):
        grad_hidden = grad_hidden + ref[first:, :].astype(F32)
    grad = mixed_ref[...] + norm_backward(grad_hidden, normed, inverse, gain_ref[...])
    grad_ref[...] = grad.astype(BF16)
    heads = local_ref.shape[0]
    small = join_parts(small_ref[small_ref.shape[0] - SMALL :, :])
    gain1_ref[...] = small[0:1]
    gain2_ref[...] = small[1:2]
    local_ref[...] = small[2, :heads]
    far_ref[...] = small[2, heads : 2 * heads]
    flag_ref[...] = jnp.zeros(flag_ref.shape, F32)


def after_kernel(source_ref, flag_ref, out_ref):
    out_ref[...] = source_ref[...]


def spread_kernel(*refs):
    piece_refs = refs[:8]
    wq_ref, wk_ref, wv_ref, wo_ref, up_ref, down_ref, pieces, chunks, sems = refs[8:]
    width = wq_ref.shape[0]
    half = width // 2
    core, quad = device_bits()
    relay(piece_refs, [pieces.at[k] for k in range(8)])
    targets = [
        up_ref.at[:, :width],
        up_ref.at[:, width:],
        down_ref.at[:width, :],
        down_ref.at[width:, :],
        wq_ref,
        wk_ref,
        wv_ref,
        wo_ref,
    ]
    copies = []
    for chunk, target in enumerate(targets):
        first = 0 if chunk < 4 else half
        for part in range(2):
            unit = 2 * (chunk % 4) + part
            rel = (core ^ (unit >> 2)) * 4 + (quad ^ (unit & 3))
            value = pieces[rel, first : first + half, :]
            chunks[chunk, part * half : (part + 1) * half, :] = value.astype(F32)
        copy = pltpu.make_async_copy(chunks.at[chunk], target, sems.at[chunk])
        copy.start()
        copies.append(copy)
    for copy in copies:
        copy.wait()


def struct(shape, dtype):
    return jax.ShapeDtypeStruct(shape, dtype)


VM = pl.BlockSpec(memory_space=pltpu.VMEM)
SM = pl.BlockSpec(memory_space=pltpu.SMEM)
ANY = pl.BlockSpec(memory_space=pl.ANY)
PARAMS = pltpu.CompilerParams(vmem_limit_bytes=VMEM_LIMIT)


def call(kernel, outs, *args, in_specs=None, **kwargs):
    return pl.pallas_call(
        kernel,
        out_shape=outs,
        in_specs=in_specs or [VM] * len(args),
        out_specs=jax.tree.map(lambda _: VM, outs),
        compiler_params=PARAMS,
        **kwargs,
    )(*args)


def flipped(x, bits_even, bits_odd):
    size = lax.axis_size("dom") * lax.axis_size("rep")
    pairs = [(i, i ^ (bits_odd if i & 1 else bits_even)) for i in range(size)]
    return lax.ppermute(x, AXES, pairs)


def local(
    node_feats,
    out_grad,
    norm1_gain,
    w_query,
    w_key,
    w_value,
    w_out,
    norm2_gain,
    w_up,
    w_down,
    local_gain,
    expander_gain,
    partner_perm,
    block_pairs,
    pair_count,
):
    feats = node_feats[0]
    partners = partner_perm[0, :, 0, :]
    rows, width = feats.shape
    heads = local_gain.shape[0]
    size = lax.axis_size("dom") * lax.axis_size("rep")
    levels = lax.axis_size("dom").bit_length() - 1
    by_bit = {}
    for matching in range(partners.shape[0]):
        by_bit.setdefault((levels - 1 - matching) % levels, []).append(matching)
    bits = sorted(by_bit)
    groups = [by_bit[b] for b in bits]

    def swapped(x, bit):
        return lax.ppermute(x, "dom", [(i, i ^ 1 << bit) for i in range(lax.axis_size("dom"))])

    rep_bits = lax.axis_size("rep").bit_length() - 1
    high_bits = [1 << k for k in range(3, size.bit_length() - 1)]
    flat = {1 << (b + rep_bits): k for k, b in enumerate(bits)}
    quad_slots = [flat.get(bit) for bit in (2, 4, 6)]
    orders = (list(zip(high_bits, high_bits[::-1])), list(zip(high_bits[::-1], high_bits)))
    high_slots = [(flat.get(even), flat.get(odd)) for even, odd in orders[0]]
    slots = [(k, k) for k in quad_slots if k is not None]
    slots += [pair for pair in high_slots if pair != (None, None)]

    others = [swapped(feats, b) for b in bits]
    count = len(bits)
    tall = count * rows
    stacked = heads * rows
    gain1 = norm1_gain.reshape(1, width)
    gain2 = norm2_gain.reshape(1, width)
    upstream = out_grad[0]
    flag = struct((8, 128), F32)
    begun = call(
        flag_kernel, flag, cost_estimate=pl.CostEstimate(flops=10**10, bytes_accessed=1, transcendentals=0)
    )
    passed = (feats, upstream, gain1, gain2)
    counts, feats_near, up_near, gain1_near, gain2_near = call(
        functools.partial(count_kernel, groups),
        (struct((rows, tall), F32),) + tuple(struct(x.shape, x.dtype) for x in passed),
        begun,
        partners,
        *passed,
        cost_estimate=pl.CostEstimate(flops=10**10, bytes_accessed=1, transcendentals=0),
    )
    out_rows, keep_wide, send_wide, keep_square, send_square, own, grad_mixed, *slot_rows = call(
        functools.partial(layer_kernel, slots, count),
        (
            struct((rows, width), BF16),
            struct((2 * width, width), BF16),
            struct((2 * width, width), BF16),
            struct((2 * width, width), BF16),
            struct((2 * width + SMALL, width), BF16),
            struct((rows, width), F32),
            struct((rows, width), F32),
        )
        + tuple(struct((rows, width), BF16) for _ in slots),
        feats_near,
        *others,
        up_near,
        gain1_near,
        w_query,
        w_key,
        w_value,
        w_out,
        gain2_near,
        w_up,
        w_down,
        local_gain,
        expander_gain,
        counts,
        in_specs=[VM] * (count + 10) + [SM, SM, VM],
        scratch_shapes=[
            pltpu.VMEM((stacked, tall + rows), F32),
            pltpu.VMEM((stacked, tall + rows), F32),
            pltpu.VMEM((stacked, tall + rows), BF16),
            pltpu.VMEM((stacked, tall + rows), BF16),
            pltpu.VMEM((4 * width, width), BF16),
            pltpu.VMEM((4 * width, width), BF16),
        ],
    )
    slot_rows = iter(slot_rows)
    slot_quad = [None if k is None else next(slot_rows) for k in quad_slots]
    slot_high = [None if pair == (None, None) else next(slot_rows) for pair in high_slots]

    def present(*items):
        return [x for x in items if x is not None]

    def sized(base, slot):
        return struct((base + (0 if slot is None else rows), width), BF16)

    half = width // 2
    recv_wide = flipped(send_wide, 1, 1)
    recv_square = flipped(send_square, 1, 1)
    data = 2 * half + SMALL
    own_quad, *send_quad = call(
        functools.partial(pair_kernel, [x is not None for x in slot_quad]),
        (struct((data, width), BF16),) + tuple(sized(data, x) for x in slot_quad),
        keep_wide,
        recv_wide,
        keep_square,
        send_square,
        recv_square,
        *present(*slot_quad),
    )
    recv_quad = [flipped(x, bit, bit) for x, bit in zip(send_quad, (2, 4, 6))]
    returned = [x for x, slot in zip(recv_quad, slot_quad) if slot is not None]
    starts = [data] * len(returned)
    wide, square = call(
        functools.partial(quad_kernel, slot_high[0] is not None),
        (sized(half, slot_high[0]), struct((half + SMALL, width), BF16)),
        own_quad,
        *recv_quad,
        *present(slot_high[0]),
    )
    for k in range(len(high_bits)):
        recv_wide = flipped(wide, *orders[0][k])
        recv_square = flipped(square, *orders[1][k])
        if slot_high[k] is not None:
            returned.append(recv_wide)
            starts.append(half)
        slot = slot_high[k + 1] if k + 1 < len(high_bits) else None
        extra = present(slot)
        wide = call(
            functools.partial(double_kernel, half, False, slot is not None),
            sized(half, slot),
            wide,
            recv_wide,
            *extra,
            square,
        )
        square = call(
            functools.partial(double_kernel, half, True, False),
            struct((half + SMALL, width), BF16),
            square,
            recv_square,
            wide,
        )
    base = call(join_kernel, struct((2 * half, width), BF16), wide, square)
    near = [base] + [flipped(base, bit, bit) for bit in (2, 4, 6)]
    over = [flipped(x, 1, 1) for x in near]
    block = struct((rows, width), BF16)
    one = struct((1, width), F32)
    full = struct((width, width), F32)
    few = struct((heads,), F32)
    node_out, grad_feats, grad_gain1, grad_gain2, grad_local, grad_far, ended = call(
        functools.partial(tail_kernel, starts),
        (block, block, one, one, few, few, flag),
        feats_near,
        out_rows,
        own,
        grad_mixed,
        gain1_near,
        square,
        *returned,
    )
    base = call(join_kernel, struct((2 * half, width), BF16), wide, square)
    near = [base] + [flipped(base, bit, bit) for bit in (2, 4, 6)]
    near[3] = call(after_kernel, struct(base.shape, BF16), near[3], ended)
    over = [flipped(x, 1, 1) for x in near]
    grad_wq, grad_wk, grad_wv, grad_wout, grad_up, grad_down = pl.pallas_call(
        spread_kernel,
        out_shape=(full,) * 4 + (struct((width, 2 * width), F32), struct((2 * width, width), F32)),
        in_specs=[VM] * 8,
        out_specs=(ANY,) * 6,
        scratch_shapes=[
            pltpu.VMEM((8, width, width), BF16),
            pltpu.VMEM((8, width, width), F32),
            pltpu.SemaphoreType.DMA((8,)),
        ],
        compiler_params=PARAMS,
    )(*near, *over)
    return (
        node_out[None],
        grad_feats[None],
        grad_gain1.reshape(width),
        grad_wq,
        grad_wk,
        grad_wv,
        grad_wout,
        grad_gain2.reshape(width),
        grad_up,
        grad_down,
        grad_local,
        grad_far,
    )


def solution(mesh):
    whole = P()
    rows = P("rep", "dom", None)
    return jax.shard_map(
        local,
        mesh=mesh,
        in_specs=(rows, rows)
        + (whole,) * 10
        + (P("rep", None, "dom", None), rows, P("rep", "dom")),
        out_specs=(rows, rows) + (whole,) * 10,
        check_vma=False,
    )
```

```python
import functools

import jax
import jax.numpy as jnp
from jax import lax
from jax.experimental import pallas as pl
from jax.experimental.pallas import tpu as pltpu
from jax.sharding import PartitionSpec as P

EPSILON = 1e-05
SCORE_CAP = 5.0
GELU_ROOT = 0.7978845608028654
GELU_CUBIC = 0.044715
SMALL = 16
AXES = ("dom", "rep")
VMEM_LIMIT = 48 * 1024 * 1024
F32 = jnp.float32
BF16 = jnp.bfloat16


def dot(a, b):
    return lax.dot_general(a, b, (((1,), (0,)), ((), ())), preferred_element_type=F32)


def dot_rhs_t(a, b):
    return lax.dot_general(a, b, (((1,), (1,)), ((), ())), preferred_element_type=F32)


def dot_lhs_t(a, b):
    return lax.dot_general(a, b, (((0,), (0,)), ((), ())), preferred_element_type=F32)


def norm_forward(matrix):
    center = jnp.mean(matrix, axis=-1, keepdims=True)
    shifted = matrix - center
    inverse = lax.rsqrt(jnp.mean(shifted * shifted, axis=-1, keepdims=True) + EPSILON)
    return (shifted * inverse, inverse)


def norm_backward(upstream, normed, inverse, gain):
    scaled_up = upstream * gain
    return inverse * (
        scaled_up
        - jnp.mean(scaled_up, axis=-1, keepdims=True)
        - normed * jnp.mean(scaled_up * normed, axis=-1, keepdims=True)
    )


def gelu_parts(preact):
    tangent = jnp.tanh(GELU_ROOT * (preact + GELU_CUBIC * preact * preact * preact))
    result = 0.5 * preact * (1.0 + tangent)
    derivative = 0.5 * (1.0 + tangent) + 0.5 * preact * (1.0 - tangent * tangent) * GELU_ROOT * (
        1.0 + 3.0 * GELU_CUBIC * preact * preact
    )
    return (result, derivative)


def split_parts(rows):
    high = rows.astype(BF16).astype(F32)
    return jnp.concatenate([high, rows - high], axis=0).astype(BF16)


def join_parts(packed):
    wide = packed.astype(F32)
    return wide[: SMALL // 2] + wide[SMALL // 2 :]


def device_bits():
    flat = lax.axis_index("dom") * lax.axis_size("rep") + lax.axis_index("rep")
    return (flat & 1, (flat >> 1) & 3)


def head_masks_of(shape, heads):
    lane = lax.broadcasted_iota(jnp.int32, shape, 1) // (shape[1] // heads)
    return [lane == h for h in range(heads)]


def stack_heads(matrix, masks):
    return jnp.concatenate([jnp.where(m, matrix, 0.0) for m in masks], axis=0).astype(BF16)


def relay(source_refs, out_refs):
    for source, out in zip(source_refs, out_refs):
        out[...] = source[...]


def flag_kernel(flag_ref):
    flag_ref[...] = jnp.zeros(flag_ref.shape, F32)


def count_kernel(groups, flag_ref, perm_ref, local_ref, far_ref, *refs):
    sources = refs[: len(refs) // 2 - 1]
    count_ref, scale_ref = refs[len(sources) : len(sources) + 2]
    relay(sources, refs[len(sources) + 2 :])
    rows = perm_ref.shape[1]
    target = lax.broadcasted_iota(jnp.int32, (rows, rows), 0)
    count_ref[:, :rows] = jnp.ones((rows, rows), F32)
    for g, members in enumerate(groups):
        total = 0.0
        for m in members:
            total = total + jnp.where(target == perm_ref[m : m + 1, :], 1.0, 0.0)
        count_ref[:, (g + 1) * rows : (g + 2) * rows] = total.T
    near = lax.broadcasted_iota(jnp.int32, (1, scale_ref.shape[1]), 1) < rows
    for h in range(local_ref.shape[0]):
        scale_ref[h : h + 1, :] = jnp.where(near, local_ref[h], far_ref[h])


def sort_units(units_ref, keep_ref, send_ref, bits):
    core, quad = bits
    rows = units_ref.shape[0] // 8
    for r in range(4):
        span = slice(r * rows, (r + 1) * rows)
        for owner, out_ref in ((core, keep_ref), (1 - core, send_ref)):
            start = pl.multiple_of((owner * 4 + (quad ^ r)) * rows, rows)
            out_ref[span, :] = units_ref[pl.ds(start, rows), :]


def collapse(matrix, masks):
    rows = matrix.shape[0] // len(masks)
    total = jnp.where(masks[0], matrix[:rows], 0.0)
    for h in range(1, len(masks)):
        total = total + jnp.where(masks[h], matrix[h * rows : (h + 1) * rows], 0.0)
    return total


def layer_kernel(slots, count, *refs):
    feats_refs = refs[: count + 1]
    (
        up_ref,
        gain1_ref,
        wq_ref,
        wk_ref,
        wv_ref,
        wo_ref,
        gain2_ref,
        wup_ref,
        wdown_ref,
        scale_ref,
        count_ref,
    ) = refs[count + 1 : count + 12]
    out_ref, keepw_ref, sendw_ref, keeps_ref, sends_ref, own_ref, mixed_ref = refs[count + 12 : count + 19]
    slot_refs = refs[count + 19 : count + 19 + len(slots)]
    raw_s, tanh_s, weight_s, dscore_s, wide_s, square_s = refs[count + 19 + len(slots) :]

    rows, width = out_ref.shape
    heads = raw_s.shape[0] // rows
    head_dim = width // heads
    scale = 1.0 / float(head_dim) ** 0.5
    bits = device_bits()
    core = bits[0]

    gain1 = gain1_ref[...]
    gain2 = gain2_ref[...]
    upstream = up_ref[...]
    feats = jnp.concatenate([ref[...] for ref in feats_refs], axis=0).astype(F32)
    normed1, _ = norm_forward(feats)
    hidden = (normed1 * gain1).astype(BF16)
    queries = dot(hidden[:rows], wq_ref[...])
    key_all = dot(hidden, wk_ref[...]).astype(BF16)
    value_all = dot(hidden, wv_ref[...]).astype(BF16)

    head_masks = head_masks_of((rows, width), heads)
    query_stack = stack_heads(queries, head_masks)
    raw_s[...] = dot_rhs_t(query_stack, key_all) * scale

    counts = count_ref[...]
    for h in range(heads):
        block = pl.ds(h * rows, rows)
        tangent = jnp.tanh(raw_s[block, :] * (scale_ref[h : h + 1, :] * (1.0 / SCORE_CAP)))
        tanh_s[block, :] = tangent
        powers = jnp.exp(SCORE_CAP * tangent) * counts
        weight_s[block, :] = (powers * (1.0 / jnp.sum(powers, axis=1, keepdims=True))).astype(BF16)

    attended32 = collapse(dot(weight_s[...], value_all), head_masks)
    attended = attended32.astype(BF16)
    mixed = (feats[:rows] + dot(attended, wo_ref[...])).astype(BF16)
    normed2, inverse2 = norm_forward(mixed.astype(F32))
    hidden2 = (normed2 * gain2).astype(BF16)
    preact = dot(hidden2, wup_ref[...])
    act32, derivative = gelu_parts(preact)
    act = act32.astype(BF16)
    out_ref[...] = (mixed.astype(F32) + dot(act, wdown_ref[...])).astype(BF16)
    grad_down = dot_lhs_t(act, upstream)
    wide_s[2 * width : 3 * width, :] = grad_down[:width].astype(BF16)
    wide_s[3 * width : 4 * width, :] = grad_down[width:].astype(BF16)
    grad_pre = (dot_rhs_t(upstream, wdown_ref[...]) * derivative).astype(BF16)
    grad_up = dot_lhs_t(hidden2, grad_pre)
    wide_s[0 * width : 1 * width, :] = grad_up[:, :width].astype(BF16)
    wide_s[1 * width : 2 * width, :] = grad_up[:, width:].astype(BF16)
    grad_hidden2 = dot_rhs_t(grad_pre, wup_ref[...])
    grad_gain2 = jnp.sum(grad_hidden2 * normed2, axis=0, keepdims=True)
    grad_mixed = upstream.astype(F32) + norm_backward(grad_hidden2, normed2, inverse2, gain2)
    mixed_ref[...] = grad_mixed
    grad_mixed16 = grad_mixed.astype(BF16)
    square_s[3 * width : 4 * width, :] = dot_lhs_t(attended, grad_mixed16).astype(BF16)
    grad_att = dot_rhs_t(grad_mixed16, wo_ref[...]).astype(BF16).astype(F32)
    grad_stack = stack_heads(grad_att, head_masks)
    product = grad_att * attended32
    dots = dot_rhs_t(grad_stack, value_all)

    local_terms = []
    far_terms = []
    for h in range(heads):
        block = pl.ds(h * rows, rows)
        delta = jnp.sum(jnp.where(head_masks[h], product, 0.0), axis=1, keepdims=True)
        tangent = tanh_s[block, :]
        slope = 1.0 - tangent * tangent
        dlogit = weight_s[block, :].astype(F32) * (dots[h * rows : (h + 1) * rows] - delta)
        sloped = dlogit * slope
        terms = jnp.sum(sloped * raw_s[block, :], axis=0, keepdims=True)
        local_terms.append(jnp.sum(terms[:, :rows], axis=1, keepdims=True))
        far_terms.append(jnp.sum(terms[:, rows:], axis=1, keepdims=True))
        dscore_s[block, :] = (sloped * (scale_ref[h : h + 1, :] * scale)).astype(BF16)

    grad_query = collapse(dot(dscore_s[...], key_all), head_masks).astype(BF16)
    grad_key = dot_lhs_t(dscore_s[...], query_stack).astype(BF16)
    grad_value = dot_lhs_t(weight_s[...], grad_stack).astype(BF16)
    square_s[0 * width : 1 * width, :] = dot_lhs_t(hidden[:rows], grad_query).astype(BF16)
    square_s[1 * width : 2 * width, :] = dot_lhs_t(hidden, grad_key).astype(BF16)
    square_s[2 * width : 3 * width, :] = dot_lhs_t(hidden, grad_value).astype(BF16)
    grad_hidden = dot_rhs_t(grad_key, wk_ref[...]) + dot_rhs_t(grad_value, wv_ref[...])
    own = grad_hidden[:rows] + dot_rhs_t(grad_query, wq_ref[...])
    own_ref[...] = own
    grad_gain1 = jnp.sum(own * normed1[:rows], axis=0, keepdims=True)
    grad_gain1 = grad_gain1 + jnp.sum(grad_hidden[rows:] * normed1[rows:], axis=0, keepdims=True)
    back = [grad_hidden[(k + 1) * rows : (k + 2) * rows] for k in range(count)]
    for (even, odd), ref in zip(slots, slot_refs):
        ref[...] = jnp.where(
            core == 1, 0.0 if odd is None else back[odd], 0.0 if even is None else back[even]
        ).astype(BF16)

    column = lax.broadcasted_iota(jnp.int32, (1, width), 1)
    gains = jnp.zeros((1, width), F32)
    for h in range(heads):
        gains = jnp.where(column == h, local_terms[h], gains)
        gains = jnp.where(column == heads + h, far_terms[h], gains)
    line = lax.broadcasted_iota(jnp.int32, (SMALL // 2, width), 0)
    small = jnp.where(line == 0, grad_gain1, jnp.where(line == 1, grad_gain2, jnp.where(line == 2, gains, 0.0)))
    sends_ref[keeps_ref.shape[0] :, :] = split_parts(small)
    sort_units(wide_s, keepw_ref, sendw_ref, bits)
    sort_units(square_s, keeps_ref, sends_ref, bits)


def pair_kernel(slots, keepw_ref, recvw_ref, keeps_ref, sents_ref, recvs_ref, *refs):
    slot_refs = refs[: sum(slots)]
    out_refs = refs[sum(slots) :]
    rows = keepw_ref.shape[0] // 4
    wide = (keepw_ref[...].astype(F32) + recvw_ref[...].astype(F32)).astype(BF16)
    square = (keeps_ref[...].astype(F32) + recvs_ref[: 4 * rows, :].astype(F32)).astype(BF16)
    packed = split_parts(join_parts(sents_ref[4 * rows :, :]) + join_parts(recvs_ref[4 * rows :, :]))
    used = 0
    for r in range(4):
        span = slice(r * rows, (r + 1) * rows)
        out_refs[r][:rows, :] = wide[span]
        out_refs[r][rows : 2 * rows, :] = square[span]
        out_refs[r][2 * rows : 2 * rows + SMALL, :] = packed
        if r and slots[r - 1]:
            out_refs[r][2 * rows + SMALL :, :] = slot_refs[used][...]
            used += 1


def quad_kernel(has_slot, own_ref, one_ref, two_ref, three_ref, *refs):
    wide_ref, square_ref = refs[-2:]
    total_rows = own_ref.shape[0]
    rows = (total_rows - SMALL) // 2
    data = [ref[: 2 * rows, :].astype(F32) for ref in (own_ref, one_ref, two_ref, three_ref)]
    small = [join_parts(ref[2 * rows : total_rows, :]) for ref in (own_ref, one_ref, two_ref, three_ref)]
    total = ((data[0] + data[1]) + (data[2] + data[3])).astype(BF16)
    wide_ref[:rows, :] = total[:rows]
    square_ref[:rows, :] = total[rows:]
    square_ref[rows:, :] = split_parts((small[0] + small[1]) + (small[2] + small[3]))
    if has_slot:
        wide_ref[rows:, :] = refs[0][...]


def double_kernel(rows, small, has_slot, own_ref, recv_ref, *refs):
    out_ref = refs[-1]
    total = own_ref[:rows, :].astype(F32) + recv_ref[:rows, :].astype(F32)
    out_ref[:rows, :] = total.astype(BF16)
    if small:
        span = slice(rows, rows + SMALL)
        out_ref[span, :] = split_parts(join_parts(own_ref[span, :]) + join_parts(recv_ref[span, :]))
    if has_slot:
        out_ref[rows:, :] = refs[0][...]


def join_kernel(wide_ref, square_ref, out_ref):
    rows = out_ref.shape[0] // 2
    out_ref[:rows, :] = wide_ref[:rows, :]
    out_ref[rows:, :] = square_ref[:rows, :]


def tail_kernel(start, *refs):
    count = len(start)
    feats_ref, rows_ref, own_ref, mixed_ref, gain_ref, small_ref = refs[:6]
    out_ref, grad_ref, gain1_ref, gain2_ref, local_ref, far_ref, flag_ref = refs[6 + count :]
    out_ref[...] = rows_ref[...]
    normed, inverse = norm_forward(feats_ref[...].astype(F32))
    grad_hidden = own_ref[...]
    for ref, first in zip(refs[6 : 6 + count], start):
        grad_hidden = grad_hidden + ref[first:, :].astype(F32)
    grad = mixed_ref[...] + norm_backward(grad_hidden, normed, inverse, gain_ref[...])
    grad_ref[...] = grad.astype(BF16)
    heads = local_ref.shape[0]
    small = join_parts(small_ref[small_ref.shape[0] - SMALL :, :])
    gain1_ref[...] = small[0:1]
    gain2_ref[...] = small[1:2]
    local_ref[...] = small[2, :heads]
    far_ref[...] = small[2, heads : 2 * heads]
    flag_ref[...] = jnp.zeros(flag_ref.shape, F32)


def after_kernel(source_ref, flag_ref, out_ref):
    out_ref[...] = source_ref[...]


def spread_kernel(*refs):
    piece_refs = refs[:8]
    wq_ref, wk_ref, wv_ref, wo_ref, up_ref, down_ref, pieces, chunks, sems = refs[8:]
    width = wq_ref.shape[0]
    half = width // 2
    core, quad = device_bits()
    relay(piece_refs, [pieces.at[k] for k in range(8)])
    targets = [
        up_ref.at[:, :width],
        up_ref.at[:, width:],
        down_ref.at[:width, :],
        down_ref.at[width:, :],
        wq_ref,
        wk_ref,
        wv_ref,
        wo_ref,
    ]
    copies = []
    for chunk, target in enumerate(targets):
        first = 0 if chunk < 4 else half
        for part in range(2):
            unit = 2 * (chunk % 4) + part
            rel = (core ^ (unit >> 2)) * 4 + (quad ^ (unit & 3))
            value = pieces[rel, first : first + half, :]
            chunks[chunk, part * half : (part + 1) * half, :] = value.astype(F32)
        copy = pltpu.make_async_copy(chunks.at[chunk], target, sems.at[chunk])
        copy.start()
        copies.append(copy)
    for copy in copies:
        copy.wait()


def struct(shape, dtype):
    return jax.ShapeDtypeStruct(shape, dtype)


VM = pl.BlockSpec(memory_space=pltpu.VMEM)
SM = pl.BlockSpec(memory_space=pltpu.SMEM)
ANY = pl.BlockSpec(memory_space=pl.ANY)
PARAMS = pltpu.CompilerParams(vmem_limit_bytes=VMEM_LIMIT)


def call(kernel, outs, *args, in_specs=None, **kwargs):
    return pl.pallas_call(
        kernel,
        out_shape=outs,
        in_specs=in_specs or [VM] * len(args),
        out_specs=jax.tree.map(lambda _: VM, outs),
        compiler_params=PARAMS,
        **kwargs,
    )(*args)


def flipped(x, bits_even, bits_odd):
    size = lax.axis_size("dom") * lax.axis_size("rep")
    pairs = [(i, i ^ (bits_odd if i & 1 else bits_even)) for i in range(size)]
    return lax.ppermute(x, AXES, pairs)


def local(
    node_feats,
    out_grad,
    norm1_gain,
    w_query,
    w_key,
    w_value,
    w_out,
    norm2_gain,
    w_up,
    w_down,
    local_gain,
    expander_gain,
    partner_perm,
    block_pairs,
    pair_count,
):
    feats = node_feats[0]
    partners = partner_perm[0, :, 0, :]
    rows, width = feats.shape
    heads = local_gain.shape[0]
    size = lax.axis_size("dom") * lax.axis_size("rep")
    levels = lax.axis_size("dom").bit_length() - 1
    by_bit = {}
    for matching in range(partners.shape[0]):
        by_bit.setdefault((levels - 1 - matching) % levels, []).append(matching)
    bits = sorted(by_bit)
    groups = [by_bit[b] for b in bits]

    def swapped(x, bit):
        return lax.ppermute(x, "dom", [(i, i ^ 1 << bit) for i in range(lax.axis_size("dom"))])

    rep_bits = lax.axis_size("rep").bit_length() - 1
    high_bits = [1 << k for k in range(3, size.bit_length() - 1)]
    flat = {1 << (b + rep_bits): k for k, b in enumerate(bits)}
    quad_slots = [flat.get(bit) for bit in (2, 4, 6)]
    orders = (list(zip(high_bits, high_bits[::-1])), list(zip(high_bits[::-1], high_bits)))
    high_slots = [(flat.get(even), flat.get(odd)) for even, odd in orders[0]]
    slots = [(k, k) for k in quad_slots if k is not None]
    slots += [pair for pair in high_slots if pair != (None, None)]

    others = [swapped(feats, b) for b in bits]
    count = len(bits)
    tall = count * rows
    stacked = heads * rows
    gain1 = norm1_gain.reshape(1, width)
    gain2 = norm2_gain.reshape(1, width)
    upstream = out_grad[0]
    flag = struct((8, 128), F32)
    begun = call(
        flag_kernel, flag, cost_estimate=pl.CostEstimate(flops=10**10, bytes_accessed=1, transcendentals=0)
    )
    passed = (feats, upstream, gain1, gain2)
    counts, scales, feats_near, up_near, gain1_near, gain2_near = call(
        functools.partial(count_kernel, groups),
        (struct((rows, tall + rows), F32), struct((8, tall + rows), F32))
        + tuple(struct(x.shape, x.dtype) for x in passed),
        begun,
        partners,
        local_gain,
        expander_gain,
        *passed,
        in_specs=[VM, VM, SM, SM] + [VM] * len(passed),
        cost_estimate=pl.CostEstimate(flops=10**10, bytes_accessed=1, transcendentals=0),
    )
    out_rows, keep_wide, send_wide, keep_square, send_square, own, grad_mixed, *slot_rows = call(
        functools.partial(layer_kernel, slots, count),
        (
            struct((rows, width), BF16),
            struct((2 * width, width), BF16),
            struct((2 * width, width), BF16),
            struct((2 * width, width), BF16),
            struct((2 * width + SMALL, width), BF16),
            struct((rows, width), F32),
            struct((rows, width), F32),
        )
        + tuple(struct((rows, width), BF16) for _ in slots),
        feats_near,
        *others,
        up_near,
        gain1_near,
        w_query,
        w_key,
        w_value,
        w_out,
        gain2_near,
        w_up,
        w_down,
        scales,
        counts,
        scratch_shapes=[
            pltpu.VMEM((stacked, tall + rows), F32),
            pltpu.VMEM((stacked, tall + rows), F32),
            pltpu.VMEM((stacked, tall + rows), BF16),
            pltpu.VMEM((stacked, tall + rows), BF16),
            pltpu.VMEM((4 * width, width), BF16),
            pltpu.VMEM((4 * width, width), BF16),
        ],
    )
    slot_rows = iter(slot_rows)
    slot_quad = [None if k is None else next(slot_rows) for k in quad_slots]
    slot_high = [None if pair == (None, None) else next(slot_rows) for pair in high_slots]

    def present(*items):
        return [x for x in items if x is not None]

    def sized(base, slot):
        return struct((base + (0 if slot is None else rows), width), BF16)

    half = width // 2
    recv_wide = flipped(send_wide, 1, 1)
    recv_square = flipped(send_square, 1, 1)
    data = 2 * half + SMALL
    own_quad, *send_quad = call(
        functools.partial(pair_kernel, [x is not None for x in slot_quad]),
        (struct((data, width), BF16),) + tuple(sized(data, x) for x in slot_quad),
        keep_wide,
        recv_wide,
        keep_square,
        send_square,
        recv_square,
        *present(*slot_quad),
    )
    recv_quad = [flipped(x, bit, bit) for x, bit in zip(send_quad, (2, 4, 6))]
    returned = [x for x, slot in zip(recv_quad, slot_quad) if slot is not None]
    starts = [data] * len(returned)
    wide, square = call(
        functools.partial(quad_kernel, slot_high[0] is not None),
        (sized(half, slot_high[0]), struct((half + SMALL, width), BF16)),
        own_quad,
        *recv_quad,
        *present(slot_high[0]),
    )
    for k in range(len(high_bits)):
        recv_wide = flipped(wide, *orders[0][k])
        recv_square = flipped(square, *orders[1][k])
        if slot_high[k] is not None:
            returned.append(recv_wide)
            starts.append(half)
        slot = slot_high[k + 1] if k + 1 < len(high_bits) else None
        extra = present(slot)
        wide = call(
            functools.partial(double_kernel, half, False, slot is not None),
            sized(half, slot),
            wide,
            recv_wide,
            *extra,
            square,
        )
        square = call(
            functools.partial(double_kernel, half, True, False),
            struct((half + SMALL, width), BF16),
            square,
            recv_square,
            wide,
        )
    base = call(join_kernel, struct((2 * half, width), BF16), wide, square)
    near = [base] + [flipped(base, bit, bit) for bit in (2, 4, 6)]
    over = [flipped(x, 1, 1) for x in near]
    block = struct((rows, width), BF16)
    one = struct((1, width), F32)
    full = struct((width, width), F32)
    few = struct((heads,), F32)
    node_out, grad_feats, grad_gain1, grad_gain2, grad_local, grad_far, ended = call(
        functools.partial(tail_kernel, starts),
        (block, block, one, one, few, few, flag),
        feats_near,
        out_rows,
        own,
        grad_mixed,
        gain1_near,
        square,
        *returned,
    )
    base = call(join_kernel, struct((2 * half, width), BF16), wide, square)
    near = [base] + [flipped(base, bit, bit) for bit in (2, 4, 6)]
    near[3] = call(after_kernel, struct(base.shape, BF16), near[3], ended)
    over = [flipped(x, 1, 1) for x in near]
    grad_wq, grad_wk, grad_wv, grad_wout, grad_up, grad_down = pl.pallas_call(
        spread_kernel,
        out_shape=(full,) * 4 + (struct((width, 2 * width), F32), struct((2 * width, width), F32)),
        in_specs=[VM] * 8,
        out_specs=(ANY,) * 6,
        scratch_shapes=[
            pltpu.VMEM((8, width, width), BF16),
            pltpu.VMEM((8, width, width), F32),
            pltpu.SemaphoreType.DMA((8,)),
        ],
        compiler_params=PARAMS,
    )(*near, *over)
    return (
        node_out[None],
        grad_feats[None],
        grad_gain1.reshape(width),
        grad_wq,
        grad_wk,
        grad_wv,
        grad_wout,
        grad_gain2.reshape(width),
        grad_up,
        grad_down,
        grad_local,
        grad_far,
    )


def solution(mesh):
    whole = P()
    rows = P("rep", "dom", None)
    return jax.shard_map(
        local,
        mesh=mesh,
        in_specs=(rows, rows)
        + (whole,) * 10
        + (P("rep", None, "dom", None), rows, P("rep", "dom")),
        out_specs=(rows, rows) + (whole,) * 10,
        check_vma=False,
    )
```

```python
import functools

import jax
import jax.numpy as jnp
from jax import lax
from jax.experimental import pallas as pl
from jax.experimental.pallas import tpu as pltpu
from jax.sharding import PartitionSpec as P

EPSILON = 1e-05
SCORE_CAP = 5.0
GELU_ROOT = 0.7978845608028654
GELU_CUBIC = 0.044715
SMALL = 16
AXES = ("dom", "rep")
VMEM_LIMIT = 48 * 1024 * 1024
F32 = jnp.float32
BF16 = jnp.bfloat16


def dot(a, b):
    return lax.dot_general(a, b, (((1,), (0,)), ((), ())), preferred_element_type=F32)


def dot_rhs_t(a, b):
    return lax.dot_general(a, b, (((1,), (1,)), ((), ())), preferred_element_type=F32)


def dot_lhs_t(a, b):
    return lax.dot_general(a, b, (((0,), (0,)), ((), ())), preferred_element_type=F32)


def norm_forward(matrix):
    center = jnp.mean(matrix, axis=-1, keepdims=True)
    shifted = matrix - center
    inverse = lax.rsqrt(jnp.mean(shifted * shifted, axis=-1, keepdims=True) + EPSILON)
    return (shifted * inverse, inverse)


def norm_backward(upstream, normed, inverse, gain):
    scaled_up = upstream * gain
    return inverse * (
        scaled_up
        - jnp.mean(scaled_up, axis=-1, keepdims=True)
        - normed * jnp.mean(scaled_up * normed, axis=-1, keepdims=True)
    )


def gelu_parts(preact):
    tangent = jnp.tanh(GELU_ROOT * (preact + GELU_CUBIC * preact * preact * preact))
    result = 0.5 * preact * (1.0 + tangent)
    derivative = 0.5 * (1.0 + tangent) + 0.5 * preact * (1.0 - tangent * tangent) * GELU_ROOT * (
        1.0 + 3.0 * GELU_CUBIC * preact * preact
    )
    return (result, derivative)


def split_parts(rows):
    high = rows.astype(BF16).astype(F32)
    return jnp.concatenate([high, rows - high], axis=0).astype(BF16)


def join_parts(packed):
    wide = packed.astype(F32)
    return wide[: SMALL // 2] + wide[SMALL // 2 :]


def device_bits():
    flat = lax.axis_index("dom") * lax.axis_size("rep") + lax.axis_index("rep")
    return (flat & 1, (flat >> 1) & 3)


def head_masks_of(shape, heads):
    lane = lax.broadcasted_iota(jnp.int32, shape, 1) // (shape[1] // heads)
    return [lane == h for h in range(heads)]


def stack_heads(matrix, masks):
    return jnp.concatenate([jnp.where(m, matrix, 0.0) for m in masks], axis=0).astype(BF16)


def relay(source_refs, out_refs):
    for source, out in zip(source_refs, out_refs):
        out[...] = source[...]


def flag_kernel(flag_ref):
    flag_ref[...] = jnp.zeros(flag_ref.shape, F32)


def count_kernel(groups, flag_ref, perm_ref, local_ref, far_ref, *refs):
    sources = refs[: len(refs) // 2 - 1]
    count_ref, scale_ref = refs[len(sources) : len(sources) + 2]
    relay(sources, refs[len(sources) + 2 :])
    rows = perm_ref.shape[1]
    target = lax.broadcasted_iota(jnp.int32, (rows, rows), 0)
    count_ref[:, :rows] = jnp.ones((rows, rows), F32)
    for g, members in enumerate(groups):
        total = 0.0
        for m in members:
            total = total + jnp.where(target == perm_ref[m : m + 1, :], 1.0, 0.0)
        count_ref[:, (g + 1) * rows : (g + 2) * rows] = total.T
    near = lax.broadcasted_iota(jnp.int32, (1, scale_ref.shape[1]), 1) < rows
    for h in range(local_ref.shape[0]):
        scale_ref[h : h + 1, :] = jnp.where(near, local_ref[h], far_ref[h])


def sort_units(units_ref, keep_ref, send_ref, bits):
    core, quad = bits
    rows = units_ref.shape[0] // 8
    for r in range(4):
        span = slice(r * rows, (r + 1) * rows)
        for owner, out_ref in ((core, keep_ref), (1 - core, send_ref)):
            start = pl.multiple_of((owner * 4 + (quad ^ r)) * rows, rows)
            out_ref[span, :] = units_ref[pl.ds(start, rows), :]


def collapse(matrix, masks):
    rows = matrix.shape[0] // len(masks)
    total = jnp.where(masks[0], matrix[:rows], 0.0)
    for h in range(1, len(masks)):
        total = total + jnp.where(masks[h], matrix[h * rows : (h + 1) * rows], 0.0)
    return total


def layer_kernel(slots, count, *refs):
    feats_refs = refs[: count + 1]
    (
        up_ref,
        gain1_ref,
        wq_ref,
        wk_ref,
        wv_ref,
        wo_ref,
        gain2_ref,
        wup_ref,
        wdown_ref,
        scale_ref,
        count_ref,
    ) = refs[count + 1 : count + 12]
    out_ref, keepw_ref, sendw_ref, keeps_ref, sends_ref, own_ref, mixed_ref = refs[count + 12 : count + 19]
    slot_refs = refs[count + 19 : count + 19 + len(slots)]
    raw_s, tanh_s, weight_s, dscore_s, wide_s, square_s = refs[count + 19 + len(slots) :]

    rows, width = out_ref.shape
    heads = raw_s.shape[0] // rows
    head_dim = width // heads
    scale = 1.0 / float(head_dim) ** 0.5
    bits = device_bits()
    core = bits[0]

    gain1 = gain1_ref[...]
    gain2 = gain2_ref[...]
    upstream = up_ref[...]
    feats = jnp.concatenate([ref[...] for ref in feats_refs], axis=0).astype(F32)
    normed1, _ = norm_forward(feats)
    hidden = (normed1 * gain1).astype(BF16)
    queries = dot(hidden[:rows], wq_ref[...])
    key_all = dot(hidden, wk_ref[...]).astype(BF16)
    value_all = dot(hidden, wv_ref[...]).astype(BF16)

    head_masks = head_masks_of((rows, width), heads)
    query_stack = stack_heads(queries, head_masks)
    raw_s[...] = dot_rhs_t(query_stack, key_all) * scale

    counts = count_ref[...]
    for h in range(heads):
        block = pl.ds(h * rows, rows)
        tangent = jnp.tanh(raw_s[block, :] * (scale_ref[h : h + 1, :] * (1.0 / SCORE_CAP)))
        tanh_s[block, :] = tangent
        powers = jnp.exp(SCORE_CAP * tangent) * counts
        weight_s[block, :] = (powers * (1.0 / jnp.sum(powers, axis=1, keepdims=True))).astype(BF16)

    attended32 = collapse(dot(weight_s[...], value_all), head_masks)
    attended = attended32.astype(BF16)
    mixed = (feats[:rows] + dot(attended, wo_ref[...])).astype(BF16)
    normed2, inverse2 = norm_forward(mixed.astype(F32))
    hidden2 = (normed2 * gain2).astype(BF16)
    preact = dot(hidden2, wup_ref[...])
    act32, derivative = gelu_parts(preact)
    act = act32.astype(BF16)
    out_ref[...] = (mixed.astype(F32) + dot(act, wdown_ref[...])).astype(BF16)
    grad_down = dot_lhs_t(act, upstream)
    wide_s[2 * width : 3 * width, :] = grad_down[:width].astype(BF16)
    wide_s[3 * width : 4 * width, :] = grad_down[width:].astype(BF16)
    grad_pre = (dot_rhs_t(upstream, wdown_ref[...]) * derivative).astype(BF16)
    grad_up = dot_lhs_t(hidden2, grad_pre)
    wide_s[0 * width : 1 * width, :] = grad_up[:, :width].astype(BF16)
    wide_s[1 * width : 2 * width, :] = grad_up[:, width:].astype(BF16)
    grad_hidden2 = dot_rhs_t(grad_pre, wup_ref[...])
    grad_gain2 = jnp.sum(grad_hidden2 * normed2, axis=0, keepdims=True)
    grad_mixed = upstream.astype(F32) + norm_backward(grad_hidden2, normed2, inverse2, gain2)
    mixed_ref[...] = grad_mixed
    grad_mixed16 = grad_mixed.astype(BF16)
    square_s[3 * width : 4 * width, :] = dot_lhs_t(attended, grad_mixed16).astype(BF16)
    grad_att = dot_rhs_t(grad_mixed16, wo_ref[...]).astype(BF16).astype(F32)
    grad_stack = stack_heads(grad_att, head_masks)
    product = grad_att * attended32
    dots = dot_rhs_t(grad_stack, value_all)

    local_terms = []
    far_terms = []
    for h in range(heads):
        block = pl.ds(h * rows, rows)
        delta = jnp.sum(jnp.where(head_masks[h], product, 0.0), axis=1, keepdims=True)
        tangent = tanh_s[block, :]
        slope = 1.0 - tangent * tangent
        dlogit = weight_s[block, :].astype(F32) * (dots[h * rows : (h + 1) * rows] - delta)
        sloped = dlogit * slope
        terms = jnp.sum(sloped * raw_s[block, :], axis=0, keepdims=True)
        local_terms.append(jnp.sum(terms[:, :rows], axis=1, keepdims=True))
        far_terms.append(jnp.sum(terms[:, rows:], axis=1, keepdims=True))
        dscore_s[block, :] = (sloped * (scale_ref[h : h + 1, :] * scale)).astype(BF16)

    grad_query = collapse(dot(dscore_s[...], key_all), head_masks).astype(BF16)
    grad_key = dot_lhs_t(dscore_s[...], query_stack).astype(BF16)
    grad_value = dot_lhs_t(weight_s[...], grad_stack).astype(BF16)
    square_s[0 * width : 1 * width, :] = dot_lhs_t(hidden[:rows], grad_query).astype(BF16)
    square_s[1 * width : 2 * width, :] = dot_lhs_t(hidden, grad_key).astype(BF16)
    square_s[2 * width : 3 * width, :] = dot_lhs_t(hidden, grad_value).astype(BF16)
    grad_hidden = dot_rhs_t(grad_key, wk_ref[...]) + dot_rhs_t(grad_value, wv_ref[...])
    own = grad_hidden[:rows] + dot_rhs_t(grad_query, wq_ref[...])
    own_ref[...] = own
    grad_gain1 = jnp.sum(own * normed1[:rows], axis=0, keepdims=True)
    grad_gain1 = grad_gain1 + jnp.sum(grad_hidden[rows:] * normed1[rows:], axis=0, keepdims=True)
    back = [grad_hidden[(k + 1) * rows : (k + 2) * rows] for k in range(count)]
    for (even, odd), ref in zip(slots, slot_refs):
        ref[...] = jnp.where(
            core == 1, 0.0 if odd is None else back[odd], 0.0 if even is None else back[even]
        ).astype(BF16)

    column = lax.broadcasted_iota(jnp.int32, (1, width), 1)
    gains = jnp.zeros((1, width), F32)
    for h in range(heads):
        gains = jnp.where(column == h, local_terms[h], gains)
        gains = jnp.where(column == heads + h, far_terms[h], gains)
    line = lax.broadcasted_iota(jnp.int32, (SMALL // 2, width), 0)
    small = jnp.where(line == 0, grad_gain1, jnp.where(line == 1, grad_gain2, jnp.where(line == 2, gains, 0.0)))
    sends_ref[keeps_ref.shape[0] :, :] = split_parts(small)
    sort_units(wide_s, keepw_ref, sendw_ref, bits)
    sort_units(square_s, keeps_ref, sends_ref, bits)


def pair_kernel(slots, apart, keepw_ref, recvw_ref, keeps_ref, sents_ref, recvs_ref, *refs):
    slot_refs = refs[: sum(slots)]
    out_refs = refs[sum(slots) + apart :]
    relay(refs[sum(slots) : sum(slots) + apart], out_refs[4:])
    rows = keepw_ref.shape[0] // 4
    wide = (keepw_ref[...].astype(F32) + recvw_ref[...].astype(F32)).astype(BF16)
    square = (keeps_ref[...].astype(F32) + recvs_ref[: 4 * rows, :].astype(F32)).astype(BF16)
    packed = split_parts(join_parts(sents_ref[4 * rows :, :]) + join_parts(recvs_ref[4 * rows :, :]))
    used = 0
    for r in range(4):
        span = slice(r * rows, (r + 1) * rows)
        out_refs[r][:rows, :] = wide[span]
        out_refs[r][rows : 2 * rows, :] = square[span]
        out_refs[r][2 * rows : 2 * rows + SMALL, :] = packed
        if r and slots[r - 1]:
            out_refs[r][2 * rows + SMALL :, :] = slot_refs[used][...]
            used += 1


def quad_kernel(has_slot, own_ref, one_ref, two_ref, three_ref, *refs):
    wide_ref, square_ref = refs[-2:]
    total_rows = own_ref.shape[0]
    rows = (total_rows - SMALL) // 2
    data = [ref[: 2 * rows, :].astype(F32) for ref in (own_ref, one_ref, two_ref, three_ref)]
    small = [join_parts(ref[2 * rows : total_rows, :]) for ref in (own_ref, one_ref, two_ref, three_ref)]
    total = ((data[0] + data[1]) + (data[2] + data[3])).astype(BF16)
    wide_ref[:rows, :] = total[:rows]
    square_ref[:rows, :] = total[rows:]
    square_ref[rows:, :] = split_parts((small[0] + small[1]) + (small[2] + small[3]))
    if has_slot:
        wide_ref[rows:, :] = refs[0][...]


def double_kernel(rows, small, has_slot, own_ref, recv_ref, *refs):
    out_ref = refs[-1]
    total = own_ref[:rows, :].astype(F32) + recv_ref[:rows, :].astype(F32)
    out_ref[:rows, :] = total.astype(BF16)
    if small:
        span = slice(rows, rows + SMALL)
        out_ref[span, :] = split_parts(join_parts(own_ref[span, :]) + join_parts(recv_ref[span, :]))
    if has_slot:
        out_ref[rows:, :] = refs[0][...]


def join_kernel(wide_ref, square_ref, out_ref):
    rows = out_ref.shape[0] // 2
    out_ref[:rows, :] = wide_ref[:rows, :]
    out_ref[rows:, :] = square_ref[:rows, :]


def tail_kernel(start, *refs):
    count = len(start)
    feats_ref, rows_ref, own_ref, mixed_ref, gain_ref, small_ref = refs[:6]
    out_ref, grad_ref, gain1_ref, gain2_ref, local_ref, far_ref, flag_ref = refs[6 + count :]
    out_ref[...] = rows_ref[...]
    normed, inverse = norm_forward(feats_ref[...].astype(F32))
    grad_hidden = own_ref[...]
    for ref, first in zip(refs[6 : 6 + count], start):
        grad_hidden = grad_hidden + ref[first:, :].astype(F32)
    grad = mixed_ref[...] + norm_backward(grad_hidden, normed, inverse, gain_ref[...])
    grad_ref[...] = grad.astype(BF16)
    heads = local_ref.shape[0]
    small = join_parts(small_ref[small_ref.shape[0] - SMALL :, :])
    gain1_ref[...] = small[0:1]
    gain2_ref[...] = small[1:2]
    local_ref[...] = small[2, :heads]
    far_ref[...] = small[2, heads : 2 * heads]
    flag_ref[...] = jnp.zeros(flag_ref.shape, F32)


def after_kernel(source_ref, flag_ref, out_ref):
    out_ref[...] = source_ref[...]


def spread_kernel(*refs):
    piece_refs = refs[:8]
    wq_ref, wk_ref, wv_ref, wo_ref, up_ref, down_ref, pieces, chunks, sems = refs[8:]
    width = wq_ref.shape[0]
    half = width // 2
    core, quad = device_bits()
    relay(piece_refs, [pieces.at[k] for k in range(8)])
    targets = [
        up_ref.at[:, :width],
        up_ref.at[:, width:],
        down_ref.at[:width, :],
        down_ref.at[width:, :],
        wq_ref,
        wk_ref,
        wv_ref,
        wo_ref,
    ]
    copies = []
    for chunk, target in enumerate(targets):
        first = 0 if chunk < 4 else half
        for part in range(2):
            unit = 2 * (chunk % 4) + part
            rel = (core ^ (unit >> 2)) * 4 + (quad ^ (unit & 3))
            value = pieces[rel, first : first + half, :]
            chunks[chunk, part * half : (part + 1) * half, :] = value.astype(F32)
        copy = pltpu.make_async_copy(chunks.at[chunk], target, sems.at[chunk])
        copy.start()
        copies.append(copy)
    for copy in copies:
        copy.wait()


def struct(shape, dtype):
    return jax.ShapeDtypeStruct(shape, dtype)


VM = pl.BlockSpec(memory_space=pltpu.VMEM)
SM = pl.BlockSpec(memory_space=pltpu.SMEM)
ANY = pl.BlockSpec(memory_space=pl.ANY)
PARAMS = pltpu.CompilerParams(vmem_limit_bytes=VMEM_LIMIT)


def call(kernel, outs, *args, in_specs=None, **kwargs):
    return pl.pallas_call(
        kernel,
        out_shape=outs,
        in_specs=in_specs or [VM] * len(args),
        out_specs=jax.tree.map(lambda _: VM, outs),
        compiler_params=PARAMS,
        **kwargs,
    )(*args)


def flipped(x, bits_even, bits_odd):
    size = lax.axis_size("dom") * lax.axis_size("rep")
    pairs = [(i, i ^ (bits_odd if i & 1 else bits_even)) for i in range(size)]
    return lax.ppermute(x, AXES, pairs)


def local(
    node_feats,
    out_grad,
    norm1_gain,
    w_query,
    w_key,
    w_value,
    w_out,
    norm2_gain,
    w_up,
    w_down,
    local_gain,
    expander_gain,
    partner_perm,
    block_pairs,
    pair_count,
):
    feats = node_feats[0]
    partners = partner_perm[0, :, 0, :]
    rows, width = feats.shape
    heads = local_gain.shape[0]
    size = lax.axis_size("dom") * lax.axis_size("rep")
    levels = lax.axis_size("dom").bit_length() - 1
    by_bit = {}
    for matching in range(partners.shape[0]):
        by_bit.setdefault((levels - 1 - matching) % levels, []).append(matching)
    bits = sorted(by_bit)
    groups = [by_bit[b] for b in bits]

    def swapped(x, bit):
        return lax.ppermute(x, "dom", [(i, i ^ 1 << bit) for i in range(lax.axis_size("dom"))])

    rep_bits = lax.axis_size("rep").bit_length() - 1
    high_bits = [1 << k for k in range(3, size.bit_length() - 1)]
    flat = {1 << (b + rep_bits): k for k, b in enumerate(bits)}
    quad_slots = [flat.get(bit) for bit in (2, 4, 6)]
    orders = (list(zip(high_bits, high_bits[::-1])), list(zip(high_bits[::-1], high_bits)))
    apart = [k for bit, k in flat.items() if bit > 4]
    slots = [(k, k) for k in quad_slots if k is not None]
    slots += [(k, k) for k in apart]

    others = [swapped(feats, b) for b in bits]
    count = len(bits)
    tall = count * rows
    stacked = heads * rows
    gain1 = norm1_gain.reshape(1, width)
    gain2 = norm2_gain.reshape(1, width)
    upstream = out_grad[0]
    flag = struct((8, 128), F32)
    begun = call(
        flag_kernel, flag, cost_estimate=pl.CostEstimate(flops=10**10, bytes_accessed=1, transcendentals=0)
    )
    passed = (feats, upstream, gain1, gain2)
    counts, scales, feats_near, up_near, gain1_near, gain2_near = call(
        functools.partial(count_kernel, groups),
        (struct((rows, tall + rows), F32), struct((8, tall + rows), F32))
        + tuple(struct(x.shape, x.dtype) for x in passed),
        begun,
        partners,
        local_gain,
        expander_gain,
        *passed,
        in_specs=[VM, VM, SM, SM] + [VM] * len(passed),
        cost_estimate=pl.CostEstimate(flops=10**10, bytes_accessed=1, transcendentals=0),
    )
    out_rows, keep_wide, send_wide, keep_square, send_square, own, grad_mixed, *slot_rows = call(
        functools.partial(layer_kernel, slots, count),
        (
            struct((rows, width), BF16),
            struct((2 * width, width), BF16),
            struct((2 * width, width), BF16),
            struct((2 * width, width), BF16),
            struct((2 * width + SMALL, width), BF16),
            struct((rows, width), F32),
            struct((rows, width), F32),
        )
        + tuple(struct((rows, width), BF16) for _ in slots),
        feats_near,
        *others,
        up_near,
        gain1_near,
        w_query,
        w_key,
        w_value,
        w_out,
        gain2_near,
        w_up,
        w_down,
        scales,
        counts,
        scratch_shapes=[
            pltpu.VMEM((stacked, tall + rows), F32),
            pltpu.VMEM((stacked, tall + rows), F32),
            pltpu.VMEM((stacked, tall + rows), BF16),
            pltpu.VMEM((stacked, tall + rows), BF16),
            pltpu.VMEM((4 * width, width), BF16),
            pltpu.VMEM((4 * width, width), BF16),
        ],
    )
    slot_rows = iter(slot_rows)
    slot_quad = [None if k is None else next(slot_rows) for k in quad_slots]
    slot_apart = list(slot_rows)

    def present(*items):
        return [x for x in items if x is not None]

    def sized(base, slot):
        return struct((base + (0 if slot is None else rows), width), BF16)

    half = width // 2
    recv_wide = flipped(send_wide, 1, 1)
    recv_square = flipped(send_square, 1, 1)
    data = 2 * half + SMALL
    block = struct((rows, width), BF16)
    own_quad, *send_quad = call(
        functools.partial(pair_kernel, [x is not None for x in slot_quad], len(apart)),
        (struct((data, width), BF16),) + tuple(sized(data, x) for x in slot_quad) + (block,) * len(apart),
        keep_wide,
        recv_wide,
        keep_square,
        send_square,
        recv_square,
        *present(*slot_quad),
        *slot_apart,
    )
    send_quad, send_apart = send_quad[:3], send_quad[3:]
    recv_quad = [flipped(x, bit, bit) for x, bit in zip(send_quad, (2, 4, 6))]
    returned = [x for x, slot in zip(recv_quad, slot_quad) if slot is not None]
    starts = [data] * len(returned) + [0] * len(apart)
    recv_apart = [swapped(x, bits[k]) for x, k in zip(send_apart, apart)]
    returned += recv_apart
    wide, square = call(
        functools.partial(quad_kernel, False),
        (struct((half, width), BF16), struct((half + SMALL, width), BF16)),
        own_quad,
        *recv_quad,
        *recv_apart,
    )
    for k in range(len(high_bits)):
        recv_wide = flipped(wide, *orders[0][k])
        recv_square = flipped(square, *orders[1][k])
        wide = call(
            functools.partial(double_kernel, half, False, False),
            struct((half, width), BF16),
            wide,
            recv_wide,
            square,
        )
        square = call(
            functools.partial(double_kernel, half, True, False),
            struct((half + SMALL, width), BF16),
            square,
            recv_square,
            wide,
        )
    block = struct((rows, width), BF16)
    one = struct((1, width), F32)
    full = struct((width, width), F32)
    few = struct((heads,), F32)
    node_out, grad_feats, grad_gain1, grad_gain2, grad_local, grad_far, ended = call(
        functools.partial(tail_kernel, starts),
        (block, block, one, one, few, few, flag),
        feats_near,
        out_rows,
        own,
        grad_mixed,
        gain1_near,
        square,
        *returned,
    )
    base = call(join_kernel, struct((2 * half, width), BF16), wide, square)
    near = [base] + [flipped(base, bit, bit) for bit in (2, 4, 6)]
    near[3] = call(after_kernel, struct(base.shape, BF16), near[3], ended)
    over = [flipped(x, 1, 1) for x in near]
    grad_wq, grad_wk, grad_wv, grad_wout, grad_up, grad_down = pl.pallas_call(
        spread_kernel,
        out_shape=(full,) * 4 + (struct((width, 2 * width), F32), struct((2 * width, width), F32)),
        in_specs=[VM] * 8,
        out_specs=(ANY,) * 6,
        scratch_shapes=[
            pltpu.VMEM((8, width, width), BF16),
            pltpu.VMEM((8, width, width), F32),
            pltpu.SemaphoreType.DMA((8,)),
        ],
        compiler_params=PARAMS,
    )(*near, *over)
    return (
        node_out[None],
        grad_feats[None],
        grad_gain1.reshape(width),
        grad_wq,
        grad_wk,
        grad_wv,
        grad_wout,
        grad_gain2.reshape(width),
        grad_up,
        grad_down,
        grad_local,
        grad_far,
    )


def solution(mesh):
    whole = P()
    rows = P("rep", "dom", None)
    return jax.shard_map(
        local,
        mesh=mesh,
        in_specs=(rows, rows)
        + (whole,) * 10
        + (P("rep", None, "dom", None), rows, P("rep", "dom")),
        out_specs=(rows, rows) + (whole,) * 10,
        check_vma=False,
    )
```

```python
import functools

import jax
import jax.numpy as jnp
from jax import lax
from jax.experimental import pallas as pl
from jax.experimental.pallas import tpu as pltpu
from jax.sharding import PartitionSpec as P

EPSILON = 1e-05
SCORE_CAP = 5.0
GELU_ROOT = 0.7978845608028654
GELU_CUBIC = 0.044715
SMALL = 16
AXES = ("dom", "rep")
VMEM_LIMIT = 48 * 1024 * 1024
F32 = jnp.float32
BF16 = jnp.bfloat16


def dot(a, b):
    return lax.dot_general(a, b, (((1,), (0,)), ((), ())), preferred_element_type=F32)


def dot_rhs_t(a, b):
    return lax.dot_general(a, b, (((1,), (1,)), ((), ())), preferred_element_type=F32)


def dot_lhs_t(a, b):
    return lax.dot_general(a, b, (((0,), (0,)), ((), ())), preferred_element_type=F32)


def norm_forward(matrix):
    center = jnp.mean(matrix, axis=-1, keepdims=True)
    shifted = matrix - center
    inverse = lax.rsqrt(jnp.mean(shifted * shifted, axis=-1, keepdims=True) + EPSILON)
    return (shifted * inverse, inverse)


def norm_backward(upstream, normed, inverse, gain):
    scaled_up = upstream * gain
    return inverse * (
        scaled_up
        - jnp.mean(scaled_up, axis=-1, keepdims=True)
        - normed * jnp.mean(scaled_up * normed, axis=-1, keepdims=True)
    )


def gelu_parts(preact):
    tangent = jnp.tanh(GELU_ROOT * (preact + GELU_CUBIC * preact * preact * preact))
    result = 0.5 * preact * (1.0 + tangent)
    derivative = 0.5 * (1.0 + tangent) + 0.5 * preact * (1.0 - tangent * tangent) * GELU_ROOT * (
        1.0 + 3.0 * GELU_CUBIC * preact * preact
    )
    return (result, derivative)


def split_parts(rows):
    high = rows.astype(BF16).astype(F32)
    return jnp.concatenate([high, rows - high], axis=0).astype(BF16)


def join_parts(packed):
    wide = packed.astype(F32)
    return wide[: SMALL // 2] + wide[SMALL // 2 :]


def device_bits():
    flat = lax.axis_index("dom") * lax.axis_size("rep") + lax.axis_index("rep")
    return (flat & 1, (flat >> 1) & 3)


def head_masks_of(shape, heads):
    lane = lax.broadcasted_iota(jnp.int32, shape, 1) // (shape[1] // heads)
    return [lane == h for h in range(heads)]


def stack_heads(matrix, masks):
    return jnp.concatenate([jnp.where(m, matrix, 0.0) for m in masks], axis=0).astype(BF16)


def relay(source_refs, out_refs):
    for source, out in zip(source_refs, out_refs):
        out[...] = source[...]


def flag_kernel(flag_ref):
    flag_ref[...] = jnp.zeros(flag_ref.shape, F32)


def count_kernel(groups, flag_ref, perm_ref, local_ref, far_ref, *refs):
    sources = refs[: len(refs) // 2 - 1]
    count_ref, scale_ref = refs[len(sources) : len(sources) + 2]
    relay(sources, refs[len(sources) + 2 :])
    rows = perm_ref.shape[1]
    target = lax.broadcasted_iota(jnp.int32, (rows, rows), 0)
    count_ref[:, :rows] = jnp.ones((rows, rows), F32)
    for g, members in enumerate(groups):
        total = 0.0
        for m in members:
            total = total + jnp.where(target == perm_ref[m : m + 1, :], 1.0, 0.0)
        count_ref[:, (g + 1) * rows : (g + 2) * rows] = total.T
    near = lax.broadcasted_iota(jnp.int32, (1, scale_ref.shape[1]), 1) < rows
    for h in range(local_ref.shape[0]):
        scale_ref[h : h + 1, :] = jnp.where(near, local_ref[h], far_ref[h])


def unit_of(units_ref, owner, rel):
    rows = units_ref.shape[0] // 8
    return units_ref[pl.ds(pl.multiple_of((owner * 4 + rel) * rows, rows), rows), :]


def sort_units(units_ref, send_ref, bits):
    core, quad = bits
    rows = units_ref.shape[0] // 8
    for r in range(4):
        send_ref[r * rows : (r + 1) * rows, :] = unit_of(units_ref, 1 - core, quad ^ r)


def collapse(matrix, masks):
    rows = matrix.shape[0] // len(masks)
    total = jnp.where(masks[0], matrix[:rows], 0.0)
    for h in range(1, len(masks)):
        total = total + jnp.where(masks[h], matrix[h * rows : (h + 1) * rows], 0.0)
    return total


def layer_kernel(slots, count, *refs):
    feats_refs = refs[: count + 1]
    (
        up_ref,
        gain1_ref,
        wq_ref,
        wk_ref,
        wv_ref,
        wo_ref,
        gain2_ref,
        wup_ref,
        wdown_ref,
        scale_ref,
        count_ref,
    ) = refs[count + 1 : count + 12]
    out_ref, wide_s, sendw_ref, square_s, sends_ref, own_ref, mixed_ref = refs[count + 12 : count + 19]
    slot_refs = refs[count + 19 : count + 19 + len(slots)]
    raw_s, tanh_s, weight_s, dscore_s = refs[count + 19 + len(slots) :]

    rows, width = out_ref.shape
    heads = raw_s.shape[0] // rows
    head_dim = width // heads
    scale = 1.0 / float(head_dim) ** 0.5
    bits = device_bits()
    core = bits[0]

    gain1 = gain1_ref[...]
    gain2 = gain2_ref[...]
    upstream = up_ref[...]
    feats = jnp.concatenate([ref[...] for ref in feats_refs], axis=0).astype(F32)
    normed1, _ = norm_forward(feats)
    hidden = (normed1 * gain1).astype(BF16)
    queries = dot(hidden[:rows], wq_ref[...])
    key_all = dot(hidden, wk_ref[...]).astype(BF16)
    value_all = dot(hidden, wv_ref[...]).astype(BF16)

    head_masks = head_masks_of((rows, width), heads)
    query_stack = stack_heads(queries, head_masks)
    raw_s[...] = dot_rhs_t(query_stack, key_all) * scale

    counts = count_ref[...]
    for h in range(heads):
        block = pl.ds(h * rows, rows)
        tangent = jnp.tanh(raw_s[block, :] * (scale_ref[h : h + 1, :] * (1.0 / SCORE_CAP)))
        tanh_s[block, :] = tangent
        powers = jnp.exp(SCORE_CAP * tangent) * counts
        weight_s[block, :] = (powers * (1.0 / jnp.sum(powers, axis=1, keepdims=True))).astype(BF16)

    attended32 = collapse(dot(weight_s[...], value_all), head_masks)
    attended = attended32.astype(BF16)
    mixed = (feats[:rows] + dot(attended, wo_ref[...])).astype(BF16)
    normed2, inverse2 = norm_forward(mixed.astype(F32))
    hidden2 = (normed2 * gain2).astype(BF16)
    preact = dot(hidden2, wup_ref[...])
    act32, derivative = gelu_parts(preact)
    act = act32.astype(BF16)
    out_ref[...] = (mixed.astype(F32) + dot(act, wdown_ref[...])).astype(BF16)
    grad_down = dot_lhs_t(act, upstream)
    wide_s[2 * width : 3 * width, :] = grad_down[:width].astype(BF16)
    wide_s[3 * width : 4 * width, :] = grad_down[width:].astype(BF16)
    grad_pre = (dot_rhs_t(upstream, wdown_ref[...]) * derivative).astype(BF16)
    grad_up = dot_lhs_t(hidden2, grad_pre)
    wide_s[0 * width : 1 * width, :] = grad_up[:, :width].astype(BF16)
    wide_s[1 * width : 2 * width, :] = grad_up[:, width:].astype(BF16)
    grad_hidden2 = dot_rhs_t(grad_pre, wup_ref[...])
    grad_gain2 = jnp.sum(grad_hidden2 * normed2, axis=0, keepdims=True)
    grad_mixed = upstream.astype(F32) + norm_backward(grad_hidden2, normed2, inverse2, gain2)
    mixed_ref[...] = grad_mixed
    grad_mixed16 = grad_mixed.astype(BF16)
    square_s[3 * width : 4 * width, :] = dot_lhs_t(attended, grad_mixed16).astype(BF16)
    grad_att = dot_rhs_t(grad_mixed16, wo_ref[...]).astype(BF16).astype(F32)
    grad_stack = stack_heads(grad_att, head_masks)
    product = grad_att * attended32
    dots = dot_rhs_t(grad_stack, value_all)

    local_terms = []
    far_terms = []
    for h in range(heads):
        block = pl.ds(h * rows, rows)
        delta = jnp.sum(jnp.where(head_masks[h], product, 0.0), axis=1, keepdims=True)
        tangent = tanh_s[block, :]
        slope = 1.0 - tangent * tangent
        dlogit = weight_s[block, :].astype(F32) * (dots[h * rows : (h + 1) * rows] - delta)
        sloped = dlogit * slope
        terms = jnp.sum(sloped * raw_s[block, :], axis=0, keepdims=True)
        local_terms.append(jnp.sum(terms[:, :rows], axis=1, keepdims=True))
        far_terms.append(jnp.sum(terms[:, rows:], axis=1, keepdims=True))
        dscore_s[block, :] = (sloped * (scale_ref[h : h + 1, :] * scale)).astype(BF16)

    grad_query = collapse(dot(dscore_s[...], key_all), head_masks).astype(BF16)
    grad_key = dot_lhs_t(dscore_s[...], query_stack).astype(BF16)
    grad_value = dot_lhs_t(weight_s[...], grad_stack).astype(BF16)
    square_s[0 * width : 1 * width, :] = dot_lhs_t(hidden[:rows], grad_query).astype(BF16)
    square_s[1 * width : 2 * width, :] = dot_lhs_t(hidden, grad_key).astype(BF16)
    square_s[2 * width : 3 * width, :] = dot_lhs_t(hidden, grad_value).astype(BF16)
    grad_hidden = dot_rhs_t(grad_key, wk_ref[...]) + dot_rhs_t(grad_value, wv_ref[...])
    own = grad_hidden[:rows] + dot_rhs_t(grad_query, wq_ref[...])
    own_ref[...] = own
    grad_gain1 = jnp.sum(own * normed1[:rows], axis=0, keepdims=True)
    grad_gain1 = grad_gain1 + jnp.sum(grad_hidden[rows:] * normed1[rows:], axis=0, keepdims=True)
    back = [grad_hidden[(k + 1) * rows : (k + 2) * rows] for k in range(count)]
    for (even, odd), ref in zip(slots, slot_refs):
        ref[...] = jnp.where(
            core == 1, 0.0 if odd is None else back[odd], 0.0 if even is None else back[even]
        ).astype(BF16)

    column = lax.broadcasted_iota(jnp.int32, (1, width), 1)
    gains = jnp.zeros((1, width), F32)
    for h in range(heads):
        gains = jnp.where(column == h, local_terms[h], gains)
        gains = jnp.where(column == heads + h, far_terms[h], gains)
    line = lax.broadcasted_iota(jnp.int32, (SMALL // 2, width), 0)
    small = jnp.where(line == 0, grad_gain1, jnp.where(line == 1, grad_gain2, jnp.where(line == 2, gains, 0.0)))
    sends_ref[sendw_ref.shape[0] :, :] = split_parts(small)
    sort_units(wide_s, sendw_ref, bits)
    sort_units(square_s, sends_ref, bits)


def pair_kernel(slots, apart, keepw_ref, recvw_ref, keeps_ref, sents_ref, recvs_ref, *refs):
    slot_refs = refs[: sum(slots)]
    out_refs = refs[sum(slots) + apart :]
    relay(refs[sum(slots) : sum(slots) + apart], out_refs[4:])
    rows = keepw_ref.shape[0] // 8
    core, quad = device_bits()
    packed = split_parts(join_parts(sents_ref[4 * rows :, :]) + join_parts(recvs_ref[4 * rows :, :]))
    used = 0
    for r in range(4):
        span = slice(r * rows, (r + 1) * rows)
        wide = unit_of(keepw_ref, core, quad ^ r).astype(F32) + recvw_ref[span, :].astype(F32)
        square = unit_of(keeps_ref, core, quad ^ r).astype(F32) + recvs_ref[span, :].astype(F32)
        out_refs[r][:rows, :] = wide.astype(BF16)
        out_refs[r][rows : 2 * rows, :] = square.astype(BF16)
        out_refs[r][2 * rows : 2 * rows + SMALL, :] = packed
        if r and slots[r - 1]:
            out_refs[r][2 * rows + SMALL :, :] = slot_refs[used][...]
            used += 1


def quad_kernel(has_slot, own_ref, one_ref, two_ref, three_ref, *refs):
    wide_ref, square_ref = refs[-2:]
    total_rows = own_ref.shape[0]
    rows = (total_rows - SMALL) // 2
    data = [ref[: 2 * rows, :].astype(F32) for ref in (own_ref, one_ref, two_ref, three_ref)]
    small = [join_parts(ref[2 * rows : total_rows, :]) for ref in (own_ref, one_ref, two_ref, three_ref)]
    total = ((data[0] + data[1]) + (data[2] + data[3])).astype(BF16)
    wide_ref[:rows, :] = total[:rows]
    square_ref[:rows, :] = total[rows:]
    square_ref[rows:, :] = split_parts((small[0] + small[1]) + (small[2] + small[3]))
    if has_slot:
        wide_ref[rows:, :] = refs[0][...]


def double_kernel(rows, small, has_slot, own_ref, recv_ref, *refs):
    out_ref = refs[-1]
    total = own_ref[:rows, :].astype(F32) + recv_ref[:rows, :].astype(F32)
    out_ref[:rows, :] = total.astype(BF16)
    if small:
        span = slice(rows, rows + SMALL)
        out_ref[span, :] = split_parts(join_parts(own_ref[span, :]) + join_parts(recv_ref[span, :]))
    if has_slot:
        out_ref[rows:, :] = refs[0][...]


def join_kernel(wide_ref, square_ref, out_ref):
    rows = out_ref.shape[0] // 2
    out_ref[:rows, :] = wide_ref[:rows, :]
    out_ref[rows:, :] = square_ref[:rows, :]


def tail_kernel(start, *refs):
    count = len(start)
    feats_ref, rows_ref, own_ref, mixed_ref, gain_ref, small_ref = refs[:6]
    out_ref, grad_ref, gain1_ref, gain2_ref, local_ref, far_ref, flag_ref = refs[6 + count :]
    out_ref[...] = rows_ref[...]
    normed, inverse = norm_forward(feats_ref[...].astype(F32))
    grad_hidden = own_ref[...]
    for ref, first in zip(refs[6 : 6 + count], start):
        grad_hidden = grad_hidden + ref[first:, :].astype(F32)
    grad = mixed_ref[...] + norm_backward(grad_hidden, normed, inverse, gain_ref[...])
    grad_ref[...] = grad.astype(BF16)
    heads = local_ref.shape[0]
    small = join_parts(small_ref[small_ref.shape[0] - SMALL :, :])
    gain1_ref[...] = small[0:1]
    gain2_ref[...] = small[1:2]
    local_ref[...] = small[2, :heads]
    far_ref[...] = small[2, heads : 2 * heads]
    flag_ref[...] = jnp.zeros(flag_ref.shape, F32)


def after_kernel(source_ref, flag_ref, out_ref):
    out_ref[...] = source_ref[...]


def spread_kernel(own, *refs):
    piece_refs = refs[:4]
    wq_ref, wk_ref, wv_ref, wo_ref, up_ref, down_ref, pieces, chunks, sems = refs[-9:]
    width = wq_ref.shape[0]
    half = width // 2
    core, quad = device_bits()
    side = core if own else 1 - core
    relay(piece_refs, [pieces.at[k] for k in range(4)])
    low = [up_ref.at[:, :width], up_ref.at[:, width:], wq_ref, wk_ref]
    high = [down_ref.at[:width, :], down_ref.at[width:, :], wv_ref, wo_ref]

    for bit, targets in enumerate((low, high)):

        @pl.when(side == bit)
        def _():
            copies = []
            for slot, target in enumerate(targets):
                first = 0 if slot < 2 else half
                for part in range(2):
                    value = pieces[quad ^ (2 * (slot % 2) + part), first : first + half, :]
                    chunks[slot, part * half : (part + 1) * half, :] = value.astype(F32)
                copy = pltpu.make_async_copy(chunks.at[slot], target, sems.at[slot])
                copy.start()
                copies.append(copy)
            for copy in copies:
                copy.wait()


def struct(shape, dtype):
    return jax.ShapeDtypeStruct(shape, dtype)


VM = pl.BlockSpec(memory_space=pltpu.VMEM)
SM = pl.BlockSpec(memory_space=pltpu.SMEM)
ANY = pl.BlockSpec(memory_space=pl.ANY)
PARAMS = pltpu.CompilerParams(vmem_limit_bytes=VMEM_LIMIT)


def call(kernel, outs, *args, in_specs=None, **kwargs):
    return pl.pallas_call(
        kernel,
        out_shape=outs,
        in_specs=in_specs or [VM] * len(args),
        out_specs=jax.tree.map(lambda _: VM, outs),
        compiler_params=PARAMS,
        **kwargs,
    )(*args)


def flipped(x, bits_even, bits_odd):
    size = lax.axis_size("dom") * lax.axis_size("rep")
    pairs = [(i, i ^ (bits_odd if i & 1 else bits_even)) for i in range(size)]
    return lax.ppermute(x, AXES, pairs)


def local(
    node_feats,
    out_grad,
    norm1_gain,
    w_query,
    w_key,
    w_value,
    w_out,
    norm2_gain,
    w_up,
    w_down,
    local_gain,
    expander_gain,
    partner_perm,
    block_pairs,
    pair_count,
):
    feats = node_feats[0]
    partners = partner_perm[0, :, 0, :]
    rows, width = feats.shape
    heads = local_gain.shape[0]
    size = lax.axis_size("dom") * lax.axis_size("rep")
    levels = lax.axis_size("dom").bit_length() - 1
    by_bit = {}
    for matching in range(partners.shape[0]):
        by_bit.setdefault((levels - 1 - matching) % levels, []).append(matching)
    bits = sorted(by_bit)
    groups = [by_bit[b] for b in bits]

    def swapped(x, bit):
        return lax.ppermute(x, "dom", [(i, i ^ 1 << bit) for i in range(lax.axis_size("dom"))])

    rep_bits = lax.axis_size("rep").bit_length() - 1
    high_bits = [1 << k for k in range(3, size.bit_length() - 1)]
    flat = {1 << (b + rep_bits): k for k, b in enumerate(bits)}
    quad_slots = [flat.get(bit) for bit in (2, 4, 6)]
    orders = (list(zip(high_bits, high_bits[::-1])), list(zip(high_bits[::-1], high_bits)))
    apart = [k for bit, k in flat.items() if bit > 4]
    slots = [(k, k) for k in quad_slots if k is not None]
    slots += [(k, k) for k in apart]

    others = [swapped(feats, b) for b in bits]
    count = len(bits)
    tall = count * rows
    stacked = heads * rows
    gain1 = norm1_gain.reshape(1, width)
    gain2 = norm2_gain.reshape(1, width)
    upstream = out_grad[0]
    flag = struct((8, 128), F32)
    begun = call(
        flag_kernel, flag, cost_estimate=pl.CostEstimate(flops=10**10, bytes_accessed=1, transcendentals=0)
    )
    passed = (feats, upstream, gain1, gain2)
    counts, scales, feats_near, up_near, gain1_near, gain2_near = call(
        functools.partial(count_kernel, groups),
        (struct((rows, tall + rows), F32), struct((8, tall + rows), F32))
        + tuple(struct(x.shape, x.dtype) for x in passed),
        begun,
        partners,
        local_gain,
        expander_gain,
        *passed,
        in_specs=[VM, VM, SM, SM] + [VM] * len(passed),
        cost_estimate=pl.CostEstimate(flops=10**10, bytes_accessed=1, transcendentals=0),
    )
    out_rows, keep_wide, send_wide, keep_square, send_square, own, grad_mixed, *slot_rows = call(
        functools.partial(layer_kernel, slots, count),
        (
            struct((rows, width), BF16),
            struct((4 * width, width), BF16),
            struct((2 * width, width), BF16),
            struct((4 * width, width), BF16),
            struct((2 * width + SMALL, width), BF16),
            struct((rows, width), F32),
            struct((rows, width), F32),
        )
        + tuple(struct((rows, width), BF16) for _ in slots),
        feats_near,
        *others,
        up_near,
        gain1_near,
        w_query,
        w_key,
        w_value,
        w_out,
        gain2_near,
        w_up,
        w_down,
        scales,
        counts,
        scratch_shapes=[
            pltpu.VMEM((stacked, tall + rows), F32),
            pltpu.VMEM((stacked, tall + rows), F32),
            pltpu.VMEM((stacked, tall + rows), BF16),
            pltpu.VMEM((stacked, tall + rows), BF16),
        ],
    )
    slot_rows = iter(slot_rows)
    slot_quad = [None if k is None else next(slot_rows) for k in quad_slots]
    slot_apart = list(slot_rows)

    def present(*items):
        return [x for x in items if x is not None]

    def sized(base, slot):
        return struct((base + (0 if slot is None else rows), width), BF16)

    half = width // 2
    recv_wide = flipped(send_wide, 1, 1)
    recv_square = flipped(send_square, 1, 1)
    data = 2 * half + SMALL
    block = struct((rows, width), BF16)
    own_quad, *send_quad = call(
        functools.partial(pair_kernel, [x is not None for x in slot_quad], len(apart)),
        (struct((data, width), BF16),) + tuple(sized(data, x) for x in slot_quad) + (block,) * len(apart),
        keep_wide,
        recv_wide,
        keep_square,
        send_square,
        recv_square,
        *present(*slot_quad),
        *slot_apart,
    )
    send_quad, send_apart = send_quad[:3], send_quad[3:]
    recv_quad = [flipped(x, bit, bit) for x, bit in zip(send_quad, (2, 4, 6))]
    returned = [x for x, slot in zip(recv_quad, slot_quad) if slot is not None]
    starts = [data] * len(returned) + [0] * len(apart)
    recv_apart = [swapped(x, bits[k]) for x, k in zip(send_apart, apart)]
    returned += recv_apart
    wide, square = call(
        functools.partial(quad_kernel, False),
        (struct((half, width), BF16), struct((half + SMALL, width), BF16)),
        own_quad,
        *recv_quad,
        *recv_apart,
    )
    for k in range(len(high_bits)):
        recv_wide = flipped(wide, *orders[0][k])
        recv_square = flipped(square, *orders[1][k])
        wide = call(
            functools.partial(double_kernel, half, False, False),
            struct((half, width), BF16),
            wide,
            recv_wide,
            square,
        )
        square = call(
            functools.partial(double_kernel, half, True, False),
            struct((half + SMALL, width), BF16),
            square,
            recv_square,
            wide,
        )
    block = struct((rows, width), BF16)
    one = struct((1, width), F32)
    full = struct((width, width), F32)
    few = struct((heads,), F32)
    node_out, grad_feats, grad_gain1, grad_gain2, grad_local, grad_far, ended = call(
        functools.partial(tail_kernel, starts),
        (block, block, one, one, few, few, flag),
        feats_near,
        out_rows,
        own,
        grad_mixed,
        gain1_near,
        square,
        *returned,
    )
    base = call(join_kernel, struct((2 * half, width), BF16), wide, square)
    near = [base] + [flipped(base, bit, bit) for bit in (2, 4, 6)]
    near[3] = call(after_kernel, struct(base.shape, BF16), near[3], ended)
    over = [flipped(x, 1, 1) for x in near]
    grads = (full,) * 4 + (struct((width, 2 * width), F32), struct((2 * width, width), F32))
    for own in (True, False):
        before = [] if own else grads
        grads = pl.pallas_call(
            functools.partial(spread_kernel, own),
            out_shape=tuple(struct(x.shape, x.dtype) for x in grads),
            in_specs=[VM] * 4 + [ANY] * len(before),
            out_specs=(ANY,) * 6,
            scratch_shapes=[
                pltpu.VMEM((4, width, width), BF16),
                pltpu.VMEM((4, width, width), F32),
                pltpu.SemaphoreType.DMA((4,)),
            ],
            input_output_aliases={4 + k: k for k in range(len(before))},
            compiler_params=PARAMS,
        )(*(near if own else over), *before)
    grad_wq, grad_wk, grad_wv, grad_wout, grad_up, grad_down = grads
    return (
        node_out[None],
        grad_feats[None],
        grad_gain1.reshape(width),
        grad_wq,
        grad_wk,
        grad_wv,
        grad_wout,
        grad_gain2.reshape(width),
        grad_up,
        grad_down,
        grad_local,
        grad_far,
    )


def solution(mesh):
    whole = P()
    rows = P("rep", "dom", None)
    return jax.shard_map(
        local,
        mesh=mesh,
        in_specs=(rows, rows)
        + (whole,) * 10
        + (P("rep", None, "dom", None), rows, P("rep", "dom")),
        out_specs=(rows, rows) + (whole,) * 10,
        check_vma=False,
    )
```

```python
import functools

import jax
import jax.numpy as jnp
from jax import lax
from jax.experimental import pallas as pl
from jax.experimental.pallas import tpu as pltpu
from jax.sharding import PartitionSpec as P

EPSILON = 1e-05
SCORE_CAP = 5.0
GELU_ROOT = 0.7978845608028654
GELU_CUBIC = 0.044715
SMALL = 16
AXES = ("dom", "rep")
VMEM_LIMIT = 48 * 1024 * 1024
F32 = jnp.float32
BF16 = jnp.bfloat16


def dot(a, b):
    return lax.dot_general(a, b, (((1,), (0,)), ((), ())), preferred_element_type=F32)


def dot_rhs_t(a, b):
    return lax.dot_general(a, b, (((1,), (1,)), ((), ())), preferred_element_type=F32)


def dot_lhs_t(a, b):
    return lax.dot_general(a, b, (((0,), (0,)), ((), ())), preferred_element_type=F32)


def norm_forward(matrix):
    center = jnp.mean(matrix, axis=-1, keepdims=True)
    shifted = matrix - center
    inverse = lax.rsqrt(jnp.mean(shifted * shifted, axis=-1, keepdims=True) + EPSILON)
    return (shifted * inverse, inverse)


def norm_backward(upstream, normed, inverse, gain):
    scaled_up = upstream * gain
    return inverse * (
        scaled_up
        - jnp.mean(scaled_up, axis=-1, keepdims=True)
        - normed * jnp.mean(scaled_up * normed, axis=-1, keepdims=True)
    )


def gelu_parts(preact):
    tangent = jnp.tanh(GELU_ROOT * (preact + GELU_CUBIC * preact * preact * preact))
    result = 0.5 * preact * (1.0 + tangent)
    derivative = 0.5 * (1.0 + tangent) + 0.5 * preact * (1.0 - tangent * tangent) * GELU_ROOT * (
        1.0 + 3.0 * GELU_CUBIC * preact * preact
    )
    return (result, derivative)


def split_parts(rows):
    high = rows.astype(BF16).astype(F32)
    return jnp.concatenate([high, rows - high], axis=0).astype(BF16)


def join_parts(packed):
    wide = packed.astype(F32)
    return wide[: SMALL // 2] + wide[SMALL // 2 :]


def device_bits():
    flat = lax.axis_index("dom") * lax.axis_size("rep") + lax.axis_index("rep")
    return (flat & 1, (flat >> 1) & 3)


def head_masks_of(shape, heads):
    lane = lax.broadcasted_iota(jnp.int32, shape, 1) // (shape[1] // heads)
    return [lane == h for h in range(heads)]


def stack_heads(matrix, masks):
    return jnp.concatenate([jnp.where(m, matrix, 0.0) for m in masks], axis=0).astype(BF16)


def relay(source_refs, out_refs):
    for source, out in zip(source_refs, out_refs):
        out[...] = source[...]


def flag_kernel(flag_ref):
    flag_ref[...] = jnp.zeros(flag_ref.shape, F32)


def count_kernel(groups, flag_ref, perm_ref, local_ref, far_ref, *refs):
    sources = refs[: len(refs) // 2 - 1]
    count_ref, scale_ref = refs[len(sources) : len(sources) + 2]
    relay(sources, refs[len(sources) + 2 :])
    rows = perm_ref.shape[1]
    target = lax.broadcasted_iota(jnp.int32, (rows, rows), 0)
    count_ref[:, :rows] = jnp.ones((rows, rows), F32)
    for g, members in enumerate(groups):
        total = 0.0
        for m in members:
            total = total + jnp.where(target == perm_ref[m : m + 1, :], 1.0, 0.0)
        count_ref[:, (g + 1) * rows : (g + 2) * rows] = total.T
    near = lax.broadcasted_iota(jnp.int32, (1, scale_ref.shape[1]), 1) < rows
    for h in range(local_ref.shape[0]):
        scale_ref[h : h + 1, :] = jnp.where(near, local_ref[h], far_ref[h])


def unit_of(units_ref, owner, rel):
    rows = units_ref.shape[0] // 8
    return units_ref[pl.ds(pl.multiple_of((owner * 4 + rel) * rows, rows), rows), :]


def sort_units(units_ref, send_ref, bits):
    core, quad = bits
    rows = units_ref.shape[0] // 8
    for r in range(4):
        send_ref[r * rows : (r + 1) * rows, :] = unit_of(units_ref, 1 - core, quad ^ r)


def collapse(matrix, masks):
    rows = matrix.shape[0] // len(masks)
    total = jnp.where(masks[0], matrix[:rows], 0.0)
    for h in range(1, len(masks)):
        total = total + jnp.where(masks[h], matrix[h * rows : (h + 1) * rows], 0.0)
    return total


def layer_kernel(slots, count, *refs):
    feats_refs = refs[: count + 1]
    (
        up_ref,
        gain1_ref,
        wq_ref,
        wk_ref,
        wv_ref,
        wo_ref,
        gain2_ref,
        wup_ref,
        wdown_ref,
        scale_ref,
        count_ref,
    ) = refs[count + 1 : count + 12]
    out_ref, wide_s, sendw_ref, square_s, sends_ref, own_ref, mixed_ref = refs[count + 12 : count + 19]
    slot_refs = refs[count + 19 : count + 19 + len(slots)]
    raw_s, tanh_s, weight_s, dscore_s = refs[count + 19 + len(slots) :]

    rows, width = out_ref.shape
    heads = raw_s.shape[0] // rows
    head_dim = width // heads
    scale = 1.0 / float(head_dim) ** 0.5
    bits = device_bits()
    core = bits[0]

    gain1 = gain1_ref[...]
    gain2 = gain2_ref[...]
    upstream = up_ref[...]
    feats = jnp.concatenate([ref[...] for ref in feats_refs], axis=0).astype(F32)
    normed1, _ = norm_forward(feats)
    hidden = (normed1 * gain1).astype(BF16)
    queries = dot(hidden[:rows], wq_ref[...])
    key_all = dot(hidden, wk_ref[...]).astype(BF16)
    value_all = dot(hidden, wv_ref[...]).astype(BF16)

    head_masks = head_masks_of((rows, width), heads)
    query_stack = stack_heads(queries, head_masks)
    raw_s[...] = dot_rhs_t(query_stack, key_all) * scale

    back = dot_rhs_t(upstream, wdown_ref[...])
    counts = count_ref[...]
    for h in range(heads):
        block = pl.ds(h * rows, rows)
        tangent = jnp.tanh(raw_s[block, :] * (scale_ref[h : h + 1, :] * (1.0 / SCORE_CAP)))
        tanh_s[block, :] = tangent
        powers = jnp.exp(SCORE_CAP * tangent) * counts
        weight_s[block, :] = (powers * (1.0 / jnp.sum(powers, axis=1, keepdims=True))).astype(BF16)

    attended32 = collapse(dot(weight_s[...], value_all), head_masks)
    attended = attended32.astype(BF16)
    mixed = (feats[:rows] + dot(attended, wo_ref[...])).astype(BF16)
    normed2, inverse2 = norm_forward(mixed.astype(F32))
    hidden2 = (normed2 * gain2).astype(BF16)
    preact = dot(hidden2, wup_ref[...])
    act32, derivative = gelu_parts(preact)
    act = act32.astype(BF16)
    grad_pre = (back * derivative).astype(BF16)
    grad_hidden2 = dot_rhs_t(grad_pre, wup_ref[...])
    grad_gain2 = jnp.sum(grad_hidden2 * normed2, axis=0, keepdims=True)
    grad_mixed = upstream.astype(F32) + norm_backward(grad_hidden2, normed2, inverse2, gain2)
    mixed_ref[...] = grad_mixed
    grad_mixed16 = grad_mixed.astype(BF16)
    grad_att = dot_rhs_t(grad_mixed16, wo_ref[...]).astype(BF16).astype(F32)
    grad_stack = stack_heads(grad_att, head_masks)
    product = grad_att * attended32
    dots = dot_rhs_t(grad_stack, value_all)

    out_ref[...] = (mixed.astype(F32) + dot(act, wdown_ref[...])).astype(BF16)
    grad_down = dot_lhs_t(act, upstream)
    wide_s[2 * width : 3 * width, :] = grad_down[:width].astype(BF16)
    wide_s[3 * width : 4 * width, :] = grad_down[width:].astype(BF16)
    grad_up = dot_lhs_t(hidden2, grad_pre)
    wide_s[0 * width : 1 * width, :] = grad_up[:, :width].astype(BF16)
    wide_s[1 * width : 2 * width, :] = grad_up[:, width:].astype(BF16)
    square_s[3 * width : 4 * width, :] = dot_lhs_t(attended, grad_mixed16).astype(BF16)
    local_terms = []
    far_terms = []
    for h in range(heads):
        block = pl.ds(h * rows, rows)
        delta = jnp.sum(jnp.where(head_masks[h], product, 0.0), axis=1, keepdims=True)
        tangent = tanh_s[block, :]
        slope = 1.0 - tangent * tangent
        dlogit = weight_s[block, :].astype(F32) * (dots[h * rows : (h + 1) * rows] - delta)
        sloped = dlogit * slope
        terms = jnp.sum(sloped * raw_s[block, :], axis=0, keepdims=True)
        local_terms.append(jnp.sum(terms[:, :rows], axis=1, keepdims=True))
        far_terms.append(jnp.sum(terms[:, rows:], axis=1, keepdims=True))
        dscore_s[block, :] = (sloped * (scale_ref[h : h + 1, :] * scale)).astype(BF16)

    grad_query = collapse(dot(dscore_s[...], key_all), head_masks).astype(BF16)
    grad_key = dot_lhs_t(dscore_s[...], query_stack).astype(BF16)
    grad_value = dot_lhs_t(weight_s[...], grad_stack).astype(BF16)
    square_s[0 * width : 1 * width, :] = dot_lhs_t(hidden[:rows], grad_query).astype(BF16)
    square_s[1 * width : 2 * width, :] = dot_lhs_t(hidden, grad_key).astype(BF16)
    square_s[2 * width : 3 * width, :] = dot_lhs_t(hidden, grad_value).astype(BF16)
    grad_hidden = dot_rhs_t(grad_key, wk_ref[...]) + dot_rhs_t(grad_value, wv_ref[...])
    own = grad_hidden[:rows] + dot_rhs_t(grad_query, wq_ref[...])
    own_ref[...] = own
    grad_gain1 = jnp.sum(own * normed1[:rows], axis=0, keepdims=True)
    grad_gain1 = grad_gain1 + jnp.sum(grad_hidden[rows:] * normed1[rows:], axis=0, keepdims=True)
    back = [grad_hidden[(k + 1) * rows : (k + 2) * rows] for k in range(count)]
    for (even, odd), ref in zip(slots, slot_refs):
        ref[...] = jnp.where(
            core == 1, 0.0 if odd is None else back[odd], 0.0 if even is None else back[even]
        ).astype(BF16)

    column = lax.broadcasted_iota(jnp.int32, (1, width), 1)
    gains = jnp.zeros((1, width), F32)
    for h in range(heads):
        gains = jnp.where(column == h, local_terms[h], gains)
        gains = jnp.where(column == heads + h, far_terms[h], gains)
    line = lax.broadcasted_iota(jnp.int32, (SMALL // 2, width), 0)
    small = jnp.where(line == 0, grad_gain1, jnp.where(line == 1, grad_gain2, jnp.where(line == 2, gains, 0.0)))
    sends_ref[sendw_ref.shape[0] :, :] = split_parts(small)
    sort_units(wide_s, sendw_ref, bits)
    sort_units(square_s, sends_ref, bits)


def pair_kernel(slots, apart, keepw_ref, recvw_ref, keeps_ref, sents_ref, recvs_ref, *refs):
    slot_refs = refs[: sum(slots)]
    out_refs = refs[sum(slots) + apart :]
    relay(refs[sum(slots) : sum(slots) + apart], out_refs[4:])
    rows = keepw_ref.shape[0] // 8
    core, quad = device_bits()
    packed = split_parts(join_parts(sents_ref[4 * rows :, :]) + join_parts(recvs_ref[4 * rows :, :]))
    used = 0
    for r in range(4):
        span = slice(r * rows, (r + 1) * rows)
        wide = unit_of(keepw_ref, core, quad ^ r).astype(F32) + recvw_ref[span, :].astype(F32)
        square = unit_of(keeps_ref, core, quad ^ r).astype(F32) + recvs_ref[span, :].astype(F32)
        out_refs[r][:rows, :] = wide.astype(BF16)
        out_refs[r][rows : 2 * rows, :] = square.astype(BF16)
        out_refs[r][2 * rows : 2 * rows + SMALL, :] = packed
        if r and slots[r - 1]:
            out_refs[r][2 * rows + SMALL :, :] = slot_refs[used][...]
            used += 1


def quad_kernel(has_slot, own_ref, one_ref, two_ref, three_ref, *refs):
    wide_ref, square_ref = refs[-2:]
    total_rows = own_ref.shape[0]
    rows = (total_rows - SMALL) // 2
    data = [ref[: 2 * rows, :].astype(F32) for ref in (own_ref, one_ref, two_ref, three_ref)]
    small = [join_parts(ref[2 * rows : total_rows, :]) for ref in (own_ref, one_ref, two_ref, three_ref)]
    total = ((data[0] + data[1]) + (data[2] + data[3])).astype(BF16)
    wide_ref[:rows, :] = total[:rows]
    square_ref[:rows, :] = total[rows:]
    square_ref[rows:, :] = split_parts((small[0] + small[1]) + (small[2] + small[3]))
    if has_slot:
        wide_ref[rows:, :] = refs[0][...]


def double_kernel(rows, small, has_slot, own_ref, recv_ref, *refs):
    out_ref = refs[-1]
    total = own_ref[:rows, :].astype(F32) + recv_ref[:rows, :].astype(F32)
    out_ref[:rows, :] = total.astype(BF16)
    if small:
        span = slice(rows, rows + SMALL)
        out_ref[span, :] = split_parts(join_parts(own_ref[span, :]) + join_parts(recv_ref[span, :]))
    if has_slot:
        out_ref[rows:, :] = refs[0][...]


def join_kernel(wide_ref, square_ref, out_ref):
    rows = out_ref.shape[0] // 2
    out_ref[:rows, :] = wide_ref[:rows, :]
    out_ref[rows:, :] = square_ref[:rows, :]


def tail_kernel(start, *refs):
    count = len(start)
    feats_ref, rows_ref, own_ref, mixed_ref, gain_ref, small_ref = refs[:6]
    out_ref, grad_ref, gain1_ref, gain2_ref, local_ref, far_ref, flag_ref = refs[6 + count :]
    out_ref[...] = rows_ref[...]
    normed, inverse = norm_forward(feats_ref[...].astype(F32))
    grad_hidden = own_ref[...]
    for ref, first in zip(refs[6 : 6 + count], start):
        grad_hidden = grad_hidden + ref[first:, :].astype(F32)
    grad = mixed_ref[...] + norm_backward(grad_hidden, normed, inverse, gain_ref[...])
    grad_ref[...] = grad.astype(BF16)
    heads = local_ref.shape[0]
    small = join_parts(small_ref[small_ref.shape[0] - SMALL :, :])
    gain1_ref[...] = small[0:1]
    gain2_ref[...] = small[1:2]
    local_ref[...] = small[2, :heads]
    far_ref[...] = small[2, heads : 2 * heads]
    flag_ref[...] = jnp.zeros(flag_ref.shape, F32)


def after_kernel(source_ref, flag_ref, out_ref):
    out_ref[...] = source_ref[...]


def spread_kernel(own, *refs):
    piece_refs = refs[:4]
    wq_ref, wk_ref, wv_ref, wo_ref, up_ref, down_ref, pieces, chunks, sems = refs[-9:]
    width = wq_ref.shape[0]
    half = width // 2
    core, quad = device_bits()
    side = core if own else 1 - core
    relay(piece_refs, [pieces.at[k] for k in range(4)])
    low = [up_ref.at[:, :width], up_ref.at[:, width:], wq_ref, wk_ref]
    high = [down_ref.at[:width, :], down_ref.at[width:, :], wv_ref, wo_ref]

    for bit, targets in enumerate((low, high)):

        @pl.when(side == bit)
        def _():
            copies = []
            for slot, target in enumerate(targets):
                first = 0 if slot < 2 else half
                for part in range(2):
                    value = pieces[quad ^ (2 * (slot % 2) + part), first : first + half, :]
                    chunks[slot, part * half : (part + 1) * half, :] = value.astype(F32)
                copy = pltpu.make_async_copy(chunks.at[slot], target, sems.at[slot])
                copy.start()
                copies.append(copy)
            for copy in copies:
                copy.wait()


def struct(shape, dtype):
    return jax.ShapeDtypeStruct(shape, dtype)


VM = pl.BlockSpec(memory_space=pltpu.VMEM)
SM = pl.BlockSpec(memory_space=pltpu.SMEM)
ANY = pl.BlockSpec(memory_space=pl.ANY)
PARAMS = pltpu.CompilerParams(vmem_limit_bytes=VMEM_LIMIT)


def call(kernel, outs, *args, in_specs=None, **kwargs):
    return pl.pallas_call(
        kernel,
        out_shape=outs,
        in_specs=in_specs or [VM] * len(args),
        out_specs=jax.tree.map(lambda _: VM, outs),
        compiler_params=PARAMS,
        **kwargs,
    )(*args)


def flipped(x, bits_even, bits_odd):
    size = lax.axis_size("dom") * lax.axis_size("rep")
    pairs = [(i, i ^ (bits_odd if i & 1 else bits_even)) for i in range(size)]
    return lax.ppermute(x, AXES, pairs)


def local(
    node_feats,
    out_grad,
    norm1_gain,
    w_query,
    w_key,
    w_value,
    w_out,
    norm2_gain,
    w_up,
    w_down,
    local_gain,
    expander_gain,
    partner_perm,
    block_pairs,
    pair_count,
):
    feats = node_feats[0]
    partners = partner_perm[0, :, 0, :]
    rows, width = feats.shape
    heads = local_gain.shape[0]
    size = lax.axis_size("dom") * lax.axis_size("rep")
    levels = lax.axis_size("dom").bit_length() - 1
    by_bit = {}
    for matching in range(partners.shape[0]):
        by_bit.setdefault((levels - 1 - matching) % levels, []).append(matching)
    bits = sorted(by_bit)
    groups = [by_bit[b] for b in bits]

    def swapped(x, bit):
        return lax.ppermute(x, "dom", [(i, i ^ 1 << bit) for i in range(lax.axis_size("dom"))])

    rep_bits = lax.axis_size("rep").bit_length() - 1
    high_bits = [1 << k for k in range(3, size.bit_length() - 1)]
    flat = {1 << (b + rep_bits): k for k, b in enumerate(bits)}
    quad_slots = [flat.get(bit) for bit in (2, 4, 6)]
    orders = (list(zip(high_bits, high_bits[::-1])), list(zip(high_bits[::-1], high_bits)))
    apart = [k for bit, k in flat.items() if bit > 4]
    slots = [(k, k) for k in quad_slots if k is not None]
    slots += [(k, k) for k in apart]

    others = [swapped(feats, b) for b in bits]
    count = len(bits)
    tall = count * rows
    stacked = heads * rows
    gain1 = norm1_gain.reshape(1, width)
    gain2 = norm2_gain.reshape(1, width)
    upstream = out_grad[0]
    flag = struct((8, 128), F32)
    begun = call(
        flag_kernel, flag, cost_estimate=pl.CostEstimate(flops=10**10, bytes_accessed=1, transcendentals=0)
    )
    passed = (feats, upstream, gain1, gain2)
    counts, scales, feats_near, up_near, gain1_near, gain2_near = call(
        functools.partial(count_kernel, groups),
        (struct((rows, tall + rows), F32), struct((8, tall + rows), F32))
        + tuple(struct(x.shape, x.dtype) for x in passed),
        begun,
        partners,
        local_gain,
        expander_gain,
        *passed,
        in_specs=[VM, VM, SM, SM] + [VM] * len(passed),
        cost_estimate=pl.CostEstimate(flops=10**10, bytes_accessed=1, transcendentals=0),
    )
    out_rows, keep_wide, send_wide, keep_square, send_square, own, grad_mixed, *slot_rows = call(
        functools.partial(layer_kernel, slots, count),
        (
            struct((rows, width), BF16),
            struct((4 * width, width), BF16),
            struct((2 * width, width), BF16),
            struct((4 * width, width), BF16),
            struct((2 * width + SMALL, width), BF16),
            struct((rows, width), F32),
            struct((rows, width), F32),
        )
        + tuple(struct((rows, width), BF16) for _ in slots),
        feats_near,
        *others,
        up_near,
        gain1_near,
        w_query,
        w_key,
        w_value,
        w_out,
        gain2_near,
        w_up,
        w_down,
        scales,
        counts,
        scratch_shapes=[
            pltpu.VMEM((stacked, tall + rows), F32),
            pltpu.VMEM((stacked, tall + rows), F32),
            pltpu.VMEM((stacked, tall + rows), BF16),
            pltpu.VMEM((stacked, tall + rows), BF16),
        ],
    )
    slot_rows = iter(slot_rows)
    slot_quad = [None if k is None else next(slot_rows) for k in quad_slots]
    slot_apart = list(slot_rows)

    def present(*items):
        return [x for x in items if x is not None]

    def sized(base, slot):
        return struct((base + (0 if slot is None else rows), width), BF16)

    half = width // 2
    recv_wide = flipped(send_wide, 1, 1)
    recv_square = flipped(send_square, 1, 1)
    data = 2 * half + SMALL
    block = struct((rows, width), BF16)
    own_quad, *send_quad = call(
        functools.partial(pair_kernel, [x is not None for x in slot_quad], len(apart)),
        (struct((data, width), BF16),) + tuple(sized(data, x) for x in slot_quad) + (block,) * len(apart),
        keep_wide,
        recv_wide,
        keep_square,
        send_square,
        recv_square,
        *present(*slot_quad),
        *slot_apart,
    )
    send_quad, send_apart = send_quad[:3], send_quad[3:]
    recv_quad = [flipped(x, bit, bit) for x, bit in zip(send_quad, (2, 4, 6))]
    returned = [x for x, slot in zip(recv_quad, slot_quad) if slot is not None]
    starts = [data] * len(returned) + [0] * len(apart)
    recv_apart = [swapped(x, bits[k]) for x, k in zip(send_apart, apart)]
    returned += recv_apart
    wide, square = call(
        functools.partial(quad_kernel, False),
        (struct((half, width), BF16), struct((half + SMALL, width), BF16)),
        own_quad,
        *recv_quad,
        *recv_apart,
    )
    for k in range(len(high_bits)):
        recv_wide = flipped(wide, *orders[0][k])
        recv_square = flipped(square, *orders[1][k])
        wide = call(
            functools.partial(double_kernel, half, False, False),
            struct((half, width), BF16),
            wide,
            recv_wide,
            square,
        )
        square = call(
            functools.partial(double_kernel, half, True, False),
            struct((half + SMALL, width), BF16),
            square,
            recv_square,
            wide,
        )
    block = struct((rows, width), BF16)
    one = struct((1, width), F32)
    full = struct((width, width), F32)
    few = struct((heads,), F32)
    node_out, grad_feats, grad_gain1, grad_gain2, grad_local, grad_far, ended = call(
        functools.partial(tail_kernel, starts),
        (block, block, one, one, few, few, flag),
        feats_near,
        out_rows,
        own,
        grad_mixed,
        gain1_near,
        square,
        *returned,
    )
    base = call(join_kernel, struct((2 * half, width), BF16), wide, square)
    near = [base] + [flipped(base, bit, bit) for bit in (2, 4, 6)]
    near[3] = call(after_kernel, struct(base.shape, BF16), near[3], ended)
    over = [flipped(x, 1, 1) for x in near]
    grads = (full,) * 4 + (struct((width, 2 * width), F32), struct((2 * width, width), F32))
    for own in (True, False):
        before = [] if own else grads
        grads = pl.pallas_call(
            functools.partial(spread_kernel, own),
            out_shape=tuple(struct(x.shape, x.dtype) for x in grads),
            in_specs=[VM] * 4 + [ANY] * len(before),
            out_specs=(ANY,) * 6,
            scratch_shapes=[
                pltpu.VMEM((4, width, width), BF16),
                pltpu.VMEM((4, width, width), F32),
                pltpu.SemaphoreType.DMA((4,)),
            ],
            input_output_aliases={4 + k: k for k in range(len(before))},
            compiler_params=PARAMS,
        )(*(near if own else over), *before)
    grad_wq, grad_wk, grad_wv, grad_wout, grad_up, grad_down = grads
    return (
        node_out[None],
        grad_feats[None],
        grad_gain1.reshape(width),
        grad_wq,
        grad_wk,
        grad_wv,
        grad_wout,
        grad_gain2.reshape(width),
        grad_up,
        grad_down,
        grad_local,
        grad_far,
    )


def solution(mesh):
    whole = P()
    rows = P("rep", "dom", None)
    return jax.shard_map(
        local,
        mesh=mesh,
        in_specs=(rows, rows)
        + (whole,) * 10
        + (P("rep", None, "dom", None), rows, P("rep", "dom")),
        out_specs=(rows, rows) + (whole,) * 10,
        check_vma=False,
    )
```

```python
import functools

import jax
import jax.numpy as jnp
from jax import lax
from jax.experimental import pallas as pl
from jax.experimental.pallas import tpu as pltpu
from jax.sharding import PartitionSpec as P

EPSILON = 1e-05
SCORE_CAP = 5.0
GELU_ROOT = 0.7978845608028654
GELU_CUBIC = 0.044715
SMALL = 16
AXES = ("dom", "rep")
VMEM_LIMIT = 48 * 1024 * 1024
F32 = jnp.float32
BF16 = jnp.bfloat16


def dot(a, b):
    return lax.dot_general(a, b, (((1,), (0,)), ((), ())), preferred_element_type=F32)


def dot_rhs_t(a, b):
    return lax.dot_general(a, b, (((1,), (1,)), ((), ())), preferred_element_type=F32)


def dot_lhs_t(a, b):
    return lax.dot_general(a, b, (((0,), (0,)), ((), ())), preferred_element_type=F32)


def norm_forward(matrix):
    center = jnp.mean(matrix, axis=-1, keepdims=True)
    shifted = matrix - center
    inverse = lax.rsqrt(jnp.mean(shifted * shifted, axis=-1, keepdims=True) + EPSILON)
    return (shifted * inverse, inverse)


def norm_backward(upstream, normed, inverse, gain):
    scaled_up = upstream * gain
    return inverse * (
        scaled_up
        - jnp.mean(scaled_up, axis=-1, keepdims=True)
        - normed * jnp.mean(scaled_up * normed, axis=-1, keepdims=True)
    )


def gelu_parts(preact):
    tangent = jnp.tanh(GELU_ROOT * (preact + GELU_CUBIC * preact * preact * preact))
    result = 0.5 * preact * (1.0 + tangent)
    derivative = 0.5 * (1.0 + tangent) + 0.5 * preact * (1.0 - tangent * tangent) * GELU_ROOT * (
        1.0 + 3.0 * GELU_CUBIC * preact * preact
    )
    return (result, derivative)


def split_parts(rows):
    high = rows.astype(BF16).astype(F32)
    return jnp.concatenate([high, rows - high], axis=0).astype(BF16)


def join_parts(packed):
    wide = packed.astype(F32)
    return wide[: SMALL // 2] + wide[SMALL // 2 :]


def device_bits():
    flat = lax.axis_index("dom") * lax.axis_size("rep") + lax.axis_index("rep")
    return (flat & 1, (flat >> 1) & 3)


def head_masks_of(shape, heads):
    lane = lax.broadcasted_iota(jnp.int32, shape, 1) // (shape[1] // heads)
    return [lane == h for h in range(heads)]


def stack_heads(matrix, masks):
    return jnp.concatenate([jnp.where(m, matrix, 0.0) for m in masks], axis=0).astype(BF16)


def relay(source_refs, out_refs):
    for source, out in zip(source_refs, out_refs):
        out[...] = source[...]


def flag_kernel(flag_ref):
    flag_ref[...] = jnp.zeros(flag_ref.shape, F32)


def count_kernel(groups, flag_ref, perm_ref, local_ref, far_ref, *refs):
    sources = refs[: len(refs) // 2 - 1]
    count_ref, scale_ref = refs[len(sources) : len(sources) + 2]
    relay(sources, refs[len(sources) + 2 :])
    rows = perm_ref.shape[1]
    target = lax.broadcasted_iota(jnp.int32, (rows, rows), 0)
    count_ref[:, :rows] = jnp.ones((rows, rows), F32)
    for g, members in enumerate(groups):
        total = 0.0
        for m in members:
            total = total + jnp.where(target == perm_ref[m : m + 1, :], 1.0, 0.0)
        count_ref[:, (g + 1) * rows : (g + 2) * rows] = total.T
    near = lax.broadcasted_iota(jnp.int32, (1, scale_ref.shape[1]), 1) < rows
    for h in range(local_ref.shape[0]):
        scale_ref[h : h + 1, :] = jnp.where(near, local_ref[h], far_ref[h])


def unit_of(units_ref, owner, rel):
    rows = units_ref.shape[0] // 8
    return units_ref[pl.ds(pl.multiple_of((owner * 4 + rel) * rows, rows), rows), :]


def sort_units(units_ref, send_ref, bits):
    core, quad = bits
    rows = units_ref.shape[0] // 8
    for r in range(4):
        send_ref[r * rows : (r + 1) * rows, :] = unit_of(units_ref, 1 - core, quad ^ r)


def collapse(matrix, masks):
    rows = matrix.shape[0] // len(masks)
    total = jnp.where(masks[0], matrix[:rows], 0.0)
    for h in range(1, len(masks)):
        total = total + jnp.where(masks[h], matrix[h * rows : (h + 1) * rows], 0.0)
    return total


def layer_kernel(slots, count, *refs):
    feats_refs = refs[: count + 1]
    (
        up_ref,
        gain1_ref,
        wq_ref,
        wk_ref,
        wv_ref,
        wo_ref,
        gain2_ref,
        wup_ref,
        wdown_ref,
        scale_ref,
        count_ref,
    ) = refs[count + 1 : count + 12]
    out_ref, wide_s, sendw_ref, square_s, sends_ref, own_ref, mixed_ref = refs[count + 12 : count + 19]
    slot_refs = refs[count + 19 : count + 19 + len(slots)]
    raw_s, tanh_s, weight_s, dscore_s = refs[count + 19 + len(slots) :]

    rows, width = out_ref.shape
    heads = raw_s.shape[0] // rows
    head_dim = width // heads
    scale = 1.0 / float(head_dim) ** 0.5
    bits = device_bits()
    core = bits[0]

    gain1 = gain1_ref[...]
    gain2 = gain2_ref[...]
    upstream = up_ref[...]
    feats = jnp.concatenate([ref[...] for ref in feats_refs], axis=0).astype(F32)
    normed1, _ = norm_forward(feats)
    hidden = (normed1 * gain1).astype(BF16)
    queries = dot(hidden[:rows], wq_ref[...])
    key_all = dot(hidden, wk_ref[...]).astype(BF16)
    value_all = dot(hidden, wv_ref[...]).astype(BF16)

    head_masks = head_masks_of((rows, width), heads)
    query_stack = stack_heads(queries, head_masks)
    raw_s[...] = dot_rhs_t(query_stack, key_all) * scale

    back = dot_rhs_t(upstream, wdown_ref[...])
    counts = count_ref[...]
    for h in range(heads):
        block = pl.ds(h * rows, rows)
        tangent = jnp.tanh(raw_s[block, :] * (scale_ref[h : h + 1, :] * (1.0 / SCORE_CAP)))
        tanh_s[block, :] = tangent
        powers = jnp.exp(SCORE_CAP * tangent) * counts
        weight_s[block, :] = (powers * (1.0 / jnp.sum(powers, axis=1, keepdims=True))).astype(BF16)

    attended32 = collapse(dot(weight_s[...], value_all), head_masks)
    attended = attended32.astype(BF16)
    mixed = (feats[:rows] + dot(attended, wo_ref[...])).astype(BF16)
    normed2, inverse2 = norm_forward(mixed.astype(F32))
    hidden2 = (normed2 * gain2).astype(BF16)
    preact = dot(hidden2, wup_ref[...])
    act32, derivative = gelu_parts(preact)
    act = act32.astype(BF16)
    grad_pre = (back * derivative).astype(BF16)
    grad_hidden2 = dot_rhs_t(grad_pre, wup_ref[...])
    grad_gain2 = jnp.sum(grad_hidden2 * normed2, axis=0, keepdims=True)
    grad_mixed = upstream.astype(F32) + norm_backward(grad_hidden2, normed2, inverse2, gain2)
    mixed_ref[...] = grad_mixed
    grad_mixed16 = grad_mixed.astype(BF16)
    grad_att = dot_rhs_t(grad_mixed16, wo_ref[...]).astype(BF16).astype(F32)
    grad_stack = stack_heads(grad_att, head_masks)
    product = grad_att * attended32
    dots = dot_rhs_t(grad_stack, value_all)

    out_ref[...] = (mixed.astype(F32) + dot(act, wdown_ref[...])).astype(BF16)
    grad_down = dot_lhs_t(act, upstream)
    wide_s[2 * width : 3 * width, :] = grad_down[:width].astype(BF16)
    wide_s[3 * width : 4 * width, :] = grad_down[width:].astype(BF16)
    grad_up = dot_lhs_t(hidden2, grad_pre)
    wide_s[0 * width : 1 * width, :] = grad_up[:, :width].astype(BF16)
    wide_s[1 * width : 2 * width, :] = grad_up[:, width:].astype(BF16)
    sort_units(wide_s, sendw_ref, bits)
    local_terms = []
    far_terms = []
    for h in range(heads):
        block = pl.ds(h * rows, rows)
        delta = jnp.sum(jnp.where(head_masks[h], product, 0.0), axis=1, keepdims=True)
        tangent = tanh_s[block, :]
        slope = 1.0 - tangent * tangent
        dlogit = weight_s[block, :].astype(F32) * (dots[h * rows : (h + 1) * rows] - delta)
        sloped = dlogit * slope
        terms = jnp.sum(sloped * raw_s[block, :], axis=0, keepdims=True)
        local_terms.append(jnp.sum(terms[:, :rows], axis=1, keepdims=True))
        far_terms.append(jnp.sum(terms[:, rows:], axis=1, keepdims=True))
        dscore_s[block, :] = (sloped * (scale_ref[h : h + 1, :] * scale)).astype(BF16)

    square_s[3 * width : 4 * width, :] = dot_lhs_t(attended, grad_mixed16).astype(BF16)
    grad_query = collapse(dot(dscore_s[...], key_all), head_masks).astype(BF16)
    grad_key = dot_lhs_t(dscore_s[...], query_stack).astype(BF16)
    grad_value = dot_lhs_t(weight_s[...], grad_stack).astype(BF16)
    square_s[0 * width : 1 * width, :] = dot_lhs_t(hidden[:rows], grad_query).astype(BF16)
    square_s[1 * width : 2 * width, :] = dot_lhs_t(hidden, grad_key).astype(BF16)
    square_s[2 * width : 3 * width, :] = dot_lhs_t(hidden, grad_value).astype(BF16)
    grad_hidden = dot_rhs_t(grad_key, wk_ref[...]) + dot_rhs_t(grad_value, wv_ref[...])
    own = grad_hidden[:rows] + dot_rhs_t(grad_query, wq_ref[...])
    own_ref[...] = own
    grad_gain1 = jnp.sum(own * normed1[:rows], axis=0, keepdims=True)
    grad_gain1 = grad_gain1 + jnp.sum(grad_hidden[rows:] * normed1[rows:], axis=0, keepdims=True)
    back = [grad_hidden[(k + 1) * rows : (k + 2) * rows] for k in range(count)]
    for (even, odd), ref in zip(slots, slot_refs):
        ref[...] = jnp.where(
            core == 1, 0.0 if odd is None else back[odd], 0.0 if even is None else back[even]
        ).astype(BF16)

    column = lax.broadcasted_iota(jnp.int32, (1, width), 1)
    gains = jnp.zeros((1, width), F32)
    for h in range(heads):
        gains = jnp.where(column == h, local_terms[h], gains)
        gains = jnp.where(column == heads + h, far_terms[h], gains)
    line = lax.broadcasted_iota(jnp.int32, (SMALL // 2, width), 0)
    small = jnp.where(line == 0, grad_gain1, jnp.where(line == 1, grad_gain2, jnp.where(line == 2, gains, 0.0)))
    sends_ref[sendw_ref.shape[0] :, :] = split_parts(small)
    sort_units(square_s, sends_ref, bits)


def pair_kernel(slots, apart, keepw_ref, recvw_ref, keeps_ref, sents_ref, recvs_ref, *refs):
    slot_refs = refs[: sum(slots)]
    out_refs = refs[sum(slots) + apart :]
    relay(refs[sum(slots) : sum(slots) + apart], out_refs[4:])
    rows = keepw_ref.shape[0] // 8
    core, quad = device_bits()
    packed = split_parts(join_parts(sents_ref[4 * rows :, :]) + join_parts(recvs_ref[4 * rows :, :]))
    used = 0
    for r in range(4):
        span = slice(r * rows, (r + 1) * rows)
        wide = unit_of(keepw_ref, core, quad ^ r).astype(F32) + recvw_ref[span, :].astype(F32)
        square = unit_of(keeps_ref, core, quad ^ r).astype(F32) + recvs_ref[span, :].astype(F32)
        out_refs[r][:rows, :] = wide.astype(BF16)
        out_refs[r][rows : 2 * rows, :] = square.astype(BF16)
        out_refs[r][2 * rows : 2 * rows + SMALL, :] = packed
        if r and slots[r - 1]:
            out_refs[r][2 * rows + SMALL :, :] = slot_refs[used][...]
            used += 1


def quad_kernel(has_slot, own_ref, one_ref, two_ref, three_ref, *refs):
    wide_ref, square_ref = refs[-2:]
    total_rows = own_ref.shape[0]
    rows = (total_rows - SMALL) // 2
    data = [ref[: 2 * rows, :].astype(F32) for ref in (own_ref, one_ref, two_ref, three_ref)]
    small = [join_parts(ref[2 * rows : total_rows, :]) for ref in (own_ref, one_ref, two_ref, three_ref)]
    total = ((data[0] + data[1]) + (data[2] + data[3])).astype(BF16)
    wide_ref[:rows, :] = total[:rows]
    square_ref[:rows, :] = total[rows:]
    square_ref[rows:, :] = split_parts((small[0] + small[1]) + (small[2] + small[3]))
    if has_slot:
        wide_ref[rows:, :] = refs[0][...]


def double_kernel(rows, small, has_slot, own_ref, recv_ref, *refs):
    out_ref = refs[-1]
    total = own_ref[:rows, :].astype(F32) + recv_ref[:rows, :].astype(F32)
    out_ref[:rows, :] = total.astype(BF16)
    if small:
        span = slice(rows, rows + SMALL)
        out_ref[span, :] = split_parts(join_parts(own_ref[span, :]) + join_parts(recv_ref[span, :]))
    if has_slot:
        out_ref[rows:, :] = refs[0][...]


def join_kernel(wide_ref, square_ref, out_ref):
    rows = out_ref.shape[0] // 2
    out_ref[:rows, :] = wide_ref[:rows, :]
    out_ref[rows:, :] = square_ref[:rows, :]


def tail_kernel(start, *refs):
    count = len(start)
    feats_ref, rows_ref, own_ref, mixed_ref, gain_ref, small_ref = refs[:6]
    out_ref, grad_ref, gain1_ref, gain2_ref, local_ref, far_ref, flag_ref = refs[6 + count :]
    out_ref[...] = rows_ref[...]
    normed, inverse = norm_forward(feats_ref[...].astype(F32))
    grad_hidden = own_ref[...]
    for ref, first in zip(refs[6 : 6 + count], start):
        grad_hidden = grad_hidden + ref[first:, :].astype(F32)
    grad = mixed_ref[...] + norm_backward(grad_hidden, normed, inverse, gain_ref[...])
    grad_ref[...] = grad.astype(BF16)
    heads = local_ref.shape[0]
    small = join_parts(small_ref[small_ref.shape[0] - SMALL :, :])
    gain1_ref[...] = small[0:1]
    gain2_ref[...] = small[1:2]
    local_ref[...] = small[2, :heads]
    far_ref[...] = small[2, heads : 2 * heads]
    flag_ref[...] = jnp.zeros(flag_ref.shape, F32)


def after_kernel(source_ref, flag_ref, out_ref):
    out_ref[...] = source_ref[...]


def spread_kernel(own, *refs):
    piece_refs = refs[:4]
    wq_ref, wk_ref, wv_ref, wo_ref, up_ref, down_ref, pieces, chunks, sems = refs[-9:]
    width = wq_ref.shape[0]
    half = width // 2
    core, quad = device_bits()
    side = core if own else 1 - core
    relay(piece_refs, [pieces.at[k] for k in range(4)])
    low = [up_ref.at[:, :width], up_ref.at[:, width:], wq_ref, wk_ref]
    high = [down_ref.at[:width, :], down_ref.at[width:, :], wv_ref, wo_ref]

    for bit, targets in enumerate((low, high)):

        @pl.when(side == bit)
        def _():
            copies = []
            for slot, target in enumerate(targets):
                first = 0 if slot < 2 else half
                for part in range(2):
                    value = pieces[quad ^ (2 * (slot % 2) + part), first : first + half, :]
                    chunks[slot, part * half : (part + 1) * half, :] = value.astype(F32)
                copy = pltpu.make_async_copy(chunks.at[slot], target, sems.at[slot])
                copy.start()
                copies.append(copy)
            for copy in copies:
                copy.wait()


def struct(shape, dtype):
    return jax.ShapeDtypeStruct(shape, dtype)


VM = pl.BlockSpec(memory_space=pltpu.VMEM)
SM = pl.BlockSpec(memory_space=pltpu.SMEM)
ANY = pl.BlockSpec(memory_space=pl.ANY)
PARAMS = pltpu.CompilerParams(vmem_limit_bytes=VMEM_LIMIT)


def call(kernel, outs, *args, in_specs=None, **kwargs):
    return pl.pallas_call(
        kernel,
        out_shape=outs,
        in_specs=in_specs or [VM] * len(args),
        out_specs=jax.tree.map(lambda _: VM, outs),
        compiler_params=PARAMS,
        **kwargs,
    )(*args)


def flipped(x, bits_even, bits_odd):
    size = lax.axis_size("dom") * lax.axis_size("rep")
    pairs = [(i, i ^ (bits_odd if i & 1 else bits_even)) for i in range(size)]
    return lax.ppermute(x, AXES, pairs)


def local(
    node_feats,
    out_grad,
    norm1_gain,
    w_query,
    w_key,
    w_value,
    w_out,
    norm2_gain,
    w_up,
    w_down,
    local_gain,
    expander_gain,
    partner_perm,
    block_pairs,
    pair_count,
):
    feats = node_feats[0]
    partners = partner_perm[0, :, 0, :]
    rows, width = feats.shape
    heads = local_gain.shape[0]
    size = lax.axis_size("dom") * lax.axis_size("rep")
    levels = lax.axis_size("dom").bit_length() - 1
    by_bit = {}
    for matching in range(partners.shape[0]):
        by_bit.setdefault((levels - 1 - matching) % levels, []).append(matching)
    bits = sorted(by_bit)
    groups = [by_bit[b] for b in bits]

    def swapped(x, bit):
        return lax.ppermute(x, "dom", [(i, i ^ 1 << bit) for i in range(lax.axis_size("dom"))])

    rep_bits = lax.axis_size("rep").bit_length() - 1
    high_bits = [1 << k for k in range(3, size.bit_length() - 1)]
    flat = {1 << (b + rep_bits): k for k, b in enumerate(bits)}
    quad_slots = [flat.get(bit) for bit in (2, 4, 6)]
    orders = (list(zip(high_bits, high_bits)), list(zip(high_bits[::-1], high_bits[::-1])))
    apart = [k for bit, k in flat.items() if bit > 4]
    slots = [(k, k) for k in quad_slots if k is not None]
    slots += [(k, k) for k in apart]

    others = [swapped(feats, b) for b in bits]
    count = len(bits)
    tall = count * rows
    stacked = heads * rows
    gain1 = norm1_gain.reshape(1, width)
    gain2 = norm2_gain.reshape(1, width)
    upstream = out_grad[0]
    flag = struct((8, 128), F32)
    begun = call(
        flag_kernel, flag, cost_estimate=pl.CostEstimate(flops=10**10, bytes_accessed=1, transcendentals=0)
    )
    passed = (feats, upstream, gain1, gain2)
    counts, scales, feats_near, up_near, gain1_near, gain2_near = call(
        functools.partial(count_kernel, groups),
        (struct((rows, tall + rows), F32), struct((8, tall + rows), F32))
        + tuple(struct(x.shape, x.dtype) for x in passed),
        begun,
        partners,
        local_gain,
        expander_gain,
        *passed,
        in_specs=[VM, VM, SM, SM] + [VM] * len(passed),
        cost_estimate=pl.CostEstimate(flops=10**10, bytes_accessed=1, transcendentals=0),
    )
    out_rows, keep_wide, send_wide, keep_square, send_square, own, grad_mixed, *slot_rows = call(
        functools.partial(layer_kernel, slots, count),
        (
            struct((rows, width), BF16),
            struct((4 * width, width), BF16),
            struct((2 * width, width), BF16),
            struct((4 * width, width), BF16),
            struct((2 * width + SMALL, width), BF16),
            struct((rows, width), F32),
            struct((rows, width), F32),
        )
        + tuple(struct((rows, width), BF16) for _ in slots),
        feats_near,
        *others,
        up_near,
        gain1_near,
        w_query,
        w_key,
        w_value,
        w_out,
        gain2_near,
        w_up,
        w_down,
        scales,
        counts,
        scratch_shapes=[
            pltpu.VMEM((stacked, tall + rows), F32),
            pltpu.VMEM((stacked, tall + rows), F32),
            pltpu.VMEM((stacked, tall + rows), BF16),
            pltpu.VMEM((stacked, tall + rows), BF16),
        ],
    )
    slot_rows = iter(slot_rows)
    slot_quad = [None if k is None else next(slot_rows) for k in quad_slots]
    slot_apart = list(slot_rows)

    def present(*items):
        return [x for x in items if x is not None]

    def sized(base, slot):
        return struct((base + (0 if slot is None else rows), width), BF16)

    half = width // 2
    recv_wide = flipped(send_wide, 1, 1)
    recv_square = flipped(send_square, 1, 1)
    data = 2 * half + SMALL
    block = struct((rows, width), BF16)
    own_quad, *send_quad = call(
        functools.partial(pair_kernel, [x is not None for x in slot_quad], len(apart)),
        (struct((data, width), BF16),) + tuple(sized(data, x) for x in slot_quad) + (block,) * len(apart),
        keep_wide,
        recv_wide,
        keep_square,
        send_square,
        recv_square,
        *present(*slot_quad),
        *slot_apart,
    )
    send_quad, send_apart = send_quad[:3], send_quad[3:]
    recv_quad = [flipped(x, bit, bit) for x, bit in zip(send_quad, (2, 4, 6))]
    returned = [x for x, slot in zip(recv_quad, slot_quad) if slot is not None]
    starts = [data] * len(returned) + [0] * len(apart)
    recv_apart = [swapped(x, bits[k]) for x, k in zip(send_apart, apart)]
    returned += recv_apart
    wide, square = call(
        functools.partial(quad_kernel, False),
        (struct((half, width), BF16), struct((half + SMALL, width), BF16)),
        own_quad,
        *recv_quad,
        *recv_apart,
    )
    for k in range(len(high_bits)):
        recv_wide = flipped(wide, *orders[0][k])
        recv_square = flipped(square, *orders[1][k])
        wide = call(
            functools.partial(double_kernel, half, False, False),
            struct((half, width), BF16),
            wide,
            recv_wide,
            square,
        )
        square = call(
            functools.partial(double_kernel, half, True, False),
            struct((half + SMALL, width), BF16),
            square,
            recv_square,
            wide,
        )
    block = struct((rows, width), BF16)
    one = struct((1, width), F32)
    full = struct((width, width), F32)
    few = struct((heads,), F32)
    node_out, grad_feats, grad_gain1, grad_gain2, grad_local, grad_far, ended = call(
        functools.partial(tail_kernel, starts),
        (block, block, one, one, few, few, flag),
        feats_near,
        out_rows,
        own,
        grad_mixed,
        gain1_near,
        square,
        *returned,
    )
    base = call(join_kernel, struct((2 * half, width), BF16), wide, square)
    near = [base] + [flipped(base, bit, bit) for bit in (2, 4, 6)]
    near[3] = call(after_kernel, struct(base.shape, BF16), near[3], ended)
    over = [flipped(x, 1, 1) for x in near]
    grads = (full,) * 4 + (struct((width, 2 * width), F32), struct((2 * width, width), F32))
    for own in (True, False):
        before = [] if own else grads
        grads = pl.pallas_call(
            functools.partial(spread_kernel, own),
            out_shape=tuple(struct(x.shape, x.dtype) for x in grads),
            in_specs=[VM] * 4 + [ANY] * len(before),
            out_specs=(ANY,) * 6,
            scratch_shapes=[
                pltpu.VMEM((4, width, width), BF16),
                pltpu.VMEM((4, width, width), F32),
                pltpu.SemaphoreType.DMA((4,)),
            ],
            input_output_aliases={4 + k: k for k in range(len(before))},
            compiler_params=PARAMS,
        )(*(near if own else over), *before)
    grad_wq, grad_wk, grad_wv, grad_wout, grad_up, grad_down = grads
    return (
        node_out[None],
        grad_feats[None],
        grad_gain1.reshape(width),
        grad_wq,
        grad_wk,
        grad_wv,
        grad_wout,
        grad_gain2.reshape(width),
        grad_up,
        grad_down,
        grad_local,
        grad_far,
    )


def solution(mesh):
    whole = P()
    rows = P("rep", "dom", None)
    return jax.shard_map(
        local,
        mesh=mesh,
        in_specs=(rows, rows)
        + (whole,) * 10
        + (P("rep", None, "dom", None), rows, P("rep", "dom")),
        out_specs=(rows, rows) + (whole,) * 10,
        check_vma=False,
    )
```
